32 devices in a mesh: bn: 2 (over core), fsdp: 16 (over z, y, x).
Axes of the slice: x: 2, y: 2, z: 4, core: 2. Of those that a mesh axis runs over, the one named last changes fastest.
Arguments:
- features: bfloat16 [32, 1024, 2048], P(('bn', 'fsdp')), may hold values from -6 to 6
- region_boxes: int32 [32, 4, 4], P(('bn', 'fsdp')), may hold values from 0 to 25, as said below
- branch_w: bfloat16 [2048, 2048], P('fsdp'), may hold values from -0.125 to 0.125
- merge_w: bfloat16 [4096, 4608], P('fsdp'), may hold values from -0.03125 to 0.03125
- class_w: bfloat16 [512, 19], replicated, may hold values from -0.25 to 0.25
- norm_gain: bfloat16 [5, 512], replicated, may hold values from 0.25 to 1.75
- norm_bias: bfloat16 [5, 512], replicated, may hold values from -3 to 3
- grad_logits: bfloat16 [32, 1024, 19], P(('bn', 'fsdp')), may hold values from -6 to 6
Outputs:
- logits: float32 [32, 1024, 19], P(('bn', 'fsdp'))
- grad_features: float32 [32, 1024, 2048], P(('bn', 'fsdp'))
- grad_branch_w: float32 [2048, 2048], P('fsdp')
- grad_merge_w: float32 [4096, 4608], P('fsdp')
- grad_class_w: float32 [512, 19], replicated
- grad_gain: float32 [5, 512], replicated
- grad_bias: float32 [5, 512], replicated
The draws below stay inside these ranges and needn't reach their ends.
Inputs may be any that keep to these rules, and one draw needn't show every extreme that they name: `region_boxes`: image k of a canvas lies in cell (k // 2, k % 2) of side 16, within its first 15 rows and columns; heights and widths are 6 to 15.
All inputs are finite; a program needn't handle non-finite values.
Results may differ from the reference program's by a relative error of at most 0.01.
Values may be sent and summed in bfloat16 or wider, within the bound.
A program may use at most 576 MiB of HBM per device.

```python
import jax
import jax.numpy as jnp
from jax import lax

CIN = 2048
MID = 512
CLS = 19
BR = 4
CELL = 16
GRID_C = 2
CAN_DEV = 1
CAT = 4096
IMG = 4
SIDE_R = 32
SIDE_C = 32
PIX = 1024
CANVASES = 32
N_BN = 2
N_FSDP = 16


def draw_region_boxes(key, part):
    key = jax.random.fold_in(key, 11)
    keys = jax.random.split(key, 4)
    shape = (CANVASES, IMG)
    height = jax.random.randint(keys[0], shape, 6, CELL)
    width = jax.random.randint(keys[1], shape, 6, CELL)
    canvas = jnp.arange(CANVASES, dtype=jnp.int32)[:, None]
    image = jnp.arange(IMG, dtype=jnp.int32)[None, :]
    first = (canvas == 0) & (image == 0)
    final = (canvas == 0) & (image == IMG - 1)
    height = jnp.where(first, CELL - 1, jnp.where(final, 6, height))
    width = jnp.where(first, CELL - 1, jnp.where(final, 6, width))
    shift_row = jax.random.randint(keys[2], shape, 0, CELL) % (CELL - height)
    shift_col = jax.random.randint(keys[3], shape, 0, CELL) % (CELL - width)
    shift_row = jnp.where(first, 0, jnp.where(final, CELL - 7, shift_row))
    shift_col = jnp.where(first, 0, jnp.where(final, CELL - 7, shift_col))
    top = image // GRID_C * CELL + shift_row
    left = image % GRID_C * CELL + shift_col
    return jnp.stack([top, left, height, width], axis=-1).astype(jnp.int32)


def block_scale(rng, dims, pieces, low, largest):
    def one(axis_at, blocks):
        heights = jax.random.uniform(jax.random.fold_in(jax.random.fold_in(rng, 6), axis_at), (blocks,), jnp.float32, low / len(pieces), largest / len(pieces))
        return jnp.repeat(jnp.exp(heights), dims[axis_at] // blocks).reshape((-1,) + (1,) * (len(dims) - axis_at - 1))

    loudness = one(*pieces[0])
    for cut in pieces[1:]:
        loudness = loudness * one(*cut)
    return loudness


def scatter_about(rng, extent, scale, reach, shards=(), held_as=jnp.bfloat16):
    factor_of = block_scale(rng, extent, shards, -0.22, 0.18) if shards else 1.0
    values = jax.random.normal(rng, extent, jnp.float32) * scale * factor_of
    return jnp.minimum(jnp.maximum(values, -reach), reach).astype(held_as)


def setup_inputs(seed: int = 0) -> dict:
    arg_keys = jax.random.split(jax.random.key(seed), 9)
    features = scatter_about(arg_keys[0], (CANVASES, PIX, CIN), 1.0, 6.0, ((0, 32),))
    region_boxes = draw_region_boxes(jax.random.fold_in(arg_keys[8], 71), 0)
    branch_w = scatter_about(arg_keys[2], (CIN, BR * MID), CIN ** -0.5, 0.125, ((0, 16),))
    merge_w = scatter_about(arg_keys[3], (CAT, 9 * MID), (9 * CAT) ** -0.5, 0.03125, ((0, 16),))
    class_w = scatter_about(arg_keys[4], (MID, CLS), MID ** -0.5, 0.25)
    norm_gain = jnp.clip(1.0 + 0.15 * jax.random.normal(arg_keys[5], (5, MID), jnp.float32), 0.25, 1.75).astype(jnp.bfloat16)
    norm_bias = scatter_about(arg_keys[6], (5, MID), 0.5, 3.0)
    grad_logits = scatter_about(arg_keys[7], (CANVASES, PIX, CLS), 1.0, 6.0, ((0, 32),))
    return dict(features=features, region_boxes=region_boxes, branch_w=branch_w, merge_w=merge_w, class_w=class_w, norm_gain=norm_gain, norm_bias=norm_bias, grad_logits=grad_logits)


@jax.custom_vjp
def low(v):
    return lax.optimization_barrier(v.astype(jnp.bfloat16)).astype(jnp.float32)

@jax.custom_vjp
def low_back(v):
    return v

def low_keep(v):
    return (low(v), None)

def low_pass(kept, grad):
    return (grad,)

def back_keep(v):
    return (v, None)

def back_low(kept, grad):
    return (low(grad),)
low.defvjp(low_keep, low_pass)
low_back.defvjp(back_keep, back_low)
EPSILON = 1e-05
BIN_COUNTS = (1, 2, 3, 6)
HIGH = lax.Precision.HIGHEST

def region_maps(region_boxes, bins):
    canvases = region_boxes.shape[0]
    top = region_boxes[:, :, 0][:, :, None]
    left = region_boxes[:, :, 1][:, :, None]
    height = region_boxes[:, :, 2][:, :, None]
    width = region_boxes[:, :, 3][:, :, None]
    pixel = jnp.arange(PIX, dtype=jnp.int32)
    rel_row = (pixel // SIDE_C)[None, None, :] - top
    rel_col = (pixel % SIDE_C)[None, None, :] - left
    index = jnp.arange(bins, dtype=jnp.int32)[None, None, :, None]
    row_low = index * height[..., None] // bins
    row_high = ((index + 1) * height[..., None] + bins - 1) // bins
    col_low = index * width[..., None] // bins
    col_high = ((index + 1) * width[..., None] + bins - 1) // bins
    row_in = (rel_row[:, :, None, :] >= row_low) & (rel_row[:, :, None, :] < row_high)
    col_in = (rel_col[:, :, None, :] >= col_low) & (rel_col[:, :, None, :] < col_high)
    pool = (row_in[:, :, :, None, :] & col_in[:, :, None, :, :]).reshape(canvases, IMG * bins * bins, PIX)
    inside_row = (rel_row >= 0) & (rel_row < height)
    inside_col = (rel_col >= 0) & (rel_col < width)
    near_row = rel_row * bins // height
    near_col = rel_col * bins // width
    up_row = inside_row[:, :, None, :] & (near_row[:, :, None, :] == index)
    up_col = inside_col[:, :, None, :] & (near_col[:, :, None, :] == index)
    upmap = (up_row[:, :, :, None, :] & up_col[:, :, None, :, :]).reshape(canvases, IMG * bins * bins, PIX)
    inside = jnp.any(inside_row & inside_col, axis=1)
    return (pool.astype(jnp.float32), upmap.astype(jnp.float32), inside.astype(jnp.float32))

def forward(feats, branch_w, merge_w, class_w, norm_gain, norm_bias, maps, inside):
    group = feats.shape[0]
    masked = feats * inside[:, :, None]
    parts = [masked]
    for branch in range(len(BIN_COUNTS)):
        pool, upmap = maps[branch]
        count = lax.optimization_barrier(jnp.sum(pool, axis=2))
        pooled_sum = low_back(jnp.einsum('cnp,cpd->cnd', pool, masked, precision=HIGH))
        pooled = low(pooled_sum / count[:, :, None])
        weight = branch_w[:, branch * MID:(branch + 1) * MID]
        outputs = low_back(jnp.einsum('cnd,do->cno', pooled, weight, precision=HIGH))
        mean = lax.optimization_barrier(jnp.mean(outputs, axis=(0, 1)))
        spread = lax.optimization_barrier(jnp.mean(outputs * outputs, axis=(0, 1))) - mean * mean
        normed = (outputs - mean) * lax.rsqrt(spread + EPSILON) * norm_gain[branch] + norm_bias[branch]
        active = low(jax.nn.silu(normed))
        parts.append(low_back(jnp.einsum('cnp,cno->cpo', upmap, active, precision=HIGH)))
    joined = jnp.concatenate(parts, axis=2)
    padded = jnp.pad(joined.reshape(group, SIDE_R, SIDE_C, CAT), ((0, 0), (1, 1), (1, 1), (0, 0)))
    convolved = jnp.zeros((group, PIX, MID), jnp.float32)
    for tap in range(9):
        piece = padded[:, tap // 3:tap // 3 + SIDE_R, tap % 3:tap % 3 + SIDE_C, :].reshape(group, PIX, CAT)
        convolved = convolved + jnp.einsum('cpi,io->cpo', piece, merge_w[:, tap * MID:(tap + 1) * MID], precision=HIGH)
    convolved = low_back(convolved)
    weight_in = inside[:, :, None]
    total = jnp.sum(inside)
    mean2 = lax.optimization_barrier(jnp.sum(convolved * weight_in, axis=(0, 1))) / total
    spread2 = lax.optimization_barrier(jnp.sum(convolved * convolved * weight_in, axis=(0, 1))) / total - mean2 * mean2
    normed2 = (convolved - mean2) * lax.rsqrt(spread2 + EPSILON) * norm_gain[4] + norm_bias[4]
    hidden = low(jax.nn.silu(normed2))
    return jnp.einsum('cpo,ok->cpk', hidden, class_w, precision=HIGH) * weight_in

def regroup(array):
    group = N_BN * CAN_DEV
    shaped = array.reshape((N_BN, N_FSDP, CAN_DEV) + array.shape[1:])
    return jnp.swapaxes(shaped, 0, 1).reshape((N_FSDP, group) + array.shape[1:])

def ungroup(array):
    shaped = array.reshape((N_FSDP, N_BN, CAN_DEV) + array.shape[2:])
    return jnp.swapaxes(shaped, 0, 1).reshape((CANVASES,) + array.shape[2:])

def reference(features, region_boxes, branch_w, merge_w, class_w, norm_gain, norm_bias, grad_logits):
    weights = tuple((w.astype(jnp.float32) for w in (branch_w, merge_w, class_w, norm_gain, norm_bias)))

    def step(summed, item):
        feats, boxes_here, cotangent = item
        maps = []
        inside = None
        for bins in BIN_COUNTS:
            pool, upmap, inside = region_maps(boxes_here, bins)
            maps.append((pool, upmap))

        def apply(feats_in, *params):
            return forward(feats_in, *params, maps, inside)
        logits, pull = jax.vjp(apply, feats.astype(jnp.float32), *weights)
        grads = pull(cotangent.astype(jnp.float32))
        summed = tuple((a + g for a, g in zip(summed, grads[1:])))
        return (summed, (logits, grads[0]))
    start = tuple((jnp.zeros(w.shape, jnp.float32) for w in weights))
    summed, (logits, grad_feats) = lax.scan(step, start, (regroup(features), regroup(region_boxes), regroup(grad_logits)))
    return (ungroup(logits), ungroup(grad_feats), summed[0], summed[1], summed[2], summed[3], summed[4])
```

```python
import jax
import jax.numpy as jnp
from jax import lax
from jax.sharding import PartitionSpec as P

CIN = 2048
MID = 512
CLS = 19
IMG = 4
SIDE_R = 32
SIDE_C = 32
PIX = 1024
TAPS = 9
EPSILON = 1e-05
BIN_COUNTS = (1, 2, 3, 6)
SIZES = tuple(IMG * bins * bins for bins in BIN_COUNTS)
STARTS = (0, 4, 20, 56)
BINS = 200


def region_maps(region_boxes, bins):
    canvases = region_boxes.shape[0]
    top = region_boxes[:, :, 0][:, :, None]
    left = region_boxes[:, :, 1][:, :, None]
    height = region_boxes[:, :, 2][:, :, None]
    width = region_boxes[:, :, 3][:, :, None]
    pixel = jnp.arange(PIX, dtype=jnp.int32)
    rel_row = (pixel // SIDE_C)[None, None, :] - top
    rel_col = (pixel % SIDE_C)[None, None, :] - left
    index = jnp.arange(bins, dtype=jnp.int32)[None, None, :, None]
    row_low = index * height[..., None] // bins
    row_high = ((index + 1) * height[..., None] + bins - 1) // bins
    col_low = index * width[..., None] // bins
    col_high = ((index + 1) * width[..., None] + bins - 1) // bins
    row_in = (rel_row[:, :, None, :] >= row_low) & (rel_row[:, :, None, :] < row_high)
    col_in = (rel_col[:, :, None, :] >= col_low) & (rel_col[:, :, None, :] < col_high)
    pool = (row_in[:, :, :, None, :] & col_in[:, :, None, :, :]).reshape(
        canvases, IMG * bins * bins, PIX
    )
    inside_row = (rel_row >= 0) & (rel_row < height)
    inside_col = (rel_col >= 0) & (rel_col < width)
    near_row = rel_row * bins // height
    near_col = rel_col * bins // width
    up_row = inside_row[:, :, None, :] & (near_row[:, :, None, :] == index)
    up_col = inside_col[:, :, None, :] & (near_col[:, :, None, :] == index)
    upmap = (up_row[:, :, :, None, :] & up_col[:, :, None, :, :]).reshape(
        canvases, IMG * bins * bins, PIX
    )
    inside = jnp.any(inside_row & inside_col, axis=1)
    return (pool, upmap, inside)


def silu_slope(value):
    sigma = jax.nn.sigmoid(value)
    return sigma * (1.0 + value * (1.0 - sigma))


def swap(value):
    return lax.ppermute(value, "bn", [(0, 1), (1, 0)])


def both(value):
    return jnp.concatenate([value, swap(value)], axis=0)


def dot(a, b, dims=((1,), (0,))):
    return lax.dot_general(a, b, (dims, ((), ())), preferred_element_type=jnp.float32)


def rolled(value, shift):
    rows = value.shape[0]
    if shift == 0:
        return value
    pad = jnp.zeros((abs(shift),) + value.shape[1:], value.dtype)
    if shift > 0:
        return jnp.concatenate([value[shift:], pad], axis=0)
    return jnp.concatenate([pad, value[: rows + shift]], axis=0)


def own_half(value, half, width):
    rows = value.shape[0]
    cut = value.reshape(rows, -1, 2, width)
    return lax.dynamic_index_in_dim(cut, half, axis=2, keepdims=False).reshape(rows, -1)


def gather_weights(branch_half, merge_half):
    return (
        lax.all_gather(branch_half, "fsdp", axis=0, tiled=True),
        lax.all_gather(merge_half, "fsdp", axis=0, tiled=True),
    )


def scatter_grads(grad_branch, grad_merge):
    return (
        lax.psum_scatter(grad_branch, "fsdp", scatter_dimension=0, tiled=True),
        lax.psum_scatter(grad_merge, "fsdp", scatter_dimension=0, tiled=True),
    )


def body(features, region_boxes, branch_w, merge_w, class_w, norm_gain, norm_bias, grad_logits):
    half = lax.axis_index("bn")
    wide = MID // 2
    branch_full, merge_full = gather_weights(
        own_half(branch_w, half, wide), own_half(merge_w, half, wide)
    )
    gains = lax.dynamic_slice_in_dim(norm_gain, half * wide, wide, 1).astype(jnp.float32)
    biases = lax.dynamic_slice_in_dim(norm_bias, half * wide, wide, 1).astype(jnp.float32)
    class_half = lax.dynamic_slice_in_dim(class_w, half * wide, wide, 0)
    feats = both(features)
    boxes = both(region_boxes)
    cotangent = both(grad_logits)
    pair = feats.shape[0]
    rows = pair * PIX
    pools = []
    upmaps = []
    inside = None
    for bins in BIN_COUNTS:
        pool, upmap, inside = region_maps(boxes, bins)
        pools.append(pool)
        upmaps.append(upmap)
    counts = jnp.concatenate(
        [jnp.sum(pool.astype(jnp.float32), axis=2) for pool in pools], axis=1
    )
    pools = jnp.concatenate(pools, axis=1).astype(jnp.bfloat16)
    upmaps = jnp.concatenate(upmaps, axis=1).astype(jnp.bfloat16)
    inside_float = inside.astype(jnp.float32)
    weight_in = inside_float.reshape(rows, 1)
    masked = (feats * inside.astype(jnp.bfloat16)[:, :, None]).reshape(rows, CIN)
    pooled_sum = jnp.einsum("cnp,cpd->cnd", pools, feats, preferred_element_type=jnp.float32)
    pooled = (pooled_sum / counts[:, :, None]).astype(jnp.bfloat16)

    spans = [slice(s, s + n) for s, n in zip(STARTS, SIZES)]
    outs = []
    stats = []
    for branch, span in enumerate(spans):
        entries = pair * SIZES[branch]
        value = jnp.einsum(
            "cnd,do->cno",
            pooled[:, span],
            branch_full[:, branch * wide : (branch + 1) * wide],
            preferred_element_type=jnp.float32,
        )
        mean = jnp.sum(value, axis=(0, 1)) / entries
        spread = jnp.sum(value * value, axis=(0, 1)) / entries - mean * mean
        inverse = lax.rsqrt(spread + EPSILON)
        centred = (value - mean) * inverse
        normed = centred * gains[branch] + biases[branch]
        outs.append(jax.nn.silu(normed).astype(jnp.bfloat16))
        stats.append((inverse, centred, normed, entries))
    active = jnp.concatenate(outs, axis=1)
    other = swap(active)
    active_full = jnp.where(
        half == 0,
        jnp.concatenate([active, other[::-1]], axis=2),
        jnp.concatenate([other[::-1], active], axis=2),
    )
    lifted = jnp.concatenate(
        [
            jnp.einsum(
                "cno,ok->cnk",
                active_full[:, span],
                merge_full[CIN + branch * MID : CIN + (branch + 1) * MID],
                preferred_element_type=jnp.float32,
            ).astype(jnp.bfloat16)
            for branch, span in enumerate(spans)
        ],
        axis=1,
    )
    spans_up = jnp.swapaxes(upmaps, 1, 2).reshape(rows, BINS)
    strip = 3 * wide
    column = jnp.zeros((rows, strip), jnp.float32)
    for dr in range(3):
        shift = (dr - 1) * SIDE_C
        cut = slice(dr * strip, (dr + 1) * strip)
        column = column + dot(rolled(masked, shift), merge_full[:CIN, cut])
        raised = rolled(spans_up, shift).reshape(pair, PIX, BINS)
        column = column + jnp.einsum(
            "cpn,cnk->cpk", raised, lifted[:, :, cut], preferred_element_type=jnp.float32
        ).reshape(rows, strip)
    convolved = (
        rolled(column[:, :wide], -1)
        + column[:, wide : 2 * wide]
        + rolled(column[:, 2 * wide :], 1)
    )
    pixel_count = jnp.sum(inside_float)
    mean_merged = jnp.sum(convolved * weight_in, axis=0) / pixel_count
    spread_merged = (
        jnp.sum(convolved * convolved * weight_in, axis=0) / pixel_count
        - mean_merged * mean_merged
    )
    inverse_merged = lax.rsqrt(spread_merged + EPSILON)
    centred_merged = (convolved - mean_merged) * inverse_merged
    normed_merged = centred_merged * gains[4] + biases[4]
    hidden = jax.nn.silu(normed_merged).astype(jnp.bfloat16)
    logits_part = (dot(hidden, class_half) * weight_in).reshape(pair, PIX, CLS)
    logits = logits_part[:1] + swap(logits_part[1:])

    masked_grad = (cotangent * inside.astype(jnp.bfloat16)[:, :, None]).reshape(rows, CLS)
    grad_class = dot(hidden, masked_grad, ((0,), (0,)))
    grad_hidden = dot(masked_grad, class_half, ((1,), (1,)))
    grad_normed = grad_hidden * silu_slope(normed_merged)
    gain_merged = jnp.sum(grad_normed * centred_merged * weight_in, axis=0)
    bias_merged = jnp.sum(grad_normed * weight_in, axis=0)
    grad_conv = (
        weight_in
        * gains[4]
        * inverse_merged
        * (grad_normed - (bias_merged + centred_merged * gain_merged) / pixel_count)
    ).astype(jnp.bfloat16)
    spread_grad = jnp.concatenate(
        [
            rolled(grad_conv, -((tap // 3 - 1) * SIDE_C + (tap % 3 - 1)))
            for tap in range(TAPS)
        ],
        axis=1,
    )
    binned = jnp.einsum(
        "cnp,cpk->cnk",
        upmaps,
        spread_grad.reshape(pair, PIX, TAPS * wide),
        preferred_element_type=jnp.float32,
    ).astype(jnp.bfloat16)
    merge_rows = [dot(masked, spread_grad, ((0,), (0,))).astype(jnp.bfloat16)]
    actives = []
    for branch, span in enumerate(spans):
        merge_rows.append(
            jnp.einsum(
                "cno,cnk->ok",
                active_full[:, span],
                binned[:, span],
                preferred_element_type=jnp.float32,
            ).astype(jnp.bfloat16)
        )
        actives.append(
            jnp.einsum(
                "cnk,ok->cno",
                binned[:, span],
                merge_full[CIN + branch * MID : CIN + (branch + 1) * MID],
                preferred_element_type=jnp.float32,
            )
        )
    grad_merge = jnp.concatenate(merge_rows, axis=0)
    grad_active = jnp.concatenate(actives, axis=1)
    mine = lax.dynamic_slice_in_dim(grad_active, half * wide, wide, 2)
    theirs = lax.dynamic_slice_in_dim(grad_active, (1 - half) * wide, wide, 2)
    grad_active = mine + swap(theirs.astype(jnp.bfloat16))[::-1].astype(jnp.float32)
    gain_rows = []
    bias_rows = []
    branch_columns = []
    pooled_grads = []
    for branch, span in enumerate(spans):
        inverse, centred, normed, entries = stats[branch]
        grad_branch_normed = grad_active[:, span] * silu_slope(normed)
        gain_row = jnp.sum(grad_branch_normed * centred, axis=(0, 1))
        bias_row = jnp.sum(grad_branch_normed, axis=(0, 1))
        gain_rows.append(gain_row)
        bias_rows.append(bias_row)
        grad_out = (
            gains[branch]
            * inverse
            * (grad_branch_normed - (bias_row + centred * gain_row) / entries)
        ).astype(jnp.bfloat16)
        branch_columns.append(
            jnp.einsum(
                "cnd,cno->do", pooled[:, span], grad_out, preferred_element_type=jnp.float32
            ).astype(jnp.bfloat16)
        )
        pooled_grads.append(
            jnp.einsum(
                "cno,do->cnd",
                grad_out,
                branch_full[:, branch * wide : (branch + 1) * wide],
                preferred_element_type=jnp.float32,
            )
        )
    grad_branch = jnp.concatenate(branch_columns, axis=1)
    grad_pooled = (jnp.concatenate(pooled_grads, axis=1) / counts[:, :, None]).astype(jnp.bfloat16)
    grad_masked = dot(spread_grad, merge_full[:CIN], ((1,), (1,))).reshape(pair, PIX, CIN)
    grad_masked = grad_masked + jnp.einsum(
        "cnp,cnd->cpd", pools, grad_pooled, preferred_element_type=jnp.float32
    )
    away = swap(grad_masked[1:].astype(jnp.bfloat16))
    grad_features = (grad_masked[:1] + away.astype(jnp.float32)) * inside_float[:1, :, None]

    share_branch, share_merge = scatter_grads(grad_branch, grad_merge)
    share_branch = whole_rows(share_branch, half, wide)
    share_merge = whole_rows(share_merge, half, wide)

    def placed(value, axis):
        shape = list(value.shape)
        shape[axis] = MID
        return lax.dynamic_update_slice_in_dim(
            jnp.zeros(shape, jnp.float32), value, half * wide, axis
        )

    total_class, total_gain, total_bias = lax.psum(
        (
            placed(grad_class, 0),
            placed(jnp.stack(gain_rows + [gain_merged]), 1),
            placed(jnp.stack(bias_rows + [bias_merged]), 1),
        ),
        ("bn", "fsdp"),
    )
    return (logits, grad_features, share_branch, share_merge, total_class, total_gain, total_bias)


def whole_rows(share, half, wide):
    rows = share.shape[0]
    other = swap(share)
    mine = share.reshape(rows, -1, 1, wide)
    other = other.reshape(rows, -1, 1, wide)
    joined = jnp.where(
        half == 0,
        jnp.concatenate([mine, other], axis=2),
        jnp.concatenate([other, mine], axis=2),
    )
    return joined.reshape(rows, -1).astype(jnp.float32)


def solution(mesh):
    placed = (
        P(("bn", "fsdp"), None, None),
        P(("bn", "fsdp"), None, None),
        P("fsdp", None),
        P("fsdp", None),
        P(),
        P(),
        P(),
        P(("bn", "fsdp"), None, None),
    )
    return jax.shard_map(
        body,
        mesh=mesh,
        in_specs=placed,
        out_specs=(
            P(("bn", "fsdp"), None, None),
            P(("bn", "fsdp"), None, None),
            P("fsdp", None),
            P("fsdp", None),
            P(),
            P(),
            P(),
        ),
        check_vma=False,
    )
```

```python
import jax
import jax.numpy as jnp
from jax import lax
from jax.experimental import pallas as pl
from jax.experimental.pallas import tpu as pltpu
from jax.sharding import PartitionSpec as P

CIN = 2048
MID = 512
CLS = 19
IMG = 4
SIDE_R = 32
SIDE_C = 32
PIX = 1024
TAPS = 9
EPSILON = 1e-05
BIN_COUNTS = (1, 2, 3, 6)
SIZES = tuple(IMG * bins * bins for bins in BIN_COUNTS)
STARTS = (0, 4, 20, 56)
BINS = 200


def region_maps(region_boxes, bins):
    canvases = region_boxes.shape[0]
    top = region_boxes[:, :, 0][:, :, None]
    left = region_boxes[:, :, 1][:, :, None]
    height = region_boxes[:, :, 2][:, :, None]
    width = region_boxes[:, :, 3][:, :, None]
    pixel = jnp.arange(PIX, dtype=jnp.int32)
    rel_row = (pixel // SIDE_C)[None, None, :] - top
    rel_col = (pixel % SIDE_C)[None, None, :] - left
    index = jnp.arange(bins, dtype=jnp.int32)[None, None, :, None]
    row_low = index * height[..., None] // bins
    row_high = ((index + 1) * height[..., None] + bins - 1) // bins
    col_low = index * width[..., None] // bins
    col_high = ((index + 1) * width[..., None] + bins - 1) // bins
    row_in = (rel_row[:, :, None, :] >= row_low) & (rel_row[:, :, None, :] < row_high)
    col_in = (rel_col[:, :, None, :] >= col_low) & (rel_col[:, :, None, :] < col_high)
    pool = (row_in[:, :, :, None, :] & col_in[:, :, None, :, :]).reshape(
        canvases, IMG * bins * bins, PIX
    )
    inside_row = (rel_row >= 0) & (rel_row < height)
    inside_col = (rel_col >= 0) & (rel_col < width)
    near_row = rel_row * bins // height
    near_col = rel_col * bins // width
    up_row = inside_row[:, :, None, :] & (near_row[:, :, None, :] == index)
    up_col = inside_col[:, :, None, :] & (near_col[:, :, None, :] == index)
    upmap = (up_row[:, :, :, None, :] & up_col[:, :, None, :, :]).reshape(
        canvases, IMG * bins * bins, PIX
    )
    inside = jnp.any(inside_row & inside_col, axis=1)
    return (pool, upmap, inside)


def silu_slope(value):
    sigma = jax.nn.sigmoid(value)
    return sigma * (1.0 + value * (1.0 - sigma))


def swap(value):
    return lax.ppermute(value, "bn", [(0, 1), (1, 0)])


def both(value):
    return jnp.concatenate([value, swap(value)], axis=0)


def dot(a, b, dims=((1,), (0,))):
    return lax.dot_general(a, b, (dims, ((), ())), preferred_element_type=jnp.float32)


def rolled(value, shift):
    rows = value.shape[0]
    if shift == 0:
        return value
    pad = jnp.zeros((abs(shift),) + value.shape[1:], value.dtype)
    if shift > 0:
        return jnp.concatenate([value[shift:], pad], axis=0)
    return jnp.concatenate([pad, value[: rows + shift]], axis=0)


def own_half(value, half, width):
    rows = value.shape[0]
    cut = value.reshape(rows, -1, 2, width)
    return lax.dynamic_index_in_dim(cut, half, axis=2, keepdims=False).reshape(rows, -1)


def gather_weights(branch_half, merge_half):
    return (
        lax.all_gather(branch_half, "fsdp", axis=0, tiled=True),
        lax.all_gather(merge_half, "fsdp", axis=0, tiled=True),
    )


def scatter_grads(grad_branch, grad_merge):
    return (
        lax.psum_scatter(grad_branch, "fsdp", scatter_dimension=0, tiled=True),
        lax.psum_scatter(grad_merge, "fsdp", scatter_dimension=0, tiled=True),
    )


def body(features, region_boxes, branch_w, merge_w, class_w, norm_gain, norm_bias, grad_logits):
    half = lax.axis_index("bn")
    wide = MID // 2
    branch_full, merge_full = gather_weights(
        own_half(branch_w, half, wide), own_half(merge_w, half, wide)
    )
    gains = lax.dynamic_slice_in_dim(norm_gain, half * wide, wide, 1).astype(jnp.float32)
    biases = lax.dynamic_slice_in_dim(norm_bias, half * wide, wide, 1).astype(jnp.float32)
    class_half = lax.dynamic_slice_in_dim(class_w, half * wide, wide, 0)
    feats = both(features)
    boxes = both(region_boxes)
    cotangent = both(grad_logits)
    pair = feats.shape[0]
    rows = pair * PIX
    pools = []
    upmaps = []
    inside = None
    for bins in BIN_COUNTS:
        pool, upmap, inside = region_maps(boxes, bins)
        pools.append(pool)
        upmaps.append(upmap)
    counts = jnp.concatenate(
        [jnp.sum(pool.astype(jnp.float32), axis=2) for pool in pools], axis=1
    )
    pools = jnp.concatenate(pools, axis=1).astype(jnp.bfloat16)
    upmaps = jnp.concatenate(upmaps, axis=1).astype(jnp.bfloat16)
    inside_float = inside.astype(jnp.float32)
    weight_in = inside_float.reshape(rows, 1)
    masked = (feats * inside.astype(jnp.bfloat16)[:, :, None]).reshape(rows, CIN)
    pooled_sum = jnp.einsum("cnp,cpd->cnd", pools, feats, preferred_element_type=jnp.float32)
    pooled = (pooled_sum / counts[:, :, None]).astype(jnp.bfloat16)

    spans = [slice(s, s + n) for s, n in zip(STARTS, SIZES)]
    outs = []
    stats = []
    for branch, span in enumerate(spans):
        entries = pair * SIZES[branch]
        value = jnp.einsum(
            "cnd,do->cno",
            pooled[:, span],
            branch_full[:, branch * wide : (branch + 1) * wide],
            preferred_element_type=jnp.float32,
        )
        mean = jnp.sum(value, axis=(0, 1)) / entries
        spread = jnp.sum(value * value, axis=(0, 1)) / entries - mean * mean
        inverse = lax.rsqrt(spread + EPSILON)
        centred = (value - mean) * inverse
        normed = centred * gains[branch] + biases[branch]
        outs.append(jax.nn.silu(normed).astype(jnp.bfloat16))
        stats.append((inverse, centred, normed, entries))
    active = jnp.concatenate(outs, axis=1)
    other = swap(active)
    active_full = jnp.where(
        half == 0,
        jnp.concatenate([active, other[::-1]], axis=2),
        jnp.concatenate([other[::-1], active], axis=2),
    )
    lifted = jnp.concatenate(
        [
            jnp.einsum(
                "cno,ok->cnk",
                active_full[:, span],
                merge_full[CIN + branch * MID : CIN + (branch + 1) * MID],
                preferred_element_type=jnp.float32,
            ).astype(jnp.bfloat16)
            for branch, span in enumerate(spans)
        ],
        axis=1,
    )
    spans_up = jnp.swapaxes(upmaps, 1, 2).reshape(rows, BINS)
    strip = 3 * wide
    column = jnp.zeros((rows, strip), jnp.float32)
    for dr in range(3):
        shift = (dr - 1) * SIDE_C
        cut = slice(dr * strip, (dr + 1) * strip)
        column = column + dot(rolled(masked, shift), merge_full[:CIN, cut])
        raised = rolled(spans_up, shift).reshape(pair, PIX, BINS)
        column = column + jnp.einsum(
            "cpn,cnk->cpk", raised, lifted[:, :, cut], preferred_element_type=jnp.float32
        ).reshape(rows, strip)
    convolved = (
        rolled(column[:, :wide], -1)
        + column[:, wide : 2 * wide]
        + rolled(column[:, 2 * wide :], 1)
    )
    pixel_count = jnp.sum(inside_float)
    mean_merged = jnp.sum(convolved * weight_in, axis=0) / pixel_count
    spread_merged = (
        jnp.sum(convolved * convolved * weight_in, axis=0) / pixel_count
        - mean_merged * mean_merged
    )
    inverse_merged = lax.rsqrt(spread_merged + EPSILON)
    centred_merged = (convolved - mean_merged) * inverse_merged
    normed_merged = centred_merged * gains[4] + biases[4]
    hidden = jax.nn.silu(normed_merged).astype(jnp.bfloat16)
    logits_part = (dot(hidden, class_half) * weight_in).reshape(pair, PIX, CLS)
    logits = logits_part[:1] + swap(logits_part[1:])

    masked_grad = (cotangent * inside.astype(jnp.bfloat16)[:, :, None]).reshape(rows, CLS)
    grad_class = dot(hidden, masked_grad, ((0,), (0,)))
    grad_hidden = dot(masked_grad, class_half, ((1,), (1,)))
    grad_normed = grad_hidden * silu_slope(normed_merged)
    gain_merged = jnp.sum(grad_normed * centred_merged * weight_in, axis=0)
    bias_merged = jnp.sum(grad_normed * weight_in, axis=0)
    grad_conv = (
        weight_in
        * gains[4]
        * inverse_merged
        * (grad_normed - (bias_merged + centred_merged * gain_merged) / pixel_count)
    ).astype(jnp.bfloat16)
    spread_grad = jnp.concatenate(
        [
            rolled(grad_conv, -((tap // 3 - 1) * SIDE_C + (tap % 3 - 1)))
            for tap in range(TAPS)
        ],
        axis=1,
    )
    binned = jnp.einsum(
        "cnp,cpk->cnk",
        upmaps,
        spread_grad.reshape(pair, PIX, TAPS * wide),
        preferred_element_type=jnp.float32,
    ).astype(jnp.bfloat16)
    merge_rows = [dot(masked, spread_grad, ((0,), (0,))).astype(jnp.bfloat16)]
    actives = []
    for branch, span in enumerate(spans):
        merge_rows.append(
            jnp.einsum(
                "cno,cnk->ok",
                active_full[:, span],
                binned[:, span],
                preferred_element_type=jnp.float32,
            ).astype(jnp.bfloat16)
        )
        actives.append(
            jnp.einsum(
                "cnk,ok->cno",
                binned[:, span],
                merge_full[CIN + branch * MID : CIN + (branch + 1) * MID],
                preferred_element_type=jnp.float32,
            )
        )
    grad_merge = jnp.concatenate(merge_rows, axis=0)
    grad_active = jnp.concatenate(actives, axis=1)
    mine = lax.dynamic_slice_in_dim(grad_active, half * wide, wide, 2)
    theirs = lax.dynamic_slice_in_dim(grad_active, (1 - half) * wide, wide, 2)
    grad_active = mine + swap(theirs.astype(jnp.bfloat16))[::-1].astype(jnp.float32)
    gain_rows = []
    bias_rows = []
    branch_columns = []
    pooled_grads = []
    for branch, span in enumerate(spans):
        inverse, centred, normed, entries = stats[branch]
        grad_branch_normed = grad_active[:, span] * silu_slope(normed)
        gain_row = jnp.sum(grad_branch_normed * centred, axis=(0, 1))
        bias_row = jnp.sum(grad_branch_normed, axis=(0, 1))
        gain_rows.append(gain_row)
        bias_rows.append(bias_row)
        grad_out = (
            gains[branch]
            * inverse
            * (grad_branch_normed - (bias_row + centred * gain_row) / entries)
        ).astype(jnp.bfloat16)
        branch_columns.append(
            jnp.einsum(
                "cnd,cno->do", pooled[:, span], grad_out, preferred_element_type=jnp.float32
            ).astype(jnp.bfloat16)
        )
        pooled_grads.append(
            jnp.einsum(
                "cno,do->cnd",
                grad_out,
                branch_full[:, branch * wide : (branch + 1) * wide],
                preferred_element_type=jnp.float32,
            )
        )
    grad_branch = jnp.concatenate(branch_columns, axis=1)
    grad_pooled = (jnp.concatenate(pooled_grads, axis=1) / counts[:, :, None]).astype(jnp.bfloat16)
    grad_masked = dot(spread_grad, merge_full[:CIN], ((1,), (1,))).reshape(pair, PIX, CIN)
    grad_masked = grad_masked + jnp.einsum(
        "cnp,cnd->cpd", pools, grad_pooled, preferred_element_type=jnp.float32
    )
    away = swap(grad_masked[1:].astype(jnp.bfloat16))
    grad_features = (grad_masked[:1] + away.astype(jnp.float32)) * inside_float[:1, :, None]

    share_branch, share_merge = scatter_grads(grad_branch, grad_merge)
    share_branch = whole_rows(share_branch, half, wide)
    share_merge = whole_rows(share_merge, half, wide)

    def placed(value, axis):
        shape = list(value.shape)
        shape[axis] = MID
        return lax.dynamic_update_slice_in_dim(
            jnp.zeros(shape, jnp.float32), value, half * wide, axis
        )

    total_class, total_gain, total_bias = lax.psum(
        (
            placed(grad_class, 0),
            placed(jnp.stack(gain_rows + [gain_merged]), 1),
            placed(jnp.stack(bias_rows + [bias_merged]), 1),
        ),
        ("bn", "fsdp"),
    )
    return (logits, grad_features, share_branch, share_merge, total_class, total_gain, total_bias)


def whole_rows(share, half, wide):
    rows = share.shape[0]
    other = swap(share)
    mine = share.reshape(rows, -1, 1, wide)
    other = other.reshape(rows, -1, 1, wide)
    joined = jnp.where(
        half == 0,
        jnp.concatenate([mine, other], axis=2),
        jnp.concatenate([other, mine], axis=2),
    )
    return joined.reshape(rows, -1).astype(jnp.float32)


MESH = pl.DeviceIdType.MESH
LINE, QUAD, WIDE = 4, 4, 256
CUT = 7 * WIDE

def place():
    half = lax.axis_index("bn"); f = lax.axis_index("fsdp")
    z = f // QUAD; q = f % QUAD
    return half, f, z, q

def turn(z, step):
    if step == 0: return z
    if step == 1: return z + 1 - 2 * (z % 2)
    if step == 2: return 2 - z // 2
    return 3 - 3 * (z // 2)

def greet(half, f, z, q):
    bar = pltpu.get_barrier_semaphore()
    xq = q + 1 - 2 * (q % 2); yq = q + 2 - 4 * (q // 2)
    for t in ((half, z * QUAD + xq), (half, z * QUAD + yq), (1 - half, f)):
        pl.semaphore_signal(bar, inc=1, device_id=t, device_id_type=MESH)
    @pl.when(z < LINE - 1)
    def _(): pl.semaphore_signal(bar, inc=1, device_id=(half, f + QUAD), device_id_type=MESH)
    @pl.when(z > 0)
    def _(): pl.semaphore_signal(bar, inc=1, device_id=(half, f - QUAD), device_id_type=MESH)
    many = 5 - (z // (LINE - 1)) - ((LINE - 1 - z) // (LINE - 1))
    pl.semaphore_wait(bar, many)

def gather_kernel(merge_ref, branch_ref, merge_out, branch_out, branch_own, merge_own, local_sem, z_send, z_recv, q_send, q_recv, zb_send, zb_recv):
    half, f, z, q = place()
    xq = q + 1 - 2 * (q % 2); yq = q + 2 - 4 * (q // 2); dq = 3 - q
    greet(half, f, z, q)
    own_copies = [
        pltpu.make_async_copy(branch_ref.at[:, pl.ds(pl.multiple_of(t * MID + half * WIDE, WIDE), WIDE)], branch_own.at[:, pl.ds(t * WIDE, WIDE)], local_sem.at[t]) for t in range(4)
    ] + [
        pltpu.make_async_copy(merge_ref.at[:, pl.ds(pl.multiple_of(t * MID + half * WIDE, WIDE), WIDE)], merge_own.at[:, pl.ds(t * WIDE, WIDE)], local_sem.at[4 + t]) for t in range(9)
    ]
    for c in own_copies: c.start()
    for c in own_copies: c.wait()
    keep = [pltpu.make_async_copy(branch_own, branch_out.at[f], local_sem.at[0]), pltpu.make_async_copy(merge_own, merge_out.at[f], local_sem.at[1])]
    for c in keep: c.start()

    def piece(kind, owner, part=None):
        rows = 128 if kind == 0 else 256
        ds = slice(None) if part is None else pl.ds(part * (rows // 2), rows // 2)
        if kind == 0: return branch_out.at[owner, ds]
        return merge_out.at[owner, ds, pl.ds(0, CUT) if kind == 1 else pl.ds(CUT, 2 * WIDE)]

    def own_piece(kind):
        if kind == 0: return branch_own
        return merge_own.at[:, pl.ds(0, CUT) if kind == 1 else pl.ds(CUT, 2 * WIDE)]

    def remote(ref, s, r, dev, src=None):
        return pltpu.make_async_remote_copy(src_ref=ref if src is None else src, dst_ref=ref, send_sem=s, recv_sem=r, device_id=dev, device_id_type=MESH)

    def z_copy(kind, level, d):
        return remote(piece(kind, level * QUAD + q), z_send.at[kind, d, level], z_recv.at[kind, level], (half, f + QUAD if d == 0 else f - QUAD), own_piece(kind) if level is z else None)
    def zb_copy(level, c, d):
        return remote(piece(2, level * QUAD + c), zb_send.at[d, level, c], zb_recv.at[level, c], (half, f + QUAD if d == 0 else f - QUAD))
    def z_both(level, fn):
        @pl.when((level <= z) & (z < LINE - 1))
        def _(): fn(0)
        @pl.when((level >= z) & (z > 0))
        def _(): fn(1)
    def q_copy(kind, level, axis, what):
        dev = (half, z * QUAD + (xq if axis == 0 else yq))
        if what == 0: ref = piece(kind, level * QUAD + q)
        else: ref = piece(kind, level * QUAD + (yq if axis == 0 else xq), 1 - axis)
        return remote(ref, q_send.at[kind, level, axis, what], q_recv.at[kind, level, axis, what], dev, own_piece(kind) if level is z and what == 0 else None)
    def q_arrive(kind, level, axis, what):
        if what == 0: ref = piece(kind, level * QUAD + (xq if axis == 0 else yq))
        else: ref = piece(kind, level * QUAD + dq, 1 - axis)
        remote(ref, q_send.at[kind, level, axis, what], q_recv.at[kind, level, axis, what], (half, z * QUAD + xq)).wait_recv()
    def z_arrive(kind, level):
        remote(piece(kind, level * QUAD + q), z_send.at[kind, 0, level], z_recv.at[kind, level], (half, f)).wait_recv()
    def zb_arrive(level, c):
        remote(piece(2, level * QUAD + c), zb_send.at[0, level, c], zb_recv.at[level, c], (half, f)).wait_recv()

    L = [turn(z, i) for i in range(LINE)]
    def spread(kind, level):
        for axis in (0, 1): q_copy(kind, level, axis, 0).start()
    def pass_on(kind, level):
        q_arrive(kind, level, 0, 0); q_copy(kind, level, 1, 1).start()
        q_arrive(kind, level, 1, 0); q_copy(kind, level, 0, 1).start()
    def z_step(kind, i):
        if i: z_arrive(kind, L[i])
        z_both(L[i], lambda d: z_copy(kind, L[i], d).start())
    def zb_step(i):
        for c in range(QUAD):
            if i: zb_arrive(L[i], c)
            z_both(L[i], lambda d, c=c: zb_copy(L[i], c, d).start())
    def corner(kind, level):
        q_arrive(kind, level, 0, 1); q_arrive(kind, level, 1, 1)

    z_step(0, 0); spread(0, L[0])
    z_step(1, 0); spread(2, L[0]); spread(1, L[0])
    pass_on(0, L[0]); pass_on(2, L[0])
    z_step(0, 1); spread(0, L[1])
    z_step(1, 1); spread(1, L[1])
    pass_on(1, L[0])
    corner(0, L[0]); corner(2, L[0])
    pass_on(0, L[1])
    z_step(0, 2); spread(0, L[2])
    z_step(1, 2); spread(1, L[2])
    for c in keep: c.wait()
    zb_step(0)
    pass_on(1, L[1])
    corner(1, L[0])
    z_step(0, 3); spread(0, L[3])
    z_step(1, 3); spread(1, L[3])
    zb_step(1)
    pass_on(0, L[2]); pass_on(1, L[2])
    corner(0, L[1]); corner(1, L[1])
    zb_step(2)
    pass_on(0, L[3]); pass_on(1, L[3])
    corner(0, L[2]); corner(1, L[2])
    zb_step(3)
    corner(0, L[3]); corner(1, L[3])

    for i in range(LINE):
        for kind in (0, 1):
            z_both(L[i], lambda d: z_copy(kind, L[i], d).wait_send())
        for c in range(QUAD):
            z_both(L[i], lambda d, c=c: zb_copy(L[i], c, d).wait_send())
        for kind in (0, 1) + ((2,) if i == 0 else ()):
            for axis in (0, 1):
                for what in (0, 1):
                    q_copy(kind, L[i], axis, what).wait_send()

def gather_call(branch_w, merge_w, cid=0):
    D = pltpu.SemaphoreType.DMA
    merge, branch = pl.pallas_call(
        gather_kernel,
        out_shape=(jax.ShapeDtypeStruct((16, 256, TAPS * WIDE), jnp.bfloat16), jax.ShapeDtypeStruct((16, 128, 4 * WIDE), jnp.bfloat16)),
        in_specs=[pl.BlockSpec(memory_space=pl.ANY)] * 2,
        out_specs=(pl.BlockSpec(memory_space=pl.ANY),) * 2,
        scratch_shapes=[pltpu.VMEM((128, 4 * WIDE), jnp.bfloat16), pltpu.VMEM((256, TAPS * WIDE), jnp.bfloat16), D((13,)), D((2, 2, 4)), D((2, 4)), D((3, 4, 2, 2)), D((3, 4, 2, 2)), D((2, 4, 4)), D((4, 4))],
        compiler_params=pltpu.CompilerParams(collective_id=cid, has_side_effects=True),
        name="gather",
    )(merge_w, branch_w)
    return branch, merge


BF = jnp.bfloat16
F32 = jnp.float32
ROWS = 2048
STRIP = 3 * WIDE
PAIRBINS = 512

def scatter_kernel(xt_hbm, d3_hbm, at_hbm, ud_hbm, br_hbm, w_hbm, merge_out, branch_out, own_out, far_out,
                   xt, d3, ud, g0, g1, b_all, fx0, fy0, fx1, fy1, fx2, fy2, zs0, zs1, zs2, wbuf, own_stage, far_stage,
                   local_sem, q_send, q_recv, z_send, z_recv, zb_send, zb_recv, end_send, end_recv, w_sem, own_sem, far_send, far_recv, br_sem, end_local):
    half, f, z, q = place()
    xq = q + 1 - 2 * (q % 2); yq = q + 2 - 4 * (q // 2); dq = 3 - q
    L = [turn(z, i) for i in range(LINE)]
    loads = [pltpu.make_async_copy(a, b, local_sem.at[n]) for n, (a, b) in enumerate(((d3_hbm, d3), (ud_hbm, ud)))]
    for c in loads: c.start()
    def load_w(n): return pltpu.make_async_copy(w_hbm.at[n], wbuf.at[n % 2], w_sem.at[n % 2])
    load_w(0).start()
    from_x = (fx0, fx1, fx2); from_y = (fy0, fy1, fy2); zslot = (zs0, zs1, zs2)
    HALF = (64, 128, 128)
    def fetch_rows(i):
        level = L[i]
        fine = pl.multiple_of((level % 2) * 1024, 1024)
        def feature(): return pltpu.make_async_copy(xt_hbm.at[pl.ds(fine, 1024)], xt, local_sem.at[2])
        def raised(): return pltpu.make_async_copy(at_hbm.at[pl.ds(fine, 1024)], xt.at[:, pl.ds(0, PAIRBINS)], local_sem.at[2])
        return feature, raised
    def rows_start(i):
        feature, raised = fetch_rows(i)
        @pl.when(L[i] < 2)
        def _(): feature().start()
        @pl.when(L[i] >= 2)
        def _(): raised().start()
    rows_start(3)
    greet(half, f, z, q)
    for c in loads: c.wait()

    def produce(i, after=None):
        level = L[i]
        feature, raised = fetch_rows(i)
        def store(t, value):
            value = value.astype(BF).reshape(QUAD, 256, WIDE)
            return value
        def loops(dot):
            def a_part(t, _):
                g1[i % 2, :, :, pl.ds(pl.multiple_of(t * WIDE, WIDE), WIDE)] = dot(t).astype(BF).reshape(QUAD, 256, WIDE)
                return 0
            def b_part(t, _):
                b_all[pl.ds(level * QUAD, QUAD), :, pl.ds(pl.multiple_of((t - 7) * WIDE, WIDE), WIDE)] = dot(t).astype(BF).reshape(QUAD, 256, WIDE)
                return 0
            lax.fori_loop(7, TAPS, b_part, 0)
            lax.fori_loop(0, 7, a_part, 0)
        @pl.when(level < 2)
        def _():
            feature().wait()
            loops(lambda t: jnp.dot(xt[...], d3[pl.ds(pl.multiple_of(32 * (2 - t // 3), 32), ROWS), pl.ds(pl.multiple_of((t % 3) * WIDE, WIDE), WIDE)], preferred_element_type=F32))
        @pl.when(level >= 2)
        def _():
            raised().wait()
            loops(lambda t: jnp.dot(xt[:, 0:PAIRBINS], ud[:, pl.ds(pl.multiple_of(t * WIDE, WIDE), WIDE)], preferred_element_type=F32))
        if i: rows_start(i - 1)

    def br_load(i): return pltpu.make_async_copy(br_hbm.at[pl.ds(L[i] * QUAD, QUAD)], g0.at[i % 2], br_sem.at[i % 2])

    def own(kind, i, c):
        if kind == 0: return g0.at[i % 2, c]
        if kind == 1: return g1.at[i % 2, c]
        return b_all.at[L[i] * QUAD + c]
    def part(ref, kind, h): return ref.at[pl.ds(h * HALF[kind], HALF[kind])]
    def slot(kind, i, axis, what):
        ref = (from_x, from_y)[axis][kind]
        return ref.at[L[i], what] if kind < 2 else ref.at[0, what]
    def q_copy(kind, i, axis, what):
        to = xq if axis == 0 else yq
        if what == 0: src = part(own(kind, i, dq), kind, 1 - axis)
        elif what == 1: src = part(own(kind, i, to), kind, axis)
        else: src = part(own(kind, i, to), kind, 1 - axis)
        return pltpu.make_async_remote_copy(src_ref=src, dst_ref=slot(kind, i, axis, what), send_sem=q_send.at[kind, L[i], axis, what], recv_sem=q_recv.at[kind, L[i], axis, what], device_id=(half, z * QUAD + to), device_id_type=MESH)
    def add_into(dst, *others):
        rows = dst.shape[0]
        def block(n, _):
            at_ = pl.ds(pl.multiple_of(n * 16, 16), 16)
            total = dst[at_, :].astype(F32)
            for o in others: total = total + o[at_, :].astype(F32)
            dst[at_, :] = total.astype(BF)
            return 0
        lax.fori_loop(0, rows // 16, block, 0)
    def raw(kind, i):
        for what in (0, 2):
            for axis in (0, 1): q_copy(kind, i, axis, what).start()
    def fold(kind, i):
        for axis in (1, 0):
            q_copy(kind, i, axis, 0).wait_recv()
            to = xq if axis == 1 else yq
            add_into(part(own(kind, i, to), kind, 1 - axis), slot(kind, i, axis, 0))
            q_copy(kind, i, 1 - axis, 1).start()
    def gathered(kind, i):
        for axis in (0, 1):
            for what in (1, 2): q_copy(kind, i, axis, what).wait_recv()
        mine = own(kind, i, q)
        add_into(slot(kind, i, 0, 1), part(mine, kind, 0), slot(kind, i, 1, 2))
        add_into(slot(kind, i, 0, 2), part(mine, kind, 1), slot(kind, i, 1, 1))
    def total(kind, i): return from_x[kind].at[L[i] if kind < 2 else 0, pl.ds(1, 2)]
    def z_src(kind, i, c): return total(kind, i) if kind < 2 else own(2, i, c)
    def z_dst(kind, n, c): return zslot[kind].at[n] if kind < 2 else zs2.at[n, c]
    def z_sems(kind, level, n, c):
        if kind < 2: return z_send.at[kind, level], z_recv.at[kind, n]
        return zb_send.at[level, c], zb_recv.at[n, c]
    def z_copy(kind, i, c, up):
        level = L[i]
        n = level if up else level + (LINE - level) * (1 - jnp.minimum(z - 1 - level, 1))
        s, r = z_sems(kind, level, n, c)
        return pltpu.make_async_remote_copy(src_ref=z_src(kind, i, c), dst_ref=z_dst(kind, n, c), send_sem=s, recv_sem=r, device_id=(half, f + QUAD if up else f - QUAD), device_id_type=MESH)
    def z_take(kind, i, n, c):
        s, r = z_sems(kind, L[i], n, c)
        pltpu.make_async_remote_copy(src_ref=z_src(kind, i, c), dst_ref=z_dst(kind, n, c), send_sem=s, recv_sem=r, device_id=(half, f), device_id_type=MESH).wait_recv()
        if kind < 2:
            for h in (0, 1): add_into(total(kind, i).at[h], z_dst(kind, n, c).at[h])
        else: add_into(own(2, i, c), z_dst(kind, n, c))
    def early(kind, i, c=None):
        @pl.when((L[i] > z) & (z == 0))
        def _(): z_copy(kind, i, c, True).start()
        @pl.when((L[i] < z) & (z == LINE - 1))
        def _(): z_copy(kind, i, c, False).start()
    def late(kind, i, c=None):
        @pl.when((L[i] > z) & (z > 0))
        def _():
            z_take(kind, i, L[i], c)
            z_copy(kind, i, c, True).start()
        @pl.when((L[i] < z) & (z < LINE - 1))
        def _():
            z_take(kind, i, L[i], c)
            z_copy(kind, i, c, False).start()
    def home(kind, c=None):
        @pl.when(z > 0)
        def _(): z_take(kind, 0, z, c)
        @pl.when(z < LINE - 1)
        def _(): z_take(kind, 0, LINE, c)
    def line_sent(kind, i, c=None):
        @pl.when(L[i] > z)
        def _(): z_copy(kind, i, c, True).wait_send()
        @pl.when(L[i] < z)
        def _(): z_copy(kind, i, c, False).wait_send()
    def quad_sent(kind, i):
        for axis in (0, 1):
            for what in (0, 1, 2): q_copy(kind, i, axis, what).wait_send()
    def early_b(i):
        for c in range(QUAD): early(2, i, c)
    def late_b(i):
        for c in range(QUAD): late(2, i, c)

    def own_copy(n): return pltpu.make_async_copy(own_stage.at[n % 2], own_out.at[:, pl.ds(pl.multiple_of(n * WIDE, WIDE), WIDE)], own_sem.at[n % 2])
    def far_copy(n): return pltpu.make_async_remote_copy(src_ref=far_stage.at[n % 2], dst_ref=far_out.at[:, pl.ds(pl.multiple_of(n * WIDE, WIDE), WIDE)], send_sem=far_send.at[n % 2], recv_sem=far_recv.at[n], device_id=(1 - half, f), device_id_type=MESH)
    def jobs(first, last):
        def job(n, _):
            load_w(n).wait()
            @pl.when(n < 7)
            def _(): load_w(n + 1).start()
            @pl.when(n >= 2)
            def _():
                own_copy(n - 2).wait(); far_copy(n - 2).wait_send()
            for canvas in (0, 1):
                value = None
                for dr in range(3):
                    p = lax.dot_general(d3[pl.ds(32 * (2 - dr) + canvas * PIX, PIX), :], wbuf[n % 2, :, dr * STRIP:(dr + 1) * STRIP], (((1,), (1,)), ((), ())), preferred_element_type=F32)
                    value = p if value is None else value + p
                if canvas == 0: own_stage[n % 2] = value
                else: far_stage[n % 2] = value.astype(BF)
            own_copy(n).start(); far_copy(n).start()
            return 0
        lax.fori_loop(first, last, job, 0)

    br_load(3).start(); br_load(2).start()
    produce(3); raw(1, 3); early_b(3)
    produce(2); early_b(2)
    fold(1, 3); raw(1, 2)
    br_load(3).wait(); raw(0, 3)
    jobs(0, 3)
    gathered(1, 3); early(1, 3); late_b(3)
    quad_sent(1, 3); produce(1); early_b(1)
    fold(1, 2); raw(1, 1); fold(0, 3)
    br_load(2).wait(); raw(0, 2)
    late(1, 3); late_b(2)
    gathered(0, 3); early(0, 3)
    jobs(3, 6)
    gathered(1, 2); early(1, 2)
    quad_sent(1, 2); quad_sent(0, 3); br_load(1).start()
    produce(0)
    fold(1, 1); raw(1, 0); fold(0, 2)
    br_load(1).wait(); raw(0, 1)
    late(0, 3); late(1, 2); late_b(1)
    jobs(6, 8)
    gathered(0, 2); early(0, 2)
    quad_sent(0, 2); br_load(0).start()
    gathered(1, 1); early(1, 1)
    fold(1, 0); fold(0, 1)
    br_load(0).wait(); raw(0, 0)
    for c in range(QUAD): home(2, c)
    raw(2, 0)
    gathered(0, 1); early(0, 1); late(0, 2)
    late(1, 1); late(0, 1)
    fold(0, 0); fold(2, 0)
    gathered(1, 0); gathered(0, 0); gathered(2, 0)
    home(1); home(0)

    ends = []
    def give(src, dst, column, n):
        def into(h): return dst.at[:, :, pl.ds(pl.multiple_of(column * MID + h * WIDE, WIDE), WIDE)]
        c = pltpu.make_async_remote_copy(src_ref=src, dst_ref=into(half), send_sem=end_send.at[n], recv_sem=end_recv.at[n], device_id=(1 - half, f), device_id_type=MESH)
        c.start()
        k = pltpu.make_async_copy(src, into(half), end_local.at[n])
        k.start()
        back = pltpu.make_async_remote_copy(src_ref=src, dst_ref=into(1 - half), send_sem=end_send.at[n], recv_sem=end_recv.at[n], device_id=(1 - half, f), device_id_type=MESH)
        ends.append((c, k, back))
    for t in range(TAPS):
        if t < 7: src = total(1, 0).at[:, :, pl.ds(t * WIDE, WIDE)]
        else: src = total(2, 0).at[:, :, pl.ds((t - 7) * WIDE, WIDE)]
        give(src, merge_out, t, t)
    for t in range(4):
        give(total(0, 0).at[:, :, pl.ds(t * WIDE, WIDE)], branch_out, t, TAPS + t)
    for i in range(LINE):
        if i < 2: quad_sent(0, i)
        if i < 2: quad_sent(1, i)
        if i:
            line_sent(0, i); line_sent(1, i)
            for c in range(QUAD): line_sent(2, i, c)
    quad_sent(2, 0)
    for n in (6, 7):
        own_copy(n).wait(); far_copy(n).wait_send()
    for n in range(8): far_copy(n).wait_recv()
    for c, k, back in ends:
        c.wait_send(); k.wait(); back.wait_recv()

def scatter_call(xt, d3, at, ud, br, w, cid=2):
    D = pltpu.SemaphoreType.DMA
    V = lambda *s: pltpu.VMEM(s, BF)
    return pl.pallas_call(
        scatter_kernel,
        out_shape=(jax.ShapeDtypeStruct((2, 128, TAPS * MID), BF), jax.ShapeDtypeStruct((2, 64, 4 * MID), BF), jax.ShapeDtypeStruct((PIX, CIN), F32), jax.ShapeDtypeStruct((PIX, CIN), BF)),
        in_specs=[pl.BlockSpec(memory_space=pl.ANY)] * 6,
        out_specs=(pl.BlockSpec(memory_space=pl.ANY),) * 4,
        scratch_shapes=[V(1024, ROWS), V(ROWS + 64, STRIP), V(PAIRBINS, TAPS * WIDE), V(2, 4, 128, 1024), V(2, 4, 256, CUT), V(16, 256, 512),
            V(4, 3, 64, 1024), V(4, 3, 64, 1024), V(4, 3, 128, CUT), V(4, 3, 128, CUT), V(1, 3, 128, 512), V(1, 3, 128, 512),
            V(5, 2, 64, 1024), V(5, 2, 128, CUT), V(5, 4, 256, 512), V(2, 256, TAPS * WIDE), pltpu.VMEM((2, PIX, WIDE), F32), V(2, PIX, WIDE),
            D((3,)), D((3, 4, 2, 3)), D((3, 4, 2, 3)), D((2, 4)), D((2, 5)), D((4, 4)), D((5, 4)), D((13,)), D((13,)), D((2,)), D((2,)), D((2,)), D((8,)), D((2,)), D((13,))],
        compiler_params=pltpu.CompilerParams(collective_id=cid, has_side_effects=True, vmem_limit_bytes=63 * 1024 * 1024),
        name="scatter",
    )(xt, d3, at, ud, br, w)


SPANS = ((0, 4, 16), (16, 16, 16), (32, 36, 48), (80, 144, 176))
NB = 256


def bin_bounds(region_boxes):
    canvases = region_boxes.shape[0]
    top, left, height, width = (region_boxes[:, :, n] for n in range(4))
    tables = []
    for (_, size, room), bins in zip(SPANS, BIN_COUNTS):
        index = jnp.arange(bins, dtype=jnp.int32)[None, None]

        def bounds(start, extent):
            start, extent = start[:, :, None], extent[:, :, None]
            return (
                start + index * extent // bins,
                start + ((index + 1) * extent + bins - 1) // bins,
                start + (index * extent + bins - 1) // bins,
                start + ((index + 1) * extent + bins - 1) // bins,
            )

        shape = (canvases, IMG, bins, bins)
        rows = [jnp.broadcast_to(v[:, :, :, None], shape) for v in bounds(top, height)]
        cols = [jnp.broadcast_to(v[:, :, None, :], shape) for v in bounds(left, width)]
        table = jnp.stack(rows + cols, axis=-1).reshape(canvases, size, 8)
        tables.append(jnp.pad(table, ((0, 0), (0, room - size), (0, 0))))
    return jnp.concatenate(tables, axis=1)


def paired(features, region_boxes, branch_w, merge_w, class_w, norm_gain, norm_bias, grad_logits):
    half = lax.axis_index("bn")
    branch_g, merge_g = gather_call(branch_w, merge_w)
    branch_full = branch_g.reshape(CIN, 4 * WIDE)
    merge_full = merge_g.reshape(2 * CIN, TAPS * WIDE)
    gains = lax.dynamic_slice_in_dim(norm_gain, half * WIDE, WIDE, 1).astype(jnp.float32)
    biases = lax.dynamic_slice_in_dim(norm_bias, half * WIDE, WIDE, 1).astype(jnp.float32)
    class_half = lax.dynamic_slice_in_dim(class_w, half * WIDE, WIDE, 0)
    feats = both(features)
    boxes = both(region_boxes)
    cotangent = both(grad_logits)
    pair = 2
    rows = ROWS
    bounds = bin_bounds(boxes)
    pixel = jnp.arange(PIX, dtype=jnp.int32)
    prow, pcol = pixel // SIDE_C, pixel % SIDE_C
    low = lambda n: bounds[:, :, n][:, :, None]
    pools = (
        (prow >= low(0)) & (prow < low(1)) & (pcol >= low(4)) & (pcol < low(5))
    )
    upmaps = (prow >= low(2)) & (prow < low(3)) & (pcol >= low(6)) & (pcol < low(7))
    inside = jnp.any(upmaps[:, :IMG], axis=1)
    counts = jnp.maximum(jnp.sum(pools.astype(jnp.float32), axis=2), 1.0)
    pools = pools.astype(BF)
    upmaps = upmaps.astype(BF)
    inside_float = inside.astype(jnp.float32)
    weight_in = inside_float.reshape(rows, 1)
    masked = (feats * inside.astype(BF)[:, :, None]).reshape(rows, CIN)
    pooled_sum = jnp.einsum("cnp,cpd->cnd", pools, feats, preferred_element_type=F32)
    pooled = (pooled_sum / counts[:, :, None]).astype(BF)
    branch_of = [0] * 16 + [1] * 16 + [2] * 48 + [3] * 176
    chosen = (jnp.asarray(branch_of)[:, None] == jnp.arange(4)[None, :])

    def choose(value, width):
        cut = value.reshape(pair, NB, 4, width)
        return jnp.sum(jnp.where(chosen[None, :, :, None], cut, 0), axis=2)

    def widen(value):
        cut = jnp.where(chosen[None, :, :, None], value[:, :, None, :], 0)
        return cut.reshape(pair * NB, 4 * value.shape[2])

    value = choose(dot(pooled.reshape(pair * NB, CIN), branch_full).reshape(pair, NB, -1), WIDE)
    centred, normed, inverse, entries = [], [], [], []
    for branch, (start, size, room) in enumerate(SPANS):
        count = pair * size
        cut = value[:, start : start + room]
        mean = jnp.sum(cut, axis=(0, 1)) / count
        spread = jnp.sum(cut * cut, axis=(0, 1)) / count - mean * mean
        inv = lax.rsqrt(spread + EPSILON)
        c = (cut - mean) * inv
        centred.append(c)
        normed.append(c * gains[branch] + biases[branch])
        inverse.append(inv)
        entries.append(count)
    active = jax.nn.silu(jnp.concatenate(normed, axis=1)).astype(BF)
    other = swap(active)[::-1]
    active_full = jnp.where(
        half == 0,
        jnp.concatenate([active, other], axis=2),
        jnp.concatenate([other, active], axis=2),
    )
    wide_active = widen(active_full)
    lifted = dot(wide_active, merge_full[CIN:]).astype(BF).reshape(pair, NB, TAPS * WIDE)
    spans_up = jnp.swapaxes(upmaps, 1, 2).reshape(rows, NB)
    column = jnp.zeros((rows, STRIP), F32)
    for dr in range(3):
        shift = (dr - 1) * SIDE_C
        cut = slice(dr * STRIP, (dr + 1) * STRIP)
        column = column + dot(rolled(masked, shift), merge_full[:CIN, cut])
        raised = rolled(spans_up, shift).reshape(pair, PIX, NB)
        column = column + jnp.einsum(
            "cpn,cnk->cpk", raised, lifted[:, :, cut], preferred_element_type=F32
        ).reshape(rows, STRIP)
    convolved = (
        rolled(column[:, :WIDE], -1) + column[:, WIDE : 2 * WIDE] + rolled(column[:, 2 * WIDE :], 1)
    )
    pixel_count = jnp.sum(inside_float)
    mean_merged = jnp.sum(convolved * weight_in, axis=0) / pixel_count
    spread_merged = (
        jnp.sum(convolved * convolved * weight_in, axis=0) / pixel_count
        - mean_merged * mean_merged
    )
    inverse_merged = lax.rsqrt(spread_merged + EPSILON)
    centred_merged = (convolved - mean_merged) * inverse_merged
    normed_merged = centred_merged * gains[4] + biases[4]
    hidden = jax.nn.silu(normed_merged).astype(BF)
    logits_part = (dot(hidden, class_half) * weight_in).reshape(pair, PIX, CLS)
    logits = logits_part[:1] + swap(logits_part[1:])

    masked_grad = (cotangent * inside.astype(BF)[:, :, None]).reshape(rows, CLS)
    grad_class = dot(hidden, masked_grad, ((0,), (0,)))
    grad_hidden = dot(masked_grad, class_half, ((1,), (1,)))
    grad_normed = grad_hidden * silu_slope(normed_merged)
    gain_merged = jnp.sum(grad_normed * centred_merged * weight_in, axis=0)
    bias_merged = jnp.sum(grad_normed * weight_in, axis=0)
    grad_conv = (
        weight_in
        * gains[4]
        * inverse_merged
        * (grad_normed - (bias_merged + centred_merged * gain_merged) / pixel_count)
    ).astype(BF)
    spread_grad = jnp.concatenate(
        [rolled(grad_conv, 1), grad_conv, rolled(grad_conv, -1)], axis=1
    )
    spread_grad = jnp.pad(spread_grad, ((32, 32), (0, 0)))
    binned = jnp.concatenate(
        [
            jnp.einsum(
                "cnp,cpk->cnk",
                upmaps,
                spread_grad[32 * (2 - dr) : 32 * (2 - dr) + rows].reshape(pair, PIX, STRIP),
                preferred_element_type=F32,
            )
            for dr in range(3)
        ],
        axis=2,
    ).astype(BF)
    binned = binned.reshape(pair * NB, TAPS * WIDE)
    grad_active = choose(
        dot(binned, merge_full[CIN:], ((1,), (1,))).reshape(pair, NB, -1), MID
    )
    mine = lax.dynamic_slice_in_dim(grad_active, half * WIDE, WIDE, 2)
    theirs = lax.dynamic_slice_in_dim(grad_active, (1 - half) * WIDE, WIDE, 2)
    grad_active = mine + swap(theirs.astype(BF))[::-1].astype(F32)
    gain_rows, bias_rows, outs = [], [], []
    for branch, (start, size, room) in enumerate(SPANS):
        grad_normed_b = grad_active[:, start : start + room] * silu_slope(normed[branch])
        gain_row = jnp.sum(grad_normed_b * centred[branch], axis=(0, 1))
        bias_row = jnp.sum(grad_normed_b, axis=(0, 1))
        gain_rows.append(gain_row)
        bias_rows.append(bias_row)
        outs.append(
            gains[branch]
            * inverse[branch]
            * (grad_normed_b - (bias_row + centred[branch] * gain_row) / entries[branch])
        )
    grad_out = widen(jnp.concatenate(outs, axis=1).astype(BF))
    grad_branch = dot(pooled.reshape(pair * NB, CIN), grad_out, ((0,), (0,))).astype(BF)
    grad_pooled = dot(grad_out, branch_full, ((1,), (1,))).reshape(pair, NB, CIN)
    grad_pooled = (grad_pooled / counts[:, :, None]).astype(BF)

    share_merge, share_branch, own_part, far_part = scatter_call(
        masked.T, spread_grad, wide_active.T, binned, grad_branch.reshape(16, 128, 4 * WIDE), merge_g
    )
    mine_pooled = jnp.concatenate([grad_pooled[0], swap(grad_pooled[1])], axis=0)
    mine_pools = jnp.concatenate([pools[0], pools[0]], axis=0)
    grad_features = dot(mine_pools, mine_pooled, ((0,), (0,)))
    grad_features = (grad_features + own_part + far_part.astype(F32))[None] * inside_float[:1, :, None]

    def placed(value, axis):
        shape = list(value.shape)
        shape[axis] = MID
        return lax.dynamic_update_slice_in_dim(jnp.zeros(shape, F32), value, half * WIDE, axis)

    total_class, total_gain, total_bias = lax.psum(
        (
            placed(grad_class, 0),
            placed(jnp.stack(gain_rows + [gain_merged]), 1),
            placed(jnp.stack(bias_rows + [bias_merged]), 1),
        ),
        ("bn", "fsdp"),
    )
    return (
        logits,
        grad_features,
        share_branch.reshape(128, 4 * MID).astype(F32),
        share_merge.reshape(256, TAPS * MID).astype(F32),
        total_class,
        total_gain,
        total_bias,
    )


def solution(mesh):
    placed = (
        P(("bn", "fsdp"), None, None),
        P(("bn", "fsdp"), None, None),
        P("fsdp", None),
        P("fsdp", None),
        P(),
        P(),
        P(),
        P(("bn", "fsdp"), None, None),
    )
    run = paired if dict(mesh.shape) == {"bn": 2, "fsdp": LINE * QUAD} else body
    return jax.shard_map(
        run,
        mesh=mesh,
        in_specs=placed,
        out_specs=(
            P(("bn", "fsdp"), None, None),
            P(("bn", "fsdp"), None, None),
            P("fsdp", None),
            P("fsdp", None),
            P(),
            P(),
            P(),
        ),
        check_vma=False,
    )
```

```python
import jax
import jax.numpy as jnp
from jax import lax
from jax.experimental import pallas as pl
from jax.experimental.pallas import tpu as pltpu
from jax.sharding import PartitionSpec as P

CIN = 2048
MID = 512
CLS = 19
IMG = 4
SIDE_R = 32
SIDE_C = 32
PIX = 1024
TAPS = 9
EPSILON = 1e-05
BIN_COUNTS = (1, 2, 3, 6)
SIZES = tuple(IMG * bins * bins for bins in BIN_COUNTS)
STARTS = (0, 4, 20, 56)
BINS = 200


def region_maps(region_boxes, bins):
    canvases = region_boxes.shape[0]
    top = region_boxes[:, :, 0][:, :, None]
    left = region_boxes[:, :, 1][:, :, None]
    height = region_boxes[:, :, 2][:, :, None]
    width = region_boxes[:, :, 3][:, :, None]
    pixel = jnp.arange(PIX, dtype=jnp.int32)
    rel_row = (pixel // SIDE_C)[None, None, :] - top
    rel_col = (pixel % SIDE_C)[None, None, :] - left
    index = jnp.arange(bins, dtype=jnp.int32)[None, None, :, None]
    row_low = index * height[..., None] // bins
    row_high = ((index + 1) * height[..., None] + bins - 1) // bins
    col_low = index * width[..., None] // bins
    col_high = ((index + 1) * width[..., None] + bins - 1) // bins
    row_in = (rel_row[:, :, None, :] >= row_low) & (rel_row[:, :, None, :] < row_high)
    col_in = (rel_col[:, :, None, :] >= col_low) & (rel_col[:, :, None, :] < col_high)
    pool = (row_in[:, :, :, None, :] & col_in[:, :, None, :, :]).reshape(
        canvases, IMG * bins * bins, PIX
    )
    inside_row = (rel_row >= 0) & (rel_row < height)
    inside_col = (rel_col >= 0) & (rel_col < width)
    near_row = rel_row * bins // height
    near_col = rel_col * bins // width
    up_row = inside_row[:, :, None, :] & (near_row[:, :, None, :] == index)
    up_col = inside_col[:, :, None, :] & (near_col[:, :, None, :] == index)
    upmap = (up_row[:, :, :, None, :] & up_col[:, :, None, :, :]).reshape(
        canvases, IMG * bins * bins, PIX
    )
    inside = jnp.any(inside_row & inside_col, axis=1)
    return (pool, upmap, inside)


def silu_slope(value):
    sigma = jax.nn.sigmoid(value)
    return sigma * (1.0 + value * (1.0 - sigma))


def swap(value):
    return lax.ppermute(value, "bn", [(0, 1), (1, 0)])


def both(value):
    return jnp.concatenate([value, swap(value)], axis=0)


def dot(a, b, dims=((1,), (0,))):
    return lax.dot_general(a, b, (dims, ((), ())), preferred_element_type=jnp.float32)


def rolled(value, shift):
    rows = value.shape[0]
    if shift == 0:
        return value
    pad = jnp.zeros((abs(shift),) + value.shape[1:], value.dtype)
    if shift > 0:
        return jnp.concatenate([value[shift:], pad], axis=0)
    return jnp.concatenate([pad, value[: rows + shift]], axis=0)


def own_half(value, half, width):
    rows = value.shape[0]
    cut = value.reshape(rows, -1, 2, width)
    return lax.dynamic_index_in_dim(cut, half, axis=2, keepdims=False).reshape(rows, -1)


def gather_weights(branch_half, merge_half):
    return (
        lax.all_gather(branch_half, "fsdp", axis=0, tiled=True),
        lax.all_gather(merge_half, "fsdp", axis=0, tiled=True),
    )


def scatter_grads(grad_branch, grad_merge):
    return (
        lax.psum_scatter(grad_branch, "fsdp", scatter_dimension=0, tiled=True),
        lax.psum_scatter(grad_merge, "fsdp", scatter_dimension=0, tiled=True),
    )


def body(features, region_boxes, branch_w, merge_w, class_w, norm_gain, norm_bias, grad_logits):
    half = lax.axis_index("bn")
    wide = MID // 2
    branch_full, merge_full = gather_weights(
        own_half(branch_w, half, wide), own_half(merge_w, half, wide)
    )
    gains = lax.dynamic_slice_in_dim(norm_gain, half * wide, wide, 1).astype(jnp.float32)
    biases = lax.dynamic_slice_in_dim(norm_bias, half * wide, wide, 1).astype(jnp.float32)
    class_half = lax.dynamic_slice_in_dim(class_w, half * wide, wide, 0)
    feats = both(features)
    boxes = both(region_boxes)
    cotangent = both(grad_logits)
    pair = feats.shape[0]
    rows = pair * PIX
    pools = []
    upmaps = []
    inside = None
    for bins in BIN_COUNTS:
        pool, upmap, inside = region_maps(boxes, bins)
        pools.append(pool)
        upmaps.append(upmap)
    counts = jnp.concatenate(
        [jnp.sum(pool.astype(jnp.float32), axis=2) for pool in pools], axis=1
    )
    pools = jnp.concatenate(pools, axis=1).astype(jnp.bfloat16)
    upmaps = jnp.concatenate(upmaps, axis=1).astype(jnp.bfloat16)
    inside_float = inside.astype(jnp.float32)
    weight_in = inside_float.reshape(rows, 1)
    masked = (feats * inside.astype(jnp.bfloat16)[:, :, None]).reshape(rows, CIN)
    pooled_sum = jnp.einsum("cnp,cpd->cnd", pools, feats, preferred_element_type=jnp.float32)
    pooled = (pooled_sum / counts[:, :, None]).astype(jnp.bfloat16)

    spans = [slice(s, s + n) for s, n in zip(STARTS, SIZES)]
    outs = []
    stats = []
    for branch, span in enumerate(spans):
        entries = pair * SIZES[branch]
        value = jnp.einsum(
            "cnd,do->cno",
            pooled[:, span],
            branch_full[:, branch * wide : (branch + 1) * wide],
            preferred_element_type=jnp.float32,
        )
        mean = jnp.sum(value, axis=(0, 1)) / entries
        spread = jnp.sum(value * value, axis=(0, 1)) / entries - mean * mean
        inverse = lax.rsqrt(spread + EPSILON)
        centred = (value - mean) * inverse
        normed = centred * gains[branch] + biases[branch]
        outs.append(jax.nn.silu(normed).astype(jnp.bfloat16))
        stats.append((inverse, centred, normed, entries))
    active = jnp.concatenate(outs, axis=1)
    other = swap(active)
    active_full = jnp.where(
        half == 0,
        jnp.concatenate([active, other[::-1]], axis=2),
        jnp.concatenate([other[::-1], active], axis=2),
    )
    lifted = jnp.concatenate(
        [
            jnp.einsum(
                "cno,ok->cnk",
                active_full[:, span],
                merge_full[CIN + branch * MID : CIN + (branch + 1) * MID],
                preferred_element_type=jnp.float32,
            ).astype(jnp.bfloat16)
            for branch, span in enumerate(spans)
        ],
        axis=1,
    )
    spans_up = jnp.swapaxes(upmaps, 1, 2).reshape(rows, BINS)
    strip = 3 * wide
    column = jnp.zeros((rows, strip), jnp.float32)
    for dr in range(3):
        shift = (dr - 1) * SIDE_C
        cut = slice(dr * strip, (dr + 1) * strip)
        column = column + dot(rolled(masked, shift), merge_full[:CIN, cut])
        raised = rolled(spans_up, shift).reshape(pair, PIX, BINS)
        column = column + jnp.einsum(
            "cpn,cnk->cpk", raised, lifted[:, :, cut], preferred_element_type=jnp.float32
        ).reshape(rows, strip)
    convolved = (
        rolled(column[:, :wide], -1)
        + column[:, wide : 2 * wide]
        + rolled(column[:, 2 * wide :], 1)
    )
    pixel_count = jnp.sum(inside_float)
    mean_merged = jnp.sum(convolved * weight_in, axis=0) / pixel_count
    spread_merged = (
        jnp.sum(convolved * convolved * weight_in, axis=0) / pixel_count
        - mean_merged * mean_merged
    )
    inverse_merged = lax.rsqrt(spread_merged + EPSILON)
    centred_merged = (convolved - mean_merged) * inverse_merged
    normed_merged = centred_merged * gains[4] + biases[4]
    hidden = jax.nn.silu(normed_merged).astype(jnp.bfloat16)
    logits_part = (dot(hidden, class_half) * weight_in).reshape(pair, PIX, CLS)
    logits = logits_part[:1] + swap(logits_part[1:])

    masked_grad = (cotangent * inside.astype(jnp.bfloat16)[:, :, None]).reshape(rows, CLS)
    grad_class = dot(hidden, masked_grad, ((0,), (0,)))
    grad_hidden = dot(masked_grad, class_half, ((1,), (1,)))
    grad_normed = grad_hidden * silu_slope(normed_merged)
    gain_merged = jnp.sum(grad_normed * centred_merged * weight_in, axis=0)
    bias_merged = jnp.sum(grad_normed * weight_in, axis=0)
    grad_conv = (
        weight_in
        * gains[4]
        * inverse_merged
        * (grad_normed - (bias_merged + centred_merged * gain_merged) / pixel_count)
    ).astype(jnp.bfloat16)
    spread_grad = jnp.concatenate(
        [
            rolled(grad_conv, -((tap // 3 - 1) * SIDE_C + (tap % 3 - 1)))
            for tap in range(TAPS)
        ],
        axis=1,
    )
    binned = jnp.einsum(
        "cnp,cpk->cnk",
        upmaps,
        spread_grad.reshape(pair, PIX, TAPS * wide),
        preferred_element_type=jnp.float32,
    ).astype(jnp.bfloat16)
    merge_rows = [dot(masked, spread_grad, ((0,), (0,))).astype(jnp.bfloat16)]
    actives = []
    for branch, span in enumerate(spans):
        merge_rows.append(
            jnp.einsum(
                "cno,cnk->ok",
                active_full[:, span],
                binned[:, span],
                preferred_element_type=jnp.float32,
            ).astype(jnp.bfloat16)
        )
        actives.append(
            jnp.einsum(
                "cnk,ok->cno",
                binned[:, span],
                merge_full[CIN + branch * MID : CIN + (branch + 1) * MID],
                preferred_element_type=jnp.float32,
            )
        )
    grad_merge = jnp.concatenate(merge_rows, axis=0)
    grad_active = jnp.concatenate(actives, axis=1)
    mine = lax.dynamic_slice_in_dim(grad_active, half * wide, wide, 2)
    theirs = lax.dynamic_slice_in_dim(grad_active, (1 - half) * wide, wide, 2)
    grad_active = mine + swap(theirs.astype(jnp.bfloat16))[::-1].astype(jnp.float32)
    gain_rows = []
    bias_rows = []
    branch_columns = []
    pooled_grads = []
    for branch, span in enumerate(spans):
        inverse, centred, normed, entries = stats[branch]
        grad_branch_normed = grad_active[:, span] * silu_slope(normed)
        gain_row = jnp.sum(grad_branch_normed * centred, axis=(0, 1))
        bias_row = jnp.sum(grad_branch_normed, axis=(0, 1))
        gain_rows.append(gain_row)
        bias_rows.append(bias_row)
        grad_out = (
            gains[branch]
            * inverse
            * (grad_branch_normed - (bias_row + centred * gain_row) / entries)
        ).astype(jnp.bfloat16)
        branch_columns.append(
            jnp.einsum(
                "cnd,cno->do", pooled[:, span], grad_out, preferred_element_type=jnp.float32
            ).astype(jnp.bfloat16)
        )
        pooled_grads.append(
            jnp.einsum(
                "cno,do->cnd",
                grad_out,
                branch_full[:, branch * wide : (branch + 1) * wide],
                preferred_element_type=jnp.float32,
            )
        )
    grad_branch = jnp.concatenate(branch_columns, axis=1)
    grad_pooled = (jnp.concatenate(pooled_grads, axis=1) / counts[:, :, None]).astype(jnp.bfloat16)
    grad_masked = dot(spread_grad, merge_full[:CIN], ((1,), (1,))).reshape(pair, PIX, CIN)
    grad_masked = grad_masked + jnp.einsum(
        "cnp,cnd->cpd", pools, grad_pooled, preferred_element_type=jnp.float32
    )
    away = swap(grad_masked[1:].astype(jnp.bfloat16))
    grad_features = (grad_masked[:1] + away.astype(jnp.float32)) * inside_float[:1, :, None]

    share_branch, share_merge = scatter_grads(grad_branch, grad_merge)
    share_branch = whole_rows(share_branch, half, wide)
    share_merge = whole_rows(share_merge, half, wide)

    def placed(value, axis):
        shape = list(value.shape)
        shape[axis] = MID
        return lax.dynamic_update_slice_in_dim(
            jnp.zeros(shape, jnp.float32), value, half * wide, axis
        )

    total_class, total_gain, total_bias = lax.psum(
        (
            placed(grad_class, 0),
            placed(jnp.stack(gain_rows + [gain_merged]), 1),
            placed(jnp.stack(bias_rows + [bias_merged]), 1),
        ),
        ("bn", "fsdp"),
    )
    return (logits, grad_features, share_branch, share_merge, total_class, total_gain, total_bias)


def whole_rows(share, half, wide):
    rows = share.shape[0]
    other = swap(share)
    mine = share.reshape(rows, -1, 1, wide)
    other = other.reshape(rows, -1, 1, wide)
    joined = jnp.where(
        half == 0,
        jnp.concatenate([mine, other], axis=2),
        jnp.concatenate([other, mine], axis=2),
    )
    return joined.reshape(rows, -1).astype(jnp.float32)


MESH = pl.DeviceIdType.MESH
LINE, QUAD, WIDE = 4, 4, 256
CUT = 7 * WIDE
BF = jnp.bfloat16
F32 = jnp.float32
ROWS = 2048
STRIP = 3 * WIDE
NB = 256
PAIRBINS = 2 * NB
LANES = 128
SMALL = 32
SPANS = ((0, 4, 16), (16, 16, 16), (32, 36, 48), (80, 144, 176))


def place():
    half = lax.axis_index("bn")
    f = lax.axis_index("fsdp")
    return half, f, f // QUAD, f % QUAD


def turn(z, step):
    if step == 0:
        return z
    if step == 1:
        return z + 1 - 2 * (z % 2)
    if step == 2:
        return 2 - z // 2
    return 3 - 3 * (z // 2)


def greet(half, f, z, q):
    barrier = pltpu.get_barrier_semaphore()
    xq, yq = q + 1 - 2 * (q % 2), q + 2 - 4 * (q // 2)

    def signal(device):
        pl.semaphore_signal(barrier, inc=1, device_id=device, device_id_type=MESH)

    for device in ((half, z * QUAD + xq), (half, z * QUAD + yq), (1 - half, f)):
        signal(device)

    @pl.when(z < LINE - 1)
    def _():
        signal((half, f + QUAD))

    @pl.when(z > 0)
    def _():
        signal((half, f - QUAD))

    pl.semaphore_wait(barrier, 5 - (z // (LINE - 1)) - ((LINE - 1 - z) // (LINE - 1)))


def span_mask(shape, branch):
    row = lax.broadcasted_iota(jnp.int32, shape, 0)
    row = jnp.where(row >= NB, row - NB, row)
    if isinstance(branch, int):
        start, _, room = SPANS[branch]
        return (row >= start) & (row < start + room)
    kind = (row >= 16).astype(jnp.int32) + (row >= 32).astype(jnp.int32) + (row >= 80).astype(jnp.int32)
    return kind == branch


def mm(a, b, dims=((1,), (0,))):
    return lax.dot_general(a, b, (dims, ((), ())), preferred_element_type=F32)


def block(n, size):
    return pl.ds(pl.multiple_of(n * size, size), size)


def forward_kernel(
    merge_ref, branch_ref, feats_ref, t1_ref, t2_ref, g_ref, class_ref, gain_ref, bias_ref,
    merge_out, branch_out, x_out, d3_out, ud_out, act_out, pooled_out, xhat_out, inv_out, pt_out, count_out,
    logit_own, logit_far, small_out,
    branch_own, merge_own, x, acc, wbuf, bfull, aw, awb, pm, um, ut, pt, pooled, act, act_own, xhat, inv, cv, dy, d3, ud,
    w_in, cnt, t1, t2, g, stage, small,
    local_sem, z_send, z_recv, q_send, q_recv, zb_send, zb_recv, core_send, core_recv, w_sem, out_sem,
):
    half, f, z, q = place()
    xq, yq, dq = q + 1 - 2 * (q % 2), q + 2 - 4 * (q // 2), 3 - q
    L = [turn(z, i) for i in range(LINE)]

    def cut_copy(src, dst, t, n):
        return pltpu.make_async_copy(
            src.at[:, pl.ds(pl.multiple_of(t * MID + half * WIDE, WIDE), WIDE)],
            dst.at[:, pl.ds(t * WIDE, WIDE)],
            local_sem.at[n],
        )

    own_copies = [cut_copy(branch_ref, branch_own, t, t) for t in range(4)] + [
        cut_copy(merge_ref, merge_own, t, 4 + t) for t in range(TAPS)
    ]
    for c in own_copies:
        c.start()
    core = (1 - half, f)
    own_loads = [
        pltpu.make_async_copy(t1_ref, t1.at[0], local_sem.at[13]),
        pltpu.make_async_copy(t2_ref, t2.at[0], local_sem.at[14]),
        pltpu.make_async_copy(g_ref, g.at[0], local_sem.at[15]),
        pltpu.make_async_copy(feats_ref, x.at[pl.ds(32, PIX)], local_sem.at[16]),
    ]
    for c in own_loads:
        c.start()

    def to_core(src, dst, n):
        return pltpu.make_async_remote_copy(
            src_ref=src, dst_ref=dst, send_sem=core_send.at[n], recv_sem=core_recv.at[n], device_id=core, device_id_type=MESH
        )

    crossing = [
        to_core(t1_ref, t1.at[1], 0),
        to_core(t2_ref, t2.at[1], 1),
        to_core(g_ref, g.at[1], 2),
        to_core(feats_ref, x.at[pl.ds(32 + PIX, PIX)], 3),
    ]
    greet(half, f, z, q)
    for c in own_copies:
        c.wait()
    keep = [
        pltpu.make_async_copy(branch_own, branch_out.at[f], local_sem.at[0]),
        pltpu.make_async_copy(merge_own, merge_out.at[f], local_sem.at[1]),
    ]

    def columns(kind):
        return pl.ds(0, CUT) if kind == 1 else pl.ds(CUT, 2 * WIDE)

    def piece(kind, owner, part=None):
        rows = 128 if kind == 0 else 256
        at = slice(None) if part is None else pl.ds(part * (rows // 2), rows // 2)
        return branch_out.at[owner, at] if kind == 0 else merge_out.at[owner, at, columns(kind)]

    def own_piece(kind):
        return branch_own if kind == 0 else merge_own.at[:, columns(kind)]

    def remote(ref, s, r, dev, src=None):
        return pltpu.make_async_remote_copy(
            src_ref=ref if src is None else src, dst_ref=ref, send_sem=s, recv_sem=r, device_id=dev, device_id_type=MESH
        )

    def beside(d):
        return (half, f + QUAD if d == 0 else f - QUAD)

    def z_copy(kind, i, d):
        src = own_piece(kind) if i == 0 else None
        return remote(piece(kind, L[i] * QUAD + q), z_send.at[kind, d, L[i]], z_recv.at[kind, L[i]], beside(d), src)

    def zb_copy(i, c, d):
        return remote(piece(2, L[i] * QUAD + c), zb_send.at[d, L[i], c], zb_recv.at[L[i], c], beside(d))

    def z_both(i, fn):
        @pl.when((L[i] <= z) & (z < LINE - 1))
        def _():
            fn(0)

        @pl.when((L[i] >= z) & (z > 0))
        def _():
            fn(1)

    def q_copy(kind, i, axis, what):
        dev = (half, z * QUAD + (xq if axis == 0 else yq))
        if what == 0:
            ref = piece(kind, L[i] * QUAD + q)
        else:
            ref = piece(kind, L[i] * QUAD + (yq if axis == 0 else xq), 1 - axis)
        src = own_piece(kind) if i == 0 and what == 0 else None
        return remote(ref, q_send.at[kind, L[i], axis, what], q_recv.at[kind, L[i], axis, what], dev, src)

    def q_arrive(kind, i, axis, what):
        owner = L[i] * QUAD + ((xq if axis == 0 else yq) if what == 0 else dq)
        ref = piece(kind, owner, None if what == 0 else 1 - axis)
        remote(ref, q_send.at[kind, L[i], axis, what], q_recv.at[kind, L[i], axis, what], core).wait_recv()

    def spread(kind, i):
        for axis in (0, 1):
            q_copy(kind, i, axis, 0).start()

    def pass_on(kind, i):
        for axis in (0, 1):
            q_arrive(kind, i, axis, 0)
            q_copy(kind, i, 1 - axis, 1).start()

    def corner(kind, i):
        for axis in (0, 1):
            q_arrive(kind, i, axis, 1)

    def z_step(kind, i):
        if i:
            remote(piece(kind, L[i] * QUAD + q), z_send.at[kind, 0, L[i]], z_recv.at[kind, L[i]], core).wait_recv()
        z_both(i, lambda d: z_copy(kind, i, d).start())

    def zb_step(i):
        for c in range(QUAD):
            if i:
                remote(piece(2, L[i] * QUAD + c), zb_send.at[0, L[i], c], zb_recv.at[L[i], c], core).wait_recv()
            z_both(i, lambda d: zb_copy(i, c, d).start())

    def maps(c):
        def across(n, _):
            at = block(n, 32)
            p = lax.broadcasted_iota(jnp.int32, (32, PIX), 1)
            row, col = lax.shift_right_logical(p, 5), jnp.bitwise_and(p, 31)
            t = t1[c, at, :]
            cell = lambda k: t[:, k : k + 1]
            for ref, k in ((pm, 0), (um, 2)):
                hit = (row >= cell(k)) & (row < cell(k + 1)) & (col >= cell(k + 4)) & (col < cell(k + 5))
                value = jnp.where(hit, 1.0, 0.0)
                ref[c, at, :] = value.astype(BF)
                if k == 0:
                    total = jnp.maximum(jnp.sum(value, axis=1, keepdims=True), 1.0)
                    cnt[pl.ds(pl.multiple_of(c * NB + n * 32, 32), 32), :] = jnp.broadcast_to(total, (32, LANES))
            return 0

        lax.fori_loop(0, NB // 32, across, 0)

        def down(n, _):
            p = lax.broadcasted_iota(jnp.int32, (LANES, NB), 0) + n * LANES
            row, col = lax.shift_right_logical(p, 5), jnp.bitwise_and(p, 31)
            cell = lambda k: t2[c, k : k + 1, :]
            for k in (0, 2):
                hit = (row >= cell(k)) & (row < cell(k + 1)) & (col >= cell(k + 4)) & (col < cell(k + 5))
                value = jnp.where(hit, 1.0, 0.0)
                if k == 0:
                    pt[c, block(n, LANES), :] = value.astype(BF)
                else:
                    ut[c, pl.ds(pl.multiple_of(32 + n * LANES, 32), LANES), :] = value.astype(BF)
                    first = lax.broadcasted_iota(jnp.int32, (LANES, NB), 1) < IMG
                    inside = jnp.sum(jnp.where(first, value, 0.0), axis=1, keepdims=True)
                    w_in[pl.ds(pl.multiple_of(c * PIX + n * LANES, LANES), LANES), :] = inside
            return 0

        lax.fori_loop(0, PIX // LANES, down, 0)
        ut[c, 0:32, :] = jnp.zeros((32, NB), BF)
        ut[c, 32 + PIX : 64 + PIX, :] = jnp.zeros((32, NB), BF)

    def mask_pool(c):
        def mask(n, _):
            at = pl.ds(pl.multiple_of(32 + c * PIX + n * 64, 32), 64)
            w = w_in[pl.ds(pl.multiple_of(c * PIX + n * 64, 64), 64), :]
            x[at, :] = (x[at, :].astype(F32) * w).astype(BF)
            return 0

        lax.fori_loop(0, PIX // 64, mask, 0)

        def pool(n, _):
            cols = block(n, 512)
            total = mm(pm[c], x[pl.ds(32 + c * PIX, PIX), cols])
            pooled[pl.ds(c * NB, NB), cols] = (total / cnt[pl.ds(c * NB, NB), 0:1]).astype(BF)
            return 0

        lax.fori_loop(0, CIN // 512, pool, 0)

    def branches():
        load = pltpu.make_async_copy(branch_out, bfull, local_sem.at[2])
        load.start()
        load.wait()
        for b, (_, size, _) in enumerate(SPANS):
            weight = bfull[:, :, b * WIDE : (b + 1) * WIDE].reshape(CIN, WIDE)
            here = span_mask((PAIRBINS, WIDE), b)
            value = jnp.where(here, mm(pooled[...], weight), 0.0)
            entries = 2.0 * size
            mean = jnp.sum(value, axis=0, keepdims=True) / entries
            spread_ = jnp.sum(value * value, axis=0, keepdims=True) / entries - mean * mean
            inverse = lax.rsqrt(spread_ + EPSILON)
            centred = (value - mean) * inverse
            gain = gain_ref[b : b + 1, pl.ds(pl.multiple_of(half * WIDE, WIDE), WIDE)].astype(F32)
            bias = bias_ref[b : b + 1, pl.ds(pl.multiple_of(half * WIDE, WIDE), WIDE)].astype(F32)
            normed = centred * gain + bias
            active = normed * jax.nn.sigmoid(normed)
            inv[b : b + 1, :] = inverse
            if b == 0:
                xhat[...] = jnp.where(here, centred, 0.0)
                act_own[...] = jnp.where(here, active, 0.0).astype(BF)
            else:
                xhat[...] = jnp.where(here, centred, xhat[...])
                act_own[...] = jnp.where(here, active, act_own[...].astype(F32)).astype(BF)
        inv[4:8, :] = jnp.zeros((4, WIDE), F32)
        cols = pl.ds(pl.multiple_of(half * WIDE, WIDE), WIDE)
        sends = [
            to_core(act_own.at[pl.ds(c * NB, NB)], act.at[pl.ds((1 - c) * NB, NB), cols], 4 + c) for c in (0, 1)
        ]
        for s in sends:
            s.start()
        act[:, cols] = act_own[...]
        return sends

    def act_arrive():
        cols = pl.ds(pl.multiple_of((1 - half) * WIDE, WIDE), WIDE)
        for c in (0, 1):
            to_core(act_own.at[pl.ds(c * NB, NB)], act.at[pl.ds((1 - c) * NB, NB), cols], 4 + c).wait_recv()

    def w_load(kind, i, k, c):
        cols = columns(kind)
        return pltpu.make_async_copy(merge_out.at[L[i] * QUAD + c, :, cols], wbuf.at[k, :, cols], w_sem.at[k])

    def column_of(k):
        return (q % 2 + k % 2) % 2 + 2 * ((q // 2 + k // 2) % 2)

    def contract(kind, i, ks):
        for k in ks:
            w_load(kind, i, k, column_of(k)).start()

        def feature(k, _):
            c = column_of(k)
            w_load(kind, i, k, c).wait()
            lanes = block(L[i] * QUAD + c, WIDE)
            for canvas in (0, 1):
                r = canvas * PIX
                rows = pl.ds(r, PIX)
                if kind == 1:
                    acc[rows, :] = acc[rows, :] + (
                        mm(x[pl.ds(r, PIX), lanes], wbuf[k, :, 0:STRIP])
                        + mm(x[pl.ds(r + 32, PIX), lanes], wbuf[k, :, STRIP : 2 * STRIP])
                    )
                    acc[rows, 0:WIDE] = acc[rows, 0:WIDE] + mm(x[pl.ds(r + 64, PIX), lanes], wbuf[k, :, 2 * STRIP : CUT])
                else:
                    acc[rows, WIDE:STRIP] = acc[rows, WIDE:STRIP] + mm(x[pl.ds(r + 64, PIX), lanes], wbuf[k, :, CUT:])
            return 0

        def raised(k, _):
            c = column_of(k)
            w_load(kind, i, k, c).wait()
            here = span_mask((PAIRBINS, WIDE), 2 * (L[i] - 2) + c // 2)
            lhs = jnp.where(here, act[:, block(c % 2, WIDE)].astype(F32), 0.0).astype(BF)

            def strip(n, _):
                cols = block(n, WIDE)
                aw[:, cols] = aw[:, cols] + mm(lhs, wbuf[k, :, cols])
                return 0

            if kind == 1:
                lax.fori_loop(0, 7, strip, 0)
            else:
                lax.fori_loop(7, TAPS, strip, 0)
            return 0

        @pl.when(L[i] < 2)
        def _():
            lax.fori_loop(ks[0], ks[-1] + 1, feature, 0)

        @pl.when(L[i] >= 2)
        def _():
            lax.fori_loop(ks[0], ks[-1] + 1, raised, 0)

    crossing[0].start()
    crossing[1].start()
    z_step(0, 0)
    spread(0, 0)
    spread(2, 0)
    for c in crossing[2:]:
        c.start()
    for c in keep:
        c.start()
    for c in own_loads[:2]:
        c.wait()
    z_step(0, 1)
    spread(0, 1)
    spread(1, 0)
    z_step(1, 0)
    maps(0)
    z_step(0, 2)
    spread(0, 2)
    z_step(0, 3)
    spread(0, 3)
    pass_on(0, 0)
    pass_on(2, 0)
    for c in own_loads[2:]:
        c.wait()
    mask_pool(0)
    for c in crossing[:2]:
        c.wait_recv()
    maps(1)
    pass_on(0, 1)
    z_step(1, 1)
    spread(1, 1)
    crossing[2].wait_recv()
    crossing[3].wait_recv()
    mask_pool(1)
    x_save = pltpu.make_async_copy(x.at[pl.ds(32, ROWS)], x_out, out_sem.at[0])
    x_save.start()
    pass_on(1, 0)
    pass_on(0, 2)
    pass_on(0, 3)
    corner(2, 0)
    for c in keep:
        c.wait()
    zb_step(0)
    x[0:32, :] = jnp.zeros((32, CIN), BF)
    x[32 + ROWS : 64 + ROWS, :] = jnp.zeros((32, CIN), BF)

    def clear(n, _):
        acc[block(n, LANES), :] = jnp.zeros((LANES, STRIP), F32)
        return 0

    lax.fori_loop(0, ROWS // LANES, clear, 0)

    def clear_aw(n, _):
        aw[block(n, 32), :] = jnp.zeros((32, TAPS * WIDE), F32)
        return 0

    lax.fori_loop(0, PAIRBINS // 32, clear_aw, 0)
    z_step(1, 2)
    spread(1, 2)
    for i in range(LINE):
        corner(0, i)
    act_sends = branches()
    z_step(1, 3)
    spread(1, 3)
    act_arrive()
    corner(1, 0)
    pass_on(1, 1)
    contract(1, 0, (0, 1, 2, 3))
    zb_step(1)
    contract(2, 0, (0, 1, 2, 3))
    pass_on(1, 2)
    corner(1, 1)
    contract(1, 1, (0, 1, 2, 3))
    zb_step(2)
    contract(2, 1, (0, 1, 2, 3))
    pass_on(1, 3)
    corner(1, 2)
    contract(1, 2, (0, 1, 2, 3))
    zb_step(3)
    contract(2, 2, (0, 1, 2, 3))
    contract(2, 3, (0, 1, 2, 3))
    contract(1, 3, (0, 1, 2))
    corner(1, 3)
    contract(1, 3, (3,))

    def lower(n, _):
        at = block(n, 32)
        awb[at, :] = aw[at, :].astype(BF)
        return 0

    lax.fori_loop(0, PAIRBINS // 32, lower, 0)
    ones = lambda: jnp.zeros((1, WIDE), F32)
    s1, s2, n2 = ones(), ones(), jnp.zeros((1, 1), F32)
    for c in (0, 1):
        rows = pl.ds(c * PIX, PIX)
        for dr in range(3):
            acc[rows, :] = acc[rows, :] + mm(
                ut[c, 32 * dr : 32 * dr + PIX, :], awb[c * NB : (c + 1) * NB, dr * STRIP : (dr + 1) * STRIP]
            )
        value = (
            pltpu.roll(acc[rows, 0:WIDE], 1, 0)
            + acc[rows, WIDE : 2 * WIDE]
            + pltpu.roll(acc[rows, 2 * WIDE : STRIP], PIX - 1, 0)
        )
        cv[rows, :] = value
        w = w_in[rows, :]
        kept = value * w
        s1 = s1 + jnp.sum(kept, axis=0, keepdims=True)
        s2 = s2 + jnp.sum(kept * value, axis=0, keepdims=True)
        n2 = n2 + jnp.sum(w, axis=0, keepdims=True)
    mean = s1 / n2
    inverse = lax.rsqrt(s2 / n2 - mean * mean + EPSILON)
    cols = pl.ds(pl.multiple_of(half * WIDE, WIDE), WIDE)
    gain = gain_ref[4:5, cols].astype(F32)
    bias = bias_ref[4:5, cols].astype(F32)
    weight = class_ref[cols, :]

    def slopes(n, carry):
        sum_b, sum_g, sum_c = carry
        at = block(n, 256)
        w = w_in[at, :]
        centred = (cv[at, :] - mean) * inverse
        normed = centred * gain + bias
        sigma = jax.nn.sigmoid(normed)
        hidden = (normed * sigma).astype(BF)
        stage[at, :] = mm(hidden, weight) * w
        grad = (g[n // 4, block(n % 4, 256), :].astype(F32) * w).astype(BF)
        sum_c = sum_c + mm(grad, hidden, ((0,), (0,)))
        slope = mm(grad, weight, ((1,), (1,))) * (sigma * (1.0 + normed * (1.0 - sigma)))
        dy[at, :] = slope
        cv[at, :] = centred
        return (
            sum_b + jnp.sum(slope, axis=0, keepdims=True),
            sum_g + jnp.sum(slope * centred, axis=0, keepdims=True),
            sum_c,
        )

    sum_b, sum_g, sum_c = lax.fori_loop(0, ROWS // 256, slopes, (ones(), ones(), jnp.zeros((LANES, WIDE), F32)))
    logit_sends = [
        pltpu.make_async_copy(stage.at[pl.ds(0, PIX)], logit_own, out_sem.at[1]),
        to_core(stage.at[pl.ds(PIX, PIX)], logit_far, 6),
    ]
    for c in logit_sends:
        c.start()
    small[0:24, :] = sum_c[0:24, :]
    small[24:25, :] = sum_g
    small[25:26, :] = sum_b
    small[26:SMALL, :] = jnp.zeros((SMALL - 26, WIDE), F32)
    d3[0:32, :] = jnp.zeros((32, STRIP), BF)
    d3[32 + ROWS : 64 + ROWS, :] = jnp.zeros((32, STRIP), BF)
    for c in (0, 1):
        rows = pl.ds(c * PIX, PIX)
        value = (w_in[rows, :] * (gain * inverse)) * (dy[rows, :] - (sum_b + cv[rows, :] * sum_g) / n2)
        to = pl.ds(32 + c * PIX, PIX)
        d3[to, 0:WIDE] = pltpu.roll(value, PIX - 1, 0).astype(BF)
        d3[to, WIDE : 2 * WIDE] = value.astype(BF)
        d3[to, 2 * WIDE : STRIP] = pltpu.roll(value, 1, 0).astype(BF)
    for c in (0, 1):
        for dr in range(3):
            ud[c * NB : (c + 1) * NB, dr * STRIP : (dr + 1) * STRIP] = mm(
                um[c], d3[pl.ds(32 * (2 - dr) + c * PIX, PIX), :]
            ).astype(BF)
    saves = [
        pltpu.make_async_copy(a, b, out_sem.at[2 + n])
        for n, (a, b) in enumerate(
            (
                (d3, d3_out), (ud, ud_out), (act, act_out), (pooled, pooled_out), (xhat, xhat_out),
                (inv, inv_out), (pt, pt_out), (cnt, count_out), (small, small_out),
            )
        )
    ]
    for c in saves:
        c.start()

    for i in range(LINE):
        for kind in (0, 1):
            z_both(i, lambda d: z_copy(kind, i, d).wait_send())
        for c in range(QUAD):
            z_both(i, lambda d: zb_copy(i, c, d).wait_send())
        for kind in (0, 1) + ((2,) if i == 0 else ()):
            for axis in (0, 1):
                for what in (0, 1):
                    q_copy(kind, i, axis, what).wait_send()
    for c in crossing:
        c.wait_send()
    for c in act_sends:
        c.wait_send()
    logit_sends[0].wait()
    logit_sends[1].wait()
    x_save.wait()
    for c in saves:
        c.wait()


def forward_call(merge_w, branch_w, feats, t1, t2, g, class_w, gains, biases):
    D = pltpu.SemaphoreType.DMA
    V = lambda *s: pltpu.VMEM(s, BF)
    W = lambda *s: pltpu.VMEM(s, F32)
    S = jax.ShapeDtypeStruct
    hbm = pl.BlockSpec(memory_space=pl.ANY)
    vmem = pl.BlockSpec(memory_space=pltpu.VMEM)
    outs = (
        S((16, 256, TAPS * WIDE), BF), S((16, 128, 4 * WIDE), BF), S((ROWS, CIN), BF), S((ROWS + 64, STRIP), BF),
        S((PAIRBINS, TAPS * WIDE), BF), S((PAIRBINS, MID), BF), S((PAIRBINS, CIN), BF), S((PAIRBINS, WIDE), F32),
        S((8, WIDE), F32), S((2, PIX, NB), BF), S((PAIRBINS, LANES), F32), S((PIX, LANES), F32), S((PIX, LANES), F32),
        S((SMALL, WIDE), F32),
    )
    return pl.pallas_call(
        forward_kernel,
        out_shape=outs,
        in_specs=[hbm] * 6 + [vmem] * 3,
        out_specs=(hbm,) * len(outs),
        scratch_shapes=[
            V(128, 4 * WIDE), V(256, TAPS * WIDE), V(ROWS + 64, CIN), W(ROWS, STRIP), V(QUAD, 256, TAPS * WIDE),
            V(16, 128, 4 * WIDE), W(PAIRBINS, TAPS * WIDE), V(PAIRBINS, TAPS * WIDE), V(2, NB, PIX), V(2, NB, PIX),
            V(2, PIX + 64, NB), V(2, PIX, NB), V(PAIRBINS, CIN), V(PAIRBINS, MID), V(PAIRBINS, WIDE),
            W(PAIRBINS, WIDE), W(8, WIDE), W(ROWS, WIDE), W(ROWS, WIDE), V(ROWS + 64, STRIP), V(PAIRBINS, TAPS * WIDE),
            W(ROWS, 1), W(PAIRBINS, LANES), pltpu.VMEM((2, NB, 8), jnp.int32), pltpu.VMEM((2, 8, NB), jnp.int32),
            V(2, PIX, LANES), W(ROWS, LANES), W(SMALL, WIDE),
            D((17,)), D((2, 2, 4)), D((2, 4)), D((3, 4, 2, 2)), D((3, 4, 2, 2)), D((2, 4, 4)), D((4, 4)),
            D((7,)), D((7,)), D((4,)), D((11,)),
        ],
        compiler_params=pltpu.CompilerParams(collective_id=0, has_side_effects=True, vmem_limit_bytes=63 * 1024 * 1024),
        name="forward",
    )(merge_w, branch_w, feats, t1, t2, g, class_w, gains, biases)


def scatter_kernel(x_hbm, d3_hbm, act_hbm, ud_hbm, br_hbm, w_hbm, merge_out, branch_out, own_out, far_out,
                   xt, act, d3, ud, g0, g1, b_all, fx0, fy0, fx1, fy1, fx2, fy2, zs0, zs1, zs2, wbuf, own_stage, far_stage,
                   local_sem, q_send, q_recv, z_send, z_recv, zb_send, zb_recv, end_send, end_recv, w_sem, own_sem, far_send, far_recv, br_sem, end_local):
    half, f, z, q = place()
    xq = q + 1 - 2 * (q % 2); yq = q + 2 - 4 * (q // 2); dq = 3 - q
    L = [turn(z, i) for i in range(LINE)]
    loads = [pltpu.make_async_copy(a, b, local_sem.at[n]) for n, (a, b) in enumerate(((d3_hbm, d3), (ud_hbm, ud), (act_hbm, act)))]
    for c in loads: c.start()
    def load_w(n): return pltpu.make_async_copy(w_hbm.at[n], wbuf.at[n % 2], w_sem.at[n % 2])
    load_w(0).start()
    from_x = (fx0, fx1, fx2); from_y = (fy0, fy1, fy2); zslot = (zs0, zs1, zs2)
    HALF = (64, 128, 128)
    def fetch_rows(i):
        return pltpu.make_async_copy(x_hbm.at[:, pl.ds(pl.multiple_of(L[i] * 1024, 1024), 1024)], xt, local_sem.at[3])
    def rows_start(i):
        @pl.when(L[i] < 2)
        def _(): fetch_rows(i).start()
    rows_start(3)
    greet(half, f, z, q)
    for c in loads: c.wait()

    def produce(i, after=None):
        level = L[i]
        def loops(dot):
            def a_part(t, _):
                g1[i % 2, :, :, pl.ds(pl.multiple_of(t * WIDE, WIDE), WIDE)] = dot(t).astype(BF).reshape(QUAD, 256, WIDE)
                return 0
            def b_part(t, _):
                b_all[pl.ds(level * QUAD, QUAD), :, pl.ds(pl.multiple_of((t - 7) * WIDE, WIDE), WIDE)] = dot(t).astype(BF).reshape(QUAD, 256, WIDE)
                return 0
            lax.fori_loop(7, TAPS, b_part, 0)
            lax.fori_loop(0, 7, a_part, 0)
        @pl.when(level < 2)
        def _():
            fetch_rows(i).wait()
            loops(lambda t: mm(xt[...], d3[pl.ds(pl.multiple_of(32 * (2 - t // 3), 32), ROWS), pl.ds(pl.multiple_of((t % 3) * WIDE, WIDE), WIDE)], ((0,), (0,))))
        @pl.when(level >= 2)
        def _():
            for c in range(QUAD):
                here = span_mask((PAIRBINS, WIDE), 2 * (level - 2) + c // 2)
                rows = act[:, (c % 2) * WIDE:(c % 2 + 1) * WIDE].astype(F32)
                xt[0:PAIRBINS, c * WIDE:(c + 1) * WIDE] = jnp.where(here, rows, 0.0).astype(BF)
            loops(lambda t: mm(xt[0:PAIRBINS, :], ud[:, pl.ds(pl.multiple_of(t * WIDE, WIDE), WIDE)], ((0,), (0,))))
        if i: rows_start(i - 1)

    def br_load(i): return pltpu.make_async_copy(br_hbm.at[pl.ds(L[i] * QUAD, QUAD)], g0.at[i % 2], br_sem.at[i % 2])

    def own(kind, i, c):
        if kind == 0: return g0.at[i % 2, c]
        if kind == 1: return g1.at[i % 2, c]
        return b_all.at[L[i] * QUAD + c]
    def part(ref, kind, h): return ref.at[pl.ds(h * HALF[kind], HALF[kind])]
    def slot(kind, i, axis, what):
        ref = (from_x, from_y)[axis][kind]
        return ref.at[L[i], what] if kind < 2 else ref.at[0, what]
    def q_copy(kind, i, axis, what):
        to = xq if axis == 0 else yq
        if what == 0: src = part(own(kind, i, dq), kind, 1 - axis)
        elif what == 1: src = part(own(kind, i, to), kind, axis)
        else: src = part(own(kind, i, to), kind, 1 - axis)
        return pltpu.make_async_remote_copy(src_ref=src, dst_ref=slot(kind, i, axis, what), send_sem=q_send.at[kind, L[i], axis, what], recv_sem=q_recv.at[kind, L[i], axis, what], device_id=(half, z * QUAD + to), device_id_type=MESH)
    def add_into(dst, *others):
        rows = dst.shape[0]
        def block(n, _):
            at_ = pl.ds(pl.multiple_of(n * 16, 16), 16)
            total = dst[at_, :].astype(F32)
            for o in others: total = total + o[at_, :].astype(F32)
            dst[at_, :] = total.astype(BF)
            return 0
        lax.fori_loop(0, rows // 16, block, 0)
    def raw(kind, i):
        for what in (0, 2):
            for axis in (0, 1): q_copy(kind, i, axis, what).start()
    def fold(kind, i):
        for axis in (1, 0):
            q_copy(kind, i, axis, 0).wait_recv()
            to = xq if axis == 1 else yq
            add_into(part(own(kind, i, to), kind, 1 - axis), slot(kind, i, axis, 0))
            q_copy(kind, i, 1 - axis, 1).start()
    def gathered(kind, i):
        for axis in (0, 1):
            for what in (1, 2): q_copy(kind, i, axis, what).wait_recv()
        mine = own(kind, i, q)
        add_into(slot(kind, i, 0, 1), part(mine, kind, 0), slot(kind, i, 1, 2))
        add_into(slot(kind, i, 0, 2), part(mine, kind, 1), slot(kind, i, 1, 1))
    def total(kind, i): return from_x[kind].at[L[i] if kind < 2 else 0, pl.ds(1, 2)]
    def z_src(kind, i, c): return total(kind, i) if kind < 2 else own(2, i, c)
    def z_dst(kind, n, c): return zslot[kind].at[n] if kind < 2 else zs2.at[n, c]
    def z_sems(kind, level, n, c):
        if kind < 2: return z_send.at[kind, level], z_recv.at[kind, n]
        return zb_send.at[level, c], zb_recv.at[n, c]
    def z_copy(kind, i, c, up):
        level = L[i]
        n = level if up else level + (LINE - level) * (1 - jnp.minimum(z - 1 - level, 1))
        s, r = z_sems(kind, level, n, c)
        return pltpu.make_async_remote_copy(src_ref=z_src(kind, i, c), dst_ref=z_dst(kind, n, c), send_sem=s, recv_sem=r, device_id=(half, f + QUAD if up else f - QUAD), device_id_type=MESH)
    def z_take(kind, i, n, c):
        s, r = z_sems(kind, L[i], n, c)
        pltpu.make_async_remote_copy(src_ref=z_src(kind, i, c), dst_ref=z_dst(kind, n, c), send_sem=s, recv_sem=r, device_id=(half, f), device_id_type=MESH).wait_recv()
        if kind < 2:
            for h in (0, 1): add_into(total(kind, i).at[h], z_dst(kind, n, c).at[h])
        else: add_into(own(2, i, c), z_dst(kind, n, c))
    def early(kind, i, c=None):
        @pl.when((L[i] > z) & (z == 0))
        def _(): z_copy(kind, i, c, True).start()
        @pl.when((L[i] < z) & (z == LINE - 1))
        def _(): z_copy(kind, i, c, False).start()
    def late(kind, i, c=None):
        @pl.when((L[i] > z) & (z > 0))
        def _():
            z_take(kind, i, L[i], c)
            z_copy(kind, i, c, True).start()
        @pl.when((L[i] < z) & (z < LINE - 1))
        def _():
            z_take(kind, i, L[i], c)
            z_copy(kind, i, c, False).start()
    def home(kind, c=None):
        @pl.when(z > 0)
        def _(): z_take(kind, 0, z, c)
        @pl.when(z < LINE - 1)
        def _(): z_take(kind, 0, LINE, c)
    def line_sent(kind, i, c=None):
        @pl.when(L[i] > z)
        def _(): z_copy(kind, i, c, True).wait_send()
        @pl.when(L[i] < z)
        def _(): z_copy(kind, i, c, False).wait_send()
    def quad_sent(kind, i):
        for axis in (0, 1):
            for what in (0, 1, 2): q_copy(kind, i, axis, what).wait_send()
    def early_b(i):
        for c in range(QUAD): early(2, i, c)
    def late_b(i):
        for c in range(QUAD): late(2, i, c)

    def own_copy(n): return pltpu.make_async_copy(own_stage.at[n % 2], own_out.at[:, pl.ds(pl.multiple_of(n * WIDE, WIDE), WIDE)], own_sem.at[n % 2])
    def far_copy(n): return pltpu.make_async_remote_copy(src_ref=far_stage.at[n % 2], dst_ref=far_out.at[:, pl.ds(pl.multiple_of(n * WIDE, WIDE), WIDE)], send_sem=far_send.at[n % 2], recv_sem=far_recv.at[n], device_id=(1 - half, f), device_id_type=MESH)
    def jobs(first, last):
        def job(n, _):
            load_w(n).wait()
            @pl.when(n < 7)
            def _(): load_w(n + 1).start()
            @pl.when(n >= 2)
            def _():
                own_copy(n - 2).wait(); far_copy(n - 2).wait_send()
            for canvas in (0, 1):
                value = None
                for dr in range(3):
                    p = lax.dot_general(d3[pl.ds(32 * (2 - dr) + canvas * PIX, PIX), :], wbuf[n % 2, :, dr * STRIP:(dr + 1) * STRIP], (((1,), (1,)), ((), ())), preferred_element_type=F32)
                    value = p if value is None else value + p
                if canvas == 0: own_stage[n % 2] = value
                else: far_stage[n % 2] = value.astype(BF)
            own_copy(n).start(); far_copy(n).start()
            return 0
        lax.fori_loop(first, last, job, 0)

    br_load(3).start(); br_load(2).start()
    produce(3); raw(1, 3); early_b(3)
    produce(2); early_b(2)
    fold(1, 3); raw(1, 2)
    br_load(3).wait(); raw(0, 3)
    jobs(0, 3)
    gathered(1, 3); early(1, 3); late_b(3)
    quad_sent(1, 3); produce(1); early_b(1)
    fold(1, 2); raw(1, 1); fold(0, 3)
    br_load(2).wait(); raw(0, 2)
    late(1, 3); late_b(2)
    gathered(0, 3); early(0, 3)
    jobs(3, 6)
    gathered(1, 2); early(1, 2)
    quad_sent(1, 2); quad_sent(0, 3); br_load(1).start()
    produce(0)
    fold(1, 1); raw(1, 0); fold(0, 2)
    br_load(1).wait(); raw(0, 1)
    late(0, 3); late(1, 2); late_b(1)
    jobs(6, 8)
    gathered(0, 2); early(0, 2)
    quad_sent(0, 2); br_load(0).start()
    gathered(1, 1); early(1, 1)
    fold(1, 0); fold(0, 1)
    br_load(0).wait(); raw(0, 0)
    for c in range(QUAD): home(2, c)
    raw(2, 0)
    gathered(0, 1); early(0, 1); late(0, 2)
    late(1, 1); late(0, 1)
    fold(0, 0); fold(2, 0)
    gathered(1, 0); gathered(0, 0); gathered(2, 0)
    home(1); home(0)

    ends = []
    def give(src, dst, column, n):
        def into(h): return dst.at[:, :, pl.ds(pl.multiple_of(column * MID + h * WIDE, WIDE), WIDE)]
        c = pltpu.make_async_remote_copy(src_ref=src, dst_ref=into(half), send_sem=end_send.at[n], recv_sem=end_recv.at[n], device_id=(1 - half, f), device_id_type=MESH)
        c.start()
        k = pltpu.make_async_copy(src, into(half), end_local.at[n])
        k.start()
        back = pltpu.make_async_remote_copy(src_ref=src, dst_ref=into(1 - half), send_sem=end_send.at[n], recv_sem=end_recv.at[n], device_id=(1 - half, f), device_id_type=MESH)
        ends.append((c, k, back))
    for t in range(TAPS):
        if t < 7: src = total(1, 0).at[:, :, pl.ds(t * WIDE, WIDE)]
        else: src = total(2, 0).at[:, :, pl.ds((t - 7) * WIDE, WIDE)]
        give(src, merge_out, t, t)
    for t in range(4):
        give(total(0, 0).at[:, :, pl.ds(t * WIDE, WIDE)], branch_out, t, TAPS + t)
    for i in range(LINE):
        if i < 2: quad_sent(0, i)
        if i < 2: quad_sent(1, i)
        if i:
            line_sent(0, i); line_sent(1, i)
            for c in range(QUAD): line_sent(2, i, c)
    quad_sent(2, 0)
    for n in (6, 7):
        own_copy(n).wait(); far_copy(n).wait_send()
    for n in range(8): far_copy(n).wait_recv()
    for c, k, back in ends:
        c.wait_send(); k.wait(); back.wait_recv()

def scatter_call(x, d3, act, ud, br, w, cid=2):
    D = pltpu.SemaphoreType.DMA
    V = lambda *s: pltpu.VMEM(s, BF)
    return pl.pallas_call(
        scatter_kernel,
        out_shape=(jax.ShapeDtypeStruct((2, 128, TAPS * MID), BF), jax.ShapeDtypeStruct((2, 64, 4 * MID), BF), jax.ShapeDtypeStruct((PIX, CIN), F32), jax.ShapeDtypeStruct((PIX, CIN), BF)),
        in_specs=[pl.BlockSpec(memory_space=pl.ANY)] * 6,
        out_specs=(pl.BlockSpec(memory_space=pl.ANY),) * 4,
        scratch_shapes=[V(ROWS, 1024), V(PAIRBINS, MID), V(ROWS + 64, STRIP), V(PAIRBINS, TAPS * WIDE), V(2, 4, 128, 1024), V(2, 4, 256, CUT), V(16, 256, 512),
            V(4, 3, 64, 1024), V(4, 3, 64, 1024), V(4, 3, 128, CUT), V(4, 3, 128, CUT), V(1, 3, 128, 512), V(1, 3, 128, 512),
            V(5, 2, 64, 1024), V(5, 2, 128, CUT), V(5, 4, 256, 512), V(2, 256, TAPS * WIDE), pltpu.VMEM((2, PIX, WIDE), F32), V(2, PIX, WIDE),
            D((4,)), D((3, 4, 2, 3)), D((3, 4, 2, 3)), D((2, 4)), D((2, 5)), D((4, 4)), D((5, 4)), D((13,)), D((13,)), D((2,)), D((2,)), D((2,)), D((8,)), D((2,)), D((13,))],
        compiler_params=pltpu.CompilerParams(collective_id=cid, has_side_effects=True, vmem_limit_bytes=63 * 1024 * 1024),
        name="scatter",
    )(x, d3, act, ud, br, w)


def bin_bounds(boxes, axis):
    shape = (NB, 8) if axis == 0 else (8, NB)
    bin_ = lax.broadcasted_iota(jnp.int32, shape, axis)
    what = lax.broadcasted_iota(jnp.int32, shape, 1 - axis)
    side = jnp.zeros(shape, jnp.int32)
    at = jnp.full(shape, -1, jnp.int32)
    for (start, size, _), bins in zip(SPANS, BIN_COUNTS):
        here = (bin_ >= start) & (bin_ < start + size)
        side = jnp.where(here, bins, side)
        at = jnp.where(here, bin_ - start, at)
    real = at >= 0
    side = jnp.maximum(side, 1)
    image = at // (side * side)
    across = at % side
    down = (at // side) % side
    by_row = what < 4
    base = jnp.zeros(shape, jnp.int32)
    extent = jnp.zeros(shape, jnp.int32)
    for k in range(IMG):
        base = jnp.where(image == k, jnp.where(by_row, boxes[k, 0], boxes[k, 1]), base)
        extent = jnp.where(image == k, jnp.where(by_row, boxes[k, 2], boxes[k, 3]), extent)
    index = jnp.where(by_row, down, across) + what % 2
    value = base + (index * extent + jnp.where(what % 4 == 0, 0, side - 1)) // side
    return jnp.where(real, value, 0)


def paired(features, region_boxes, branch_w, merge_w, class_w, norm_gain, norm_bias, grad_logits):
    half = lax.axis_index("bn")
    boxes = region_boxes[0]
    (
        merge_g, branch_g, masked, spread_grad, binned, active, pooled, centred, inverse, pool_t, counts,
        logit_own, logit_far, small,
    ) = forward_call(
        merge_w, branch_w, features.reshape(PIX, CIN), bin_bounds(boxes, 0), bin_bounds(boxes, 1),
        jnp.pad(grad_logits[0], ((0, 0), (0, LANES - CLS))), jnp.pad(class_w, ((0, 0), (0, LANES - CLS))),
        norm_gain, norm_bias,
    )
    logits = (logit_own[:, :CLS] + logit_far[:, :CLS])[None]
    gains = lax.dynamic_slice_in_dim(norm_gain, half * WIDE, WIDE, 1).astype(F32)
    biases = lax.dynamic_slice_in_dim(norm_bias, half * WIDE, WIDE, 1).astype(F32)
    pair = 2
    branch_full = branch_g.reshape(CIN, 4 * WIDE)
    merge_up = merge_g[8:].reshape(CIN, TAPS * WIDE)
    branch_of = [0] * 16 + [1] * 16 + [2] * 48 + [3] * 176
    chosen = jnp.asarray(branch_of)[:, None] == jnp.arange(4)[None, :]

    def choose(value, width):
        cut = value.reshape(pair, NB, 4, width)
        return jnp.sum(jnp.where(chosen[None, :, :, None], cut, 0), axis=2)

    def widen(value):
        cut = jnp.where(chosen[None, :, :, None], value[:, :, None, :], 0)
        return cut.reshape(pair * NB, 4 * value.shape[2])

    grad_active = choose(dot(binned, merge_up, ((1,), (1,))), MID)
    mine = lax.dynamic_slice_in_dim(grad_active, half * WIDE, WIDE, 2)
    theirs = lax.dynamic_slice_in_dim(grad_active, (1 - half) * WIDE, WIDE, 2)
    grad_active = mine + swap(theirs.astype(BF))[::-1].astype(F32)
    gain_rows, bias_rows, outs = [], [], []
    for branch, (start, size, room) in enumerate(SPANS):
        c = centred.reshape(pair, NB, WIDE)[:, start : start + room]
        grad_normed_b = grad_active[:, start : start + room] * silu_slope(c * gains[branch] + biases[branch])
        gain_row = jnp.sum(grad_normed_b * c, axis=(0, 1))
        bias_row = jnp.sum(grad_normed_b, axis=(0, 1))
        gain_rows.append(gain_row)
        bias_rows.append(bias_row)
        outs.append(
            gains[branch] * inverse[branch] * (grad_normed_b - (bias_row + c * gain_row) / (pair * size))
        )
    grad_out = widen(jnp.concatenate(outs, axis=1).astype(BF))
    grad_branch = dot(pooled, grad_out, ((0,), (0,))).astype(BF)
    grad_pooled = dot(grad_out, branch_full, ((1,), (1,)))
    grad_pooled = (grad_pooled / counts[:, :1]).astype(BF).reshape(pair, NB, CIN)

    share_merge, share_branch, own_part, far_part = scatter_call(
        masked, spread_grad, active, binned, grad_branch.reshape(16, 128, 4 * WIDE), merge_g
    )
    mine_pooled = jnp.concatenate([grad_pooled[0], swap(grad_pooled[1])], axis=0)
    mine_pools = jnp.concatenate([pool_t[0], pool_t[0]], axis=1)
    grad_features = dot(mine_pools, mine_pooled)
    first = bin_bounds(boxes, 1)[:, :IMG]
    pixel = jnp.arange(PIX, dtype=jnp.int32)[:, None]
    row, col = pixel // SIDE_C, pixel % SIDE_C
    inside = jnp.any((row >= first[2]) & (row < first[3]) & (col >= first[6]) & (col < first[7]), axis=1)
    grad_features = (grad_features + own_part + far_part.astype(F32))[None] * inside.astype(F32)[None, :, None]

    def placed(value, axis):
        shape = list(value.shape)
        shape[axis] = MID
        return lax.dynamic_update_slice_in_dim(jnp.zeros(shape, F32), value, half * WIDE, axis)

    total_class, total_gain, total_bias = lax.psum(
        (
            placed(small[:CLS].T, 0),
            placed(jnp.stack(gain_rows + [small[24]]), 1),
            placed(jnp.stack(bias_rows + [small[25]]), 1),
        ),
        ("bn", "fsdp"),
    )
    return (
        logits,
        grad_features,
        share_branch.reshape(128, 4 * MID).astype(F32),
        share_merge.reshape(256, TAPS * MID).astype(F32),
        total_class,
        total_gain,
        total_bias,
    )


def solution(mesh):
    placed = (
        P(("bn", "fsdp"), None, None),
        P(("bn", "fsdp"), None, None),
        P("fsdp", None),
        P("fsdp", None),
        P(),
        P(),
        P(),
        P(("bn", "fsdp"), None, None),
    )
    run = paired if dict(mesh.shape) == {"bn": 2, "fsdp": LINE * QUAD} else body
    return jax.shard_map(
        run,
        mesh=mesh,
        in_specs=placed,
        out_specs=(
            P(("bn", "fsdp"), None, None),
            P(("bn", "fsdp"), None, None),
            P("fsdp", None),
            P("fsdp", None),
            P(),
            P(),
            P(),
        ),
        check_vma=False,
    )
```

```python
import jax
import jax.numpy as jnp

from jax import lax
from jax.experimental import pallas as pl
from jax.experimental.pallas import tpu as pltpu
from jax.sharding import PartitionSpec as P

CIN = 2048
MID = 512
CLS = 19
IMG = 4
SIDE_R = 32
SIDE_C = 32
PIX = 1024
TAPS = 9
EPSILON = 1e-05
BIN_COUNTS = (1, 2, 3, 6)
SIZES = tuple(IMG * bins * bins for bins in BIN_COUNTS)
STARTS = (0, 4, 20, 56)
BINS = 200


def region_maps(region_boxes, bins):
    canvases = region_boxes.shape[0]
    top = region_boxes[:, :, 0][:, :, None]
    left = region_boxes[:, :, 1][:, :, None]
    height = region_boxes[:, :, 2][:, :, None]
    width = region_boxes[:, :, 3][:, :, None]
    pixel = jnp.arange(PIX, dtype=jnp.int32)
    rel_row = (pixel // SIDE_C)[None, None, :] - top
    rel_col = (pixel % SIDE_C)[None, None, :] - left
    index = jnp.arange(bins, dtype=jnp.int32)[None, None, :, None]
    row_low = index * height[..., None] // bins
    row_high = ((index + 1) * height[..., None] + bins - 1) // bins
    col_low = index * width[..., None] // bins
    col_high = ((index + 1) * width[..., None] + bins - 1) // bins
    row_in = (rel_row[:, :, None, :] >= row_low) & (rel_row[:, :, None, :] < row_high)
    col_in = (rel_col[:, :, None, :] >= col_low) & (rel_col[:, :, None, :] < col_high)
    pool = (row_in[:, :, :, None, :] & col_in[:, :, None, :, :]).reshape(
        canvases, IMG * bins * bins, PIX
    )
    inside_row = (rel_row >= 0) & (rel_row < height)
    inside_col = (rel_col >= 0) & (rel_col < width)
    near_row = rel_row * bins // height
    near_col = rel_col * bins // width
    up_row = inside_row[:, :, None, :] & (near_row[:, :, None, :] == index)
    up_col = inside_col[:, :, None, :] & (near_col[:, :, None, :] == index)
    upmap = (up_row[:, :, :, None, :] & up_col[:, :, None, :, :]).reshape(
        canvases, IMG * bins * bins, PIX
    )
    inside = jnp.any(inside_row & inside_col, axis=1)
    return (pool, upmap, inside)


def silu_slope(value):
    sigma = jax.nn.sigmoid(value)
    return sigma * (1.0 + value * (1.0 - sigma))


def swap(value):
    return lax.ppermute(value, "bn", [(0, 1), (1, 0)])


def both(value):
    return jnp.concatenate([value, swap(value)], axis=0)


def dot(a, b, dims=((1,), (0,))):
    return lax.dot_general(a, b, (dims, ((), ())), preferred_element_type=jnp.float32)


def rolled(value, shift):
    rows = value.shape[0]
    if shift == 0:
        return value
    pad = jnp.zeros((abs(shift),) + value.shape[1:], value.dtype)
    if shift > 0:
        return jnp.concatenate([value[shift:], pad], axis=0)
    return jnp.concatenate([pad, value[: rows + shift]], axis=0)


def own_half(value, half, width):
    rows = value.shape[0]
    cut = value.reshape(rows, -1, 2, width)
    return lax.dynamic_index_in_dim(cut, half, axis=2, keepdims=False).reshape(rows, -1)


def gather_weights(branch_half, merge_half):
    return (
        lax.all_gather(branch_half, "fsdp", axis=0, tiled=True),
        lax.all_gather(merge_half, "fsdp", axis=0, tiled=True),
    )


def scatter_grads(grad_branch, grad_merge):
    return (
        lax.psum_scatter(grad_branch, "fsdp", scatter_dimension=0, tiled=True),
        lax.psum_scatter(grad_merge, "fsdp", scatter_dimension=0, tiled=True),
    )


def body(features, region_boxes, branch_w, merge_w, class_w, norm_gain, norm_bias, grad_logits):
    half = lax.axis_index("bn")
    wide = MID // 2
    branch_full, merge_full = gather_weights(
        own_half(branch_w, half, wide), own_half(merge_w, half, wide)
    )
    gains = lax.dynamic_slice_in_dim(norm_gain, half * wide, wide, 1).astype(jnp.float32)
    biases = lax.dynamic_slice_in_dim(norm_bias, half * wide, wide, 1).astype(jnp.float32)
    class_half = lax.dynamic_slice_in_dim(class_w, half * wide, wide, 0)
    feats = both(features)
    boxes = both(region_boxes)
    cotangent = both(grad_logits)
    pair = feats.shape[0]
    rows = pair * PIX
    pools = []
    upmaps = []
    inside = None
    for bins in BIN_COUNTS:
        pool, upmap, inside = region_maps(boxes, bins)
        pools.append(pool)
        upmaps.append(upmap)
    counts = jnp.concatenate(
        [jnp.sum(pool.astype(jnp.float32), axis=2) for pool in pools], axis=1
    )
    pools = jnp.concatenate(pools, axis=1).astype(jnp.bfloat16)
    upmaps = jnp.concatenate(upmaps, axis=1).astype(jnp.bfloat16)
    inside_float = inside.astype(jnp.float32)
    weight_in = inside_float.reshape(rows, 1)
    masked = (feats * inside.astype(jnp.bfloat16)[:, :, None]).reshape(rows, CIN)
    pooled_sum = jnp.einsum("cnp,cpd->cnd", pools, feats, preferred_element_type=jnp.float32)
    pooled = (pooled_sum / counts[:, :, None]).astype(jnp.bfloat16)

    spans = [slice(s, s + n) for s, n in zip(STARTS, SIZES)]
    outs = []
    stats = []
    for branch, span in enumerate(spans):
        entries = pair * SIZES[branch]
        value = jnp.einsum(
            "cnd,do->cno",
            pooled[:, span],
            branch_full[:, branch * wide : (branch + 1) * wide],
            preferred_element_type=jnp.float32,
        )
        mean = jnp.sum(value, axis=(0, 1)) / entries
        spread = jnp.sum(value * value, axis=(0, 1)) / entries - mean * mean
        inverse = lax.rsqrt(spread + EPSILON)
        centred = (value - mean) * inverse
        normed = centred * gains[branch] + biases[branch]
        outs.append(jax.nn.silu(normed).astype(jnp.bfloat16))
        stats.append((inverse, centred, normed, entries))
    active = jnp.concatenate(outs, axis=1)
    other = swap(active)
    active_full = jnp.where(
        half == 0,
        jnp.concatenate([active, other[::-1]], axis=2),
        jnp.concatenate([other[::-1], active], axis=2),
    )
    lifted = jnp.concatenate(
        [
            jnp.einsum(
                "cno,ok->cnk",
                active_full[:, span],
                merge_full[CIN + branch * MID : CIN + (branch + 1) * MID],
                preferred_element_type=jnp.float32,
            ).astype(jnp.bfloat16)
            for branch, span in enumerate(spans)
        ],
        axis=1,
    )
    spans_up = jnp.swapaxes(upmaps, 1, 2).reshape(rows, BINS)
    strip = 3 * wide
    column = jnp.zeros((rows, strip), jnp.float32)
    for dr in range(3):
        shift = (dr - 1) * SIDE_C
        cut = slice(dr * strip, (dr + 1) * strip)
        column = column + dot(rolled(masked, shift), merge_full[:CIN, cut])
        raised = rolled(spans_up, shift).reshape(pair, PIX, BINS)
        column = column + jnp.einsum(
            "cpn,cnk->cpk", raised, lifted[:, :, cut], preferred_element_type=jnp.float32
        ).reshape(rows, strip)
    convolved = (
        rolled(column[:, :wide], -1)
        + column[:, wide : 2 * wide]
        + rolled(column[:, 2 * wide :], 1)
    )
    pixel_count = jnp.sum(inside_float)
    mean_merged = jnp.sum(convolved * weight_in, axis=0) / pixel_count
    spread_merged = (
        jnp.sum(convolved * convolved * weight_in, axis=0) / pixel_count
        - mean_merged * mean_merged
    )
    inverse_merged = lax.rsqrt(spread_merged + EPSILON)
    centred_merged = (convolved - mean_merged) * inverse_merged
    normed_merged = centred_merged * gains[4] + biases[4]
    hidden = jax.nn.silu(normed_merged).astype(jnp.bfloat16)
    logits_part = (dot(hidden, class_half) * weight_in).reshape(pair, PIX, CLS)
    logits = logits_part[:1] + swap(logits_part[1:])

    masked_grad = (cotangent * inside.astype(jnp.bfloat16)[:, :, None]).reshape(rows, CLS)
    grad_class = dot(hidden, masked_grad, ((0,), (0,)))
    grad_hidden = dot(masked_grad, class_half, ((1,), (1,)))
    grad_normed = grad_hidden * silu_slope(normed_merged)
    gain_merged = jnp.sum(grad_normed * centred_merged * weight_in, axis=0)
    bias_merged = jnp.sum(grad_normed * weight_in, axis=0)
    grad_conv = (
        weight_in
        * gains[4]
        * inverse_merged
        * (grad_normed - (bias_merged + centred_merged * gain_merged) / pixel_count)
    ).astype(jnp.bfloat16)
    spread_grad = jnp.concatenate(
        [
            rolled(grad_conv, -((tap // 3 - 1) * SIDE_C + (tap % 3 - 1)))
            for tap in range(TAPS)
        ],
        axis=1,
    )
    binned = jnp.einsum(
        "cnp,cpk->cnk",
        upmaps,
        spread_grad.reshape(pair, PIX, TAPS * wide),
        preferred_element_type=jnp.float32,
    ).astype(jnp.bfloat16)
    merge_rows = [dot(masked, spread_grad, ((0,), (0,))).astype(jnp.bfloat16)]
    actives = []
    for branch, span in enumerate(spans):
        merge_rows.append(
            jnp.einsum(
                "cno,cnk->ok",
                active_full[:, span],
                binned[:, span],
                preferred_element_type=jnp.float32,
            ).astype(jnp.bfloat16)
        )
        actives.append(
            jnp.einsum(
                "cnk,ok->cno",
                binned[:, span],
                merge_full[CIN + branch * MID : CIN + (branch + 1) * MID],
                preferred_element_type=jnp.float32,
            )
        )
    grad_merge = jnp.concatenate(merge_rows, axis=0)
    grad_active = jnp.concatenate(actives, axis=1)
    mine = lax.dynamic_slice_in_dim(grad_active, half * wide, wide, 2)
    theirs = lax.dynamic_slice_in_dim(grad_active, (1 - half) * wide, wide, 2)
    grad_active = mine + swap(theirs.astype(jnp.bfloat16))[::-1].astype(jnp.float32)
    gain_rows = []
    bias_rows = []
    branch_columns = []
    pooled_grads = []
    for branch, span in enumerate(spans):
        inverse, centred, normed, entries = stats[branch]
        grad_branch_normed = grad_active[:, span] * silu_slope(normed)
        gain_row = jnp.sum(grad_branch_normed * centred, axis=(0, 1))
        bias_row = jnp.sum(grad_branch_normed, axis=(0, 1))
        gain_rows.append(gain_row)
        bias_rows.append(bias_row)
        grad_out = (
            gains[branch]
            * inverse
            * (grad_branch_normed - (bias_row + centred * gain_row) / entries)
        ).astype(jnp.bfloat16)
        branch_columns.append(
            jnp.einsum(
                "cnd,cno->do", pooled[:, span], grad_out, preferred_element_type=jnp.float32
            ).astype(jnp.bfloat16)
        )
        pooled_grads.append(
            jnp.einsum(
                "cno,do->cnd",
                grad_out,
                branch_full[:, branch * wide : (branch + 1) * wide],
                preferred_element_type=jnp.float32,
            )
        )
    grad_branch = jnp.concatenate(branch_columns, axis=1)
    grad_pooled = (jnp.concatenate(pooled_grads, axis=1) / counts[:, :, None]).astype(jnp.bfloat16)
    grad_masked = dot(spread_grad, merge_full[:CIN], ((1,), (1,))).reshape(pair, PIX, CIN)
    grad_masked = grad_masked + jnp.einsum(
        "cnp,cnd->cpd", pools, grad_pooled, preferred_element_type=jnp.float32
    )
    away = swap(grad_masked[1:].astype(jnp.bfloat16))
    grad_features = (grad_masked[:1] + away.astype(jnp.float32)) * inside_float[:1, :, None]

    share_branch, share_merge = scatter_grads(grad_branch, grad_merge)
    share_branch = whole_rows(share_branch, half, wide)
    share_merge = whole_rows(share_merge, half, wide)

    def placed(value, axis):
        shape = list(value.shape)
        shape[axis] = MID
        return lax.dynamic_update_slice_in_dim(
            jnp.zeros(shape, jnp.float32), value, half * wide, axis
        )

    total_class, total_gain, total_bias = lax.psum(
        (
            placed(grad_class, 0),
            placed(jnp.stack(gain_rows + [gain_merged]), 1),
            placed(jnp.stack(bias_rows + [bias_merged]), 1),
        ),
        ("bn", "fsdp"),
    )
    return (logits, grad_features, share_branch, share_merge, total_class, total_gain, total_bias)


def whole_rows(share, half, wide):
    rows = share.shape[0]
    other = swap(share)
    mine = share.reshape(rows, -1, 1, wide)
    other = other.reshape(rows, -1, 1, wide)
    joined = jnp.where(
        half == 0,
        jnp.concatenate([mine, other], axis=2),
        jnp.concatenate([other, mine], axis=2),
    )
    return joined.reshape(rows, -1).astype(jnp.float32)


MESH = pl.DeviceIdType.MESH
LINE, QUAD, WIDE = 4, 4, 256
CUT = 7 * WIDE
BF = jnp.bfloat16
F32 = jnp.float32
ROWS = 2048
STRIP = 3 * WIDE
NB = 256
PAIRBINS = 2 * NB
LANES = 128
SMALL = 32
SPANS = ((0, 4, 16), (16, 16, 16), (32, 36, 48), (80, 144, 176))


def place():
    half = lax.axis_index("bn")
    f = lax.axis_index("fsdp")
    return half, f, f // QUAD, f % QUAD


def turn(z, step):
    if step == 0:
        return z
    if step == 1:
        return z + 1 - 2 * (z % 2)
    if step == 2:
        return 2 - z // 2
    return 3 - 3 * (z // 2)


def greet(half, f, z, q, far=False):
    barrier = pltpu.get_barrier_semaphore()
    xq, yq = q + 1 - 2 * (q % 2), q + 2 - 4 * (q // 2)

    def signal(device):
        pl.semaphore_signal(barrier, inc=1, device_id=device, device_id_type=MESH)

    for device in ((half, z * QUAD + xq), (half, z * QUAD + yq), (1 - half, f)):
        signal(device)

    @pl.when(z < LINE - 1)
    def _():
        signal((half, f + QUAD))

    @pl.when(z > 0)
    def _():
        signal((half, f - QUAD))

    if far:
        signal((half, f + 2 * QUAD - 4 * QUAD * (z // 2)))
    pl.semaphore_wait(barrier, 5 + int(far) - (z // (LINE - 1)) - ((LINE - 1 - z) // (LINE - 1)))


def span_mask(shape, branch):
    row = lax.broadcasted_iota(jnp.int32, shape, 0)
    row = jnp.where(row >= NB, row - NB, row)
    if isinstance(branch, int):
        start, _, room = SPANS[branch]
        return (row >= start) & (row < start + room)
    kind = (row >= 16).astype(jnp.int32) + (row >= 32).astype(jnp.int32) + (row >= 80).astype(jnp.int32)
    return kind == branch


def mm(a, b, dims=((1,), (0,))):
    return lax.dot_general(a, b, (dims, ((), ())), preferred_element_type=F32)


def block(n, size):
    return pl.ds(pl.multiple_of(n * size, size), size)


def forward_kernel(
    merge_ref, branch_ref, feats_ref, g_ref, box_ref, class_ref, gain_ref, bias_ref,
    merge_out, branch_out, x_out, d3_out, ud_out, act_out, pooled_out, xhat_out, inv_out, pt_out, count_out,
    logit_own, logit_far, small_out,
    branch_own, merge_own, x, acc, wbuf, bfull, aw, awb, pm, um, ut, pt, pooled, act, act_own, xhat, inv, cv, dy, d3, ud,
    w_in, cnt, t1, t2, g, stage, small,
    local_sem, z_send, z_recv, q_send, q_recv, zb_send, zb_recv, core_send, core_recv, w_sem, out_sem,
):
    half, f, z, q = place()
    xq, yq, dq = q + 1 - 2 * (q % 2), q + 2 - 4 * (q // 2), 3 - q
    L = [turn(z, i) for i in range(LINE)]

    def cut_copy(src, dst, t, n):
        return pltpu.make_async_copy(
            src.at[:, pl.ds(pl.multiple_of(t * MID + half * WIDE, WIDE), WIDE)],
            dst.at[:, pl.ds(t * WIDE, WIDE)],
            local_sem.at[n],
        )

    own_copies = [cut_copy(branch_ref, branch_own, t, t) for t in range(4)] + [
        cut_copy(merge_ref, merge_own, t, 4 + t) for t in range(TAPS)
    ]
    for c in own_copies:
        c.start()
    core = (1 - half, f)
    own_loads = [
        pltpu.make_async_copy(g_ref, g.at[0], local_sem.at[15]),
        pltpu.make_async_copy(feats_ref, x.at[pl.ds(32, PIX)], local_sem.at[16]),
    ]
    for c in own_loads:
        c.start()

    def to_core(src, dst, n):
        return pltpu.make_async_remote_copy(
            src_ref=src, dst_ref=dst, send_sem=core_send.at[n], recv_sem=core_recv.at[n], device_id=core, device_id_type=MESH
        )

    crossing = [
        to_core(t1.at[0], t1.at[1], 0),
        to_core(t2.at[0], t2.at[1], 1),
        to_core(g_ref, g.at[1], 2),
        to_core(feats_ref, x.at[pl.ds(32 + PIX, PIX)], 3),
    ]
    greet(half, f, z, q)
    for c in own_copies:
        c.wait()
    keep = [
        pltpu.make_async_copy(branch_own, branch_out.at[f], local_sem.at[0]),
        pltpu.make_async_copy(merge_own, merge_out.at[f], local_sem.at[1]),
    ]

    def columns(kind):
        return pl.ds(0, CUT) if kind == 1 else pl.ds(CUT, 2 * WIDE)

    def piece(kind, owner, part=None):
        rows = 128 if kind == 0 else 256
        at = slice(None) if part is None else pl.ds(part * (rows // 2), rows // 2)
        return branch_out.at[owner, at] if kind == 0 else merge_out.at[owner, at, columns(kind)]

    def own_piece(kind):
        return branch_own if kind == 0 else merge_own.at[:, columns(kind)]

    def remote(ref, s, r, dev, src=None):
        return pltpu.make_async_remote_copy(
            src_ref=ref if src is None else src, dst_ref=ref, send_sem=s, recv_sem=r, device_id=dev, device_id_type=MESH
        )

    def beside(d):
        return (half, f + QUAD if d == 0 else f - QUAD)

    def z_copy(kind, i, d):
        src = own_piece(kind) if i == 0 else None
        return remote(piece(kind, L[i] * QUAD + q), z_send.at[kind, d, L[i]], z_recv.at[kind, L[i]], beside(d), src)

    def zb_copy(i, c, d):
        return remote(piece(2, L[i] * QUAD + c), zb_send.at[d, L[i], c], zb_recv.at[L[i], c], beside(d))

    def z_both(i, fn):
        @pl.when((L[i] <= z) & (z < LINE - 1))
        def _():
            fn(0)

        @pl.when((L[i] >= z) & (z > 0))
        def _():
            fn(1)

    def q_copy(kind, i, axis, what):
        dev = (half, z * QUAD + (xq if axis == 0 else yq))
        if what == 0:
            ref = piece(kind, L[i] * QUAD + q)
        else:
            ref = piece(kind, L[i] * QUAD + (yq if axis == 0 else xq), 1 - axis)
        src = own_piece(kind) if i == 0 and what == 0 else None
        return remote(ref, q_send.at[kind, L[i], axis, what], q_recv.at[kind, L[i], axis, what], dev, src)

    def q_arrive(kind, i, axis, what):
        owner = L[i] * QUAD + ((xq if axis == 0 else yq) if what == 0 else dq)
        ref = piece(kind, owner, None if what == 0 else 1 - axis)
        remote(ref, q_send.at[kind, L[i], axis, what], q_recv.at[kind, L[i], axis, what], core).wait_recv()

    def spread(kind, i):
        for axis in (0, 1):
            q_copy(kind, i, axis, 0).start()

    def pass_on(kind, i):
        for axis in (0, 1):
            q_arrive(kind, i, axis, 0)
            q_copy(kind, i, 1 - axis, 1).start()

    def corner(kind, i):
        for axis in (0, 1):
            q_arrive(kind, i, axis, 1)

    def z_step(kind, i):
        if i:
            remote(piece(kind, L[i] * QUAD + q), z_send.at[kind, 0, L[i]], z_recv.at[kind, L[i]], core).wait_recv()
        z_both(i, lambda d: z_copy(kind, i, d).start())

    def zb_step(i):
        for c in range(QUAD):
            if i:
                remote(piece(2, L[i] * QUAD + c), zb_send.at[0, L[i], c], zb_recv.at[L[i], c], core).wait_recv()
            z_both(i, lambda d: zb_copy(i, c, d).start())

    def bounds():
        for ref, axis in ((t1, 0), (t2, 1)):
            shape = (NB, 8) if axis == 0 else (8, NB)
            bin_ = lax.broadcasted_iota(jnp.int32, shape, axis)
            what = lax.broadcasted_iota(jnp.int32, shape, 1 - axis)
            by_row = what < 4
            ceil = jnp.bitwise_and(what, 3) > 0
            result = jnp.zeros(shape, jnp.int32)
            for (start, size, room), bins in zip(SPANS, BIN_COUNTS):
                at = bin_ - start
                image = lax.shift_right_logical(at * -(-65536 // (bins * bins)), 16)
                rest = at - image * (bins * bins)
                down = lax.shift_right_logical(rest * -(-65536 // bins), 16)
                index = jnp.where(by_row, down, rest - down * bins) + jnp.bitwise_and(what, 1)
                base = jnp.zeros(shape, jnp.int32)
                extent = jnp.zeros(shape, jnp.int32)
                for k in range(IMG):
                    base = jnp.where(image == k, jnp.where(by_row, box_ref[k, 0], box_ref[k, 1]), base)
                    extent = jnp.where(image == k, jnp.where(by_row, box_ref[k, 2], box_ref[k, 3]), extent)
                value = index * extent + jnp.where(ceil, bins - 1, 0)
                value = base + lax.shift_right_logical(value * -(-65536 // bins), 16)
                result = jnp.where((at >= 0) & (at < size), value, result)
            ref[0] = result

    def maps(c):
        def across(n, _):
            at = block(n, 32)
            p = lax.broadcasted_iota(jnp.int32, (32, PIX), 1)
            row, col = lax.shift_right_logical(p, 5), jnp.bitwise_and(p, 31)
            t = t1[c, at, :]
            cell = lambda k: t[:, k : k + 1]
            for ref, k in ((pm, 0), (um, 2)):
                hit = (row >= cell(k)) & (row < cell(k + 1)) & (col >= cell(k + 4)) & (col < cell(k + 5))
                value = jnp.where(hit, 1.0, 0.0)
                ref[c, at, :] = value.astype(BF)
                if k == 0:
                    total = jnp.maximum(jnp.sum(value, axis=1, keepdims=True), 1.0)
                    cnt[pl.ds(pl.multiple_of(c * NB + n * 32, 32), 32), :] = jnp.broadcast_to(total, (32, LANES))
            return 0

        lax.fori_loop(0, NB // 32, across, 0)

        def down(n, _):
            p = lax.broadcasted_iota(jnp.int32, (LANES, NB), 0) + n * LANES
            row, col = lax.shift_right_logical(p, 5), jnp.bitwise_and(p, 31)
            cell = lambda k: t2[c, k : k + 1, :]
            for k in (0, 2):
                hit = (row >= cell(k)) & (row < cell(k + 1)) & (col >= cell(k + 4)) & (col < cell(k + 5))
                value = jnp.where(hit, 1.0, 0.0)
                if k == 0:
                    pt[c, block(n, LANES), :] = value.astype(BF)
                else:
                    ut[c, pl.ds(pl.multiple_of(32 + n * LANES, 32), LANES), :] = value.astype(BF)
                    first = lax.broadcasted_iota(jnp.int32, (LANES, NB), 1) < IMG
                    inside = jnp.sum(jnp.where(first, value, 0.0), axis=1, keepdims=True)
                    w_in[pl.ds(pl.multiple_of(c * PIX + n * LANES, LANES), LANES), :] = inside
            return 0

        lax.fori_loop(0, PIX // LANES, down, 0)
        ut[c, 0:32, :] = jnp.zeros((32, NB), BF)
        ut[c, 32 + PIX : 64 + PIX, :] = jnp.zeros((32, NB), BF)

    def mask_pool(c):
        def mask(n, _):
            at = pl.ds(pl.multiple_of(32 + c * PIX + n * 64, 32), 64)
            w = w_in[pl.ds(pl.multiple_of(c * PIX + n * 64, 64), 64), :]
            x[at, :] = (x[at, :].astype(F32) * w).astype(BF)
            return 0

        lax.fori_loop(0, PIX // 64, mask, 0)

        def pool(n, _):
            cols = block(n, 512)
            total = mm(pm[c], x[pl.ds(32 + c * PIX, PIX), cols])
            pooled[pl.ds(c * NB, NB), cols] = (total / cnt[pl.ds(c * NB, NB), 0:1]).astype(BF)
            return 0

        lax.fori_loop(0, CIN // 512, pool, 0)

    def branches():
        load = pltpu.make_async_copy(branch_out, bfull, local_sem.at[2])
        load.start()
        load.wait()
        for b, (_, size, _) in enumerate(SPANS):
            weight = bfull[:, :, b * WIDE : (b + 1) * WIDE].reshape(CIN, WIDE)
            here = span_mask((PAIRBINS, WIDE), b)
            value = jnp.where(here, mm(pooled[...], weight), 0.0)
            entries = 2.0 * size
            mean = jnp.sum(value, axis=0, keepdims=True) / entries
            spread_ = jnp.sum(value * value, axis=0, keepdims=True) / entries - mean * mean
            inverse = lax.rsqrt(spread_ + EPSILON)
            centred = (value - mean) * inverse
            gain = gain_ref[b : b + 1, pl.ds(pl.multiple_of(half * WIDE, WIDE), WIDE)].astype(F32)
            bias = bias_ref[b : b + 1, pl.ds(pl.multiple_of(half * WIDE, WIDE), WIDE)].astype(F32)
            normed = centred * gain + bias
            active = normed * jax.nn.sigmoid(normed)
            inv[b : b + 1, :] = inverse
            if b == 0:
                xhat[...] = jnp.where(here, centred, 0.0)
                act_own[...] = jnp.where(here, active, 0.0).astype(BF)
            else:
                xhat[...] = jnp.where(here, centred, xhat[...])
                act_own[...] = jnp.where(here, active, act_own[...].astype(F32)).astype(BF)
        inv[4:8, :] = jnp.zeros((4, WIDE), F32)
        cols = pl.ds(pl.multiple_of(half * WIDE, WIDE), WIDE)
        sends = [
            to_core(act_own.at[pl.ds(c * NB, NB)], act.at[pl.ds((1 - c) * NB, NB), cols], 4 + c) for c in (0, 1)
        ]
        for s in sends:
            s.start()
        act[:, cols] = act_own[...]
        return sends

    def act_arrive():
        cols = pl.ds(pl.multiple_of((1 - half) * WIDE, WIDE), WIDE)
        for c in (0, 1):
            to_core(act_own.at[pl.ds(c * NB, NB)], act.at[pl.ds((1 - c) * NB, NB), cols], 4 + c).wait_recv()

    def w_load(kind, i, k, c):
        cols = columns(kind)
        return pltpu.make_async_copy(merge_out.at[L[i] * QUAD + c, :, cols], wbuf.at[k, :, cols], w_sem.at[k])

    def column_of(k):
        return (q % 2 + k % 2) % 2 + 2 * ((q // 2 + k // 2) % 2)

    def contract(kind, i, ks):
        for k in ks:
            w_load(kind, i, k, column_of(k)).start()

        def feature(k, _):
            c = column_of(k)
            w_load(kind, i, k, c).wait()
            lanes = block(L[i] * QUAD + c, WIDE)
            for canvas in (0, 1):
                r = canvas * PIX
                rows = pl.ds(r, PIX)
                if kind == 1:
                    acc[rows, :] = acc[rows, :] + (
                        mm(x[pl.ds(r, PIX), lanes], wbuf[k, :, 0:STRIP])
                        + mm(x[pl.ds(r + 32, PIX), lanes], wbuf[k, :, STRIP : 2 * STRIP])
                    )
                    acc[rows, 0:WIDE] = acc[rows, 0:WIDE] + mm(x[pl.ds(r + 64, PIX), lanes], wbuf[k, :, 2 * STRIP : CUT])
                else:
                    acc[rows, WIDE:STRIP] = acc[rows, WIDE:STRIP] + mm(x[pl.ds(r + 64, PIX), lanes], wbuf[k, :, CUT:])
            return 0

        def raised(k, _):
            c = column_of(k)
            w_load(kind, i, k, c).wait()
            here = span_mask((PAIRBINS, WIDE), 2 * (L[i] - 2) + c // 2)
            lhs = jnp.where(here, act[:, block(c % 2, WIDE)].astype(F32), 0.0).astype(BF)

            def strip(n, _):
                cols = block(n, WIDE)
                aw[:, cols] = aw[:, cols] + mm(lhs, wbuf[k, :, cols])
                return 0

            if kind == 1:
                lax.fori_loop(0, 7, strip, 0)
            else:
                lax.fori_loop(7, TAPS, strip, 0)
            return 0

        @pl.when(L[i] < 2)
        def _():
            lax.fori_loop(ks[0], ks[-1] + 1, feature, 0)

        @pl.when(L[i] >= 2)
        def _():
            lax.fori_loop(ks[0], ks[-1] + 1, raised, 0)

    def clear():
        x[0:32, :] = jnp.zeros((32, CIN), BF)
        x[32 + ROWS : 64 + ROWS, :] = jnp.zeros((32, CIN), BF)

        def clear_acc(n, _):
            acc[block(n, LANES), :] = jnp.zeros((LANES, STRIP), F32)
            return 0

        lax.fori_loop(0, ROWS // LANES, clear_acc, 0)

        def clear_aw(n, _):
            aw[block(n, 32), :] = jnp.zeros((32, TAPS * WIDE), F32)
            return 0

        lax.fori_loop(0, PAIRBINS // 32, clear_aw, 0)

    z_step(0, 0)
    spread(0, 0)
    spread(2, 0)
    bounds()
    for c in crossing:
        c.start()
    for c in keep:
        c.start()
    z_step(0, 1)
    spread(0, 1)
    maps(0)
    z_step(0, 2)
    spread(0, 2)
    z_step(0, 3)
    spread(0, 3)
    z_step(1, 0)
    spread(1, 0)
    for c in own_loads:
        c.wait()
    mask_pool(0)
    pass_on(0, 0)
    pass_on(2, 0)
    pass_on(0, 1)
    for c in crossing:
        c.wait_recv()
    maps(1)
    pass_on(0, 2)
    pass_on(0, 3)
    mask_pool(1)
    x_save = pltpu.make_async_copy(x.at[pl.ds(32, ROWS)], x_out, out_sem.at[0])
    x_save.start()
    z_step(1, 1)
    spread(1, 1)
    corner(2, 0)
    for c in keep:
        c.wait()
    zb_step(0)
    clear()
    pass_on(1, 0)
    z_step(1, 2)
    spread(1, 2)
    for i in range(LINE):
        corner(0, i)
    act_sends = branches()
    pass_on(1, 1)
    act_arrive()
    contract(1, 0, (0, 1, 2))
    z_step(1, 3)
    spread(1, 3)
    corner(1, 0)
    contract(1, 0, (3,))
    contract(1, 1, (0, 1, 2))
    zb_step(1)
    pass_on(1, 2)
    contract(2, 0, (0, 1, 2, 3))
    contract(1, 2, (0, 1, 2))
    corner(1, 1)
    contract(1, 1, (3,))
    contract(2, 1, (0, 1, 2, 3))
    zb_step(2)
    pass_on(1, 3)
    contract(2, 2, (0, 1, 2, 3))
    contract(1, 3, (0, 1, 2))
    corner(1, 2)
    contract(1, 2, (3,))
    zb_step(3)
    contract(2, 3, (0, 1, 2, 3))
    corner(1, 3)
    contract(1, 3, (3,))

    def lower(n, _):
        at = block(n, 32)
        awb[at, :] = aw[at, :].astype(BF)
        return 0

    lax.fori_loop(0, PAIRBINS // 32, lower, 0)
    ones = lambda: jnp.zeros((1, WIDE), F32)
    s1, s2, n2 = ones(), ones(), jnp.zeros((1, 1), F32)
    for c in (0, 1):
        rows = pl.ds(c * PIX, PIX)
        for dr in range(3):
            acc[rows, :] = acc[rows, :] + mm(
                ut[c, 32 * dr : 32 * dr + PIX, :], awb[c * NB : (c + 1) * NB, dr * STRIP : (dr + 1) * STRIP]
            )
        value = (
            pltpu.roll(acc[rows, 0:WIDE], 1, 0)
            + acc[rows, WIDE : 2 * WIDE]
            + pltpu.roll(acc[rows, 2 * WIDE : STRIP], PIX - 1, 0)
        )
        cv[rows, :] = value
        w = w_in[rows, :]
        kept = value * w
        s1 = s1 + jnp.sum(kept, axis=0, keepdims=True)
        s2 = s2 + jnp.sum(kept * value, axis=0, keepdims=True)
        n2 = n2 + jnp.sum(w, axis=0, keepdims=True)
    mean = s1 / n2
    inverse = lax.rsqrt(s2 / n2 - mean * mean + EPSILON)
    cols = pl.ds(pl.multiple_of(half * WIDE, WIDE), WIDE)
    gain = gain_ref[4:5, cols].astype(F32)
    bias = bias_ref[4:5, cols].astype(F32)
    weight = class_ref[cols, :]

    def slopes(n, carry):
        sum_b, sum_g, sum_c = carry
        at = block(n, 256)
        w = w_in[at, :]
        centred = (cv[at, :] - mean) * inverse
        normed = centred * gain + bias
        sigma = jax.nn.sigmoid(normed)
        hidden = (normed * sigma).astype(BF)
        stage[at, :] = mm(hidden, weight) * w
        grad = (g[n // 4, block(n % 4, 256), :].astype(F32) * w).astype(BF)
        sum_c = sum_c + mm(grad, hidden, ((0,), (0,)))
        slope = mm(grad, weight, ((1,), (1,))) * (sigma * (1.0 + normed * (1.0 - sigma)))
        dy[at, :] = slope
        cv[at, :] = centred
        return (
            sum_b + jnp.sum(slope, axis=0, keepdims=True),
            sum_g + jnp.sum(slope * centred, axis=0, keepdims=True),
            sum_c,
        )

    sum_b, sum_g, sum_c = lax.fori_loop(0, ROWS // 256, slopes, (ones(), ones(), jnp.zeros((CLS, WIDE), F32)))
    logit_sends = [
        pltpu.make_async_copy(stage.at[pl.ds(0, PIX)], logit_own, out_sem.at[1]),
        to_core(stage.at[pl.ds(PIX, PIX)], logit_far, 6),
    ]
    for c in logit_sends:
        c.start()
    small[0:CLS, :] = sum_c
    small[CLS:24, :] = jnp.zeros((24 - CLS, WIDE), F32)
    small[24:25, :] = sum_g
    small[25:26, :] = sum_b
    small[26:SMALL, :] = jnp.zeros((SMALL - 26, WIDE), F32)
    d3[0:32, :] = jnp.zeros((32, STRIP), BF)
    d3[32 + ROWS : 64 + ROWS, :] = jnp.zeros((32, STRIP), BF)
    for c in (0, 1):
        rows = pl.ds(c * PIX, PIX)
        value = (w_in[rows, :] * (gain * inverse)) * (dy[rows, :] - (sum_b + cv[rows, :] * sum_g) / n2)
        to = pl.ds(32 + c * PIX, PIX)
        d3[to, 0:WIDE] = pltpu.roll(value, PIX - 1, 0).astype(BF)
        d3[to, WIDE : 2 * WIDE] = value.astype(BF)
        d3[to, 2 * WIDE : STRIP] = pltpu.roll(value, 1, 0).astype(BF)
    for c in (0, 1):
        for dr in range(3):
            ud[c * NB : (c + 1) * NB, dr * STRIP : (dr + 1) * STRIP] = mm(
                um[c], d3[pl.ds(32 * (2 - dr) + c * PIX, PIX), :]
            ).astype(BF)
    saves = [
        pltpu.make_async_copy(a, b, out_sem.at[2 + n])
        for n, (a, b) in enumerate(
            (
                (d3, d3_out), (ud, ud_out), (act, act_out), (pooled, pooled_out), (xhat, xhat_out),
                (inv, inv_out), (pt, pt_out), (cnt, count_out), (small, small_out),
            )
        )
    ]
    for c in saves:
        c.start()

    for i in range(LINE):
        for kind in (0, 1):
            z_both(i, lambda d: z_copy(kind, i, d).wait_send())
        for c in range(QUAD):
            z_both(i, lambda d: zb_copy(i, c, d).wait_send())
        for kind in (0, 1) + ((2,) if i == 0 else ()):
            for axis in (0, 1):
                for what in (0, 1):
                    q_copy(kind, i, axis, what).wait_send()
    for c in crossing:
        c.wait_send()
    for c in act_sends:
        c.wait_send()
    logit_sends[0].wait()
    logit_sends[1].wait()
    x_save.wait()
    for c in saves:
        c.wait()


def forward_call(merge_w, branch_w, feats, g, boxes, class_w, gains, biases):
    D = pltpu.SemaphoreType.DMA
    V = lambda *s: pltpu.VMEM(s, BF)
    W = lambda *s: pltpu.VMEM(s, F32)
    S = jax.ShapeDtypeStruct
    hbm = pl.BlockSpec(memory_space=pl.ANY)
    vmem = pl.BlockSpec(memory_space=pltpu.VMEM)
    outs = (
        S((16, 256, TAPS * WIDE), BF), S((16, 128, 4 * WIDE), BF), S((ROWS, CIN), BF), S((ROWS + 64, STRIP), BF),
        S((PAIRBINS, TAPS * WIDE), BF), S((PAIRBINS, MID), BF), S((PAIRBINS, CIN), BF), S((PAIRBINS, WIDE), F32),
        S((8, WIDE), F32), S((2, PIX, NB), BF), S((PAIRBINS, LANES), F32), S((PIX, CLS), F32), S((PIX, CLS), F32),
        S((SMALL, WIDE), F32),
    )
    return pl.pallas_call(
        forward_kernel,
        out_shape=outs,
        in_specs=[hbm] * 4 + [pl.BlockSpec(memory_space=pltpu.SMEM)] + [vmem] * 3,
        out_specs=(hbm,) * len(outs),
        scratch_shapes=[
            V(128, 4 * WIDE), V(256, TAPS * WIDE), V(ROWS + 64, CIN), W(ROWS, STRIP), V(QUAD, 256, TAPS * WIDE),
            V(16, 128, 4 * WIDE), W(PAIRBINS, TAPS * WIDE), V(PAIRBINS, TAPS * WIDE), V(2, NB, PIX), V(2, NB, PIX),
            V(2, PIX + 64, NB), V(2, PIX, NB), V(PAIRBINS, CIN), V(PAIRBINS, MID), V(PAIRBINS, WIDE),
            W(PAIRBINS, WIDE), W(8, WIDE), W(ROWS, WIDE), W(ROWS, WIDE), V(ROWS + 64, STRIP), V(PAIRBINS, TAPS * WIDE),
            W(ROWS, 1), W(PAIRBINS, LANES), pltpu.VMEM((2, NB, 8), jnp.int32), pltpu.VMEM((2, 8, NB), jnp.int32),
            V(2, PIX, CLS), W(ROWS, CLS), W(SMALL, WIDE),
            D((17,)), D((2, 2, 4)), D((2, 4)), D((3, 4, 2, 2)), D((3, 4, 2, 2)), D((2, 4, 4)), D((4, 4)),
            D((7,)), D((7,)), D((4,)), D((11,)),
        ],
        compiler_params=pltpu.CompilerParams(collective_id=0, has_side_effects=True, vmem_limit_bytes=63 * 1024 * 1024),
        name="forward",
    )(merge_w, branch_w, feats, g, boxes, class_w, gains, biases)


def backward_kernel(
    x_hbm, d3_hbm, act_hbm, ud_hbm, w_hbm, branch_hbm, pooled_hbm, xhat_hbm, pt_hbm, cnt_hbm, small_hbm, inv_ref, gain_ref, bias_ref,
    merge_out, branch_out, own_out, far_out, small_out,
    xt, act, d3, ud, g0, g1, b_all, fx0, fy0, fx1, fy1, fx2, fy2, zs0, zs1, zs2, wbuf, own_stage, far_stage,
    pooled, dzw, pt, cnt, bgbuf, small, small_in,
    local_sem, q_send, q_recv, z_send, z_recv, zb_send, zb_recv, end_send, end_recv, w_sem, own_sem, far_send, far_recv, end_local,
    act_send, act_recv, bg_sem, pool_sem, sum_send, sum_recv,
):
    half, f, z, q = place()
    xq, yq, dq = q + 1 - 2 * (q % 2), q + 2 - 4 * (q // 2), 3 - q
    L = [turn(z, i) for i in range(LINE)]
    xhat = own_stage.at[1, pl.ds(0, PAIRBINS)]
    loads = [
        pltpu.make_async_copy(a, b, local_sem.at[n])
        for n, (a, b) in enumerate(
            (
                (d3_hbm, d3), (ud_hbm, ud), (act_hbm, act), (pt_hbm, pt), (cnt_hbm, cnt), (xhat_hbm, xhat),
                (small_hbm, small.at[0, pl.ds(0, SMALL)]),
            )
        )
    ]
    for c in loads:
        c.start()

    def fetch_rows(i):
        return pltpu.make_async_copy(
            x_hbm.at[:, pl.ds(pl.multiple_of(L[i] * 1024, 1024), 1024)], xt, local_sem.at[7]
        )

    def rows_start(i):
        @pl.when(L[i] < 2)
        def _():
            fetch_rows(i).start()

    rows_start(3)
    greet(half, f, z, q, True)
    for c in loads:
        c.wait()
    from_x, from_y, zslot = (fx0, fx1, fx2), (fy0, fy1, fy2), (zs0, zs1, zs2)
    HALF = (64, 128, 128)

    def column_of(k):
        return (q % 2 + k % 2) % 2 + 2 * ((q // 2 + k // 2) % 2)

    def own(kind, i, c):
        if kind == 0:
            return g0.at[i % 2, c]
        return g1.at[i % 2, c] if kind == 1 else b_all.at[L[i] * QUAD + c]

    def part(ref, kind, h):
        return ref.at[pl.ds(h * HALF[kind], HALF[kind])]

    def slot(kind, i, axis, what):
        ref = (from_x, from_y)[axis][kind]
        return ref.at[L[i], what] if kind < 2 else ref.at[0, what]

    def q_copy(kind, i, axis, what):
        to = xq if axis == 0 else yq
        if what == 0:
            src = part(own(kind, i, dq), kind, 1 - axis)
        elif what == 1:
            src = part(own(kind, i, to), kind, axis)
        else:
            src = part(own(kind, i, to), kind, 1 - axis)
        return pltpu.make_async_remote_copy(
            src_ref=src, dst_ref=slot(kind, i, axis, what), send_sem=q_send.at[kind, L[i], axis, what],
            recv_sem=q_recv.at[kind, L[i], axis, what], device_id=(half, z * QUAD + to), device_id_type=MESH,
        )

    def add_into(dst, *others):
        def rows16(n, _):
            at = block(n, 16)
            total = dst[at, :].astype(F32)
            for o in others:
                total = total + o[at, :].astype(F32)
            dst[at, :] = total.astype(BF)
            return 0

        lax.fori_loop(0, dst.shape[0] // 16, rows16, 0)

    def raw(kind, i):
        for what in (0, 2):
            for axis in (0, 1):
                q_copy(kind, i, axis, what).start()

    def fold(kind, i):
        for axis in (1, 0):
            q_copy(kind, i, axis, 0).wait_recv()
            to = xq if axis == 1 else yq
            add_into(part(own(kind, i, to), kind, 1 - axis), slot(kind, i, axis, 0))
            q_copy(kind, i, 1 - axis, 1).start()

    def gathered(kind, i):
        for axis in (0, 1):
            for what in (1, 2):
                q_copy(kind, i, axis, what).wait_recv()
        mine = own(kind, i, q)
        add_into(slot(kind, i, 0, 1), part(mine, kind, 0), slot(kind, i, 1, 2))
        add_into(slot(kind, i, 0, 2), part(mine, kind, 1), slot(kind, i, 1, 1))

    def total(kind, i):
        return from_x[kind].at[L[i] if kind < 2 else 0, pl.ds(1, 2)]

    def z_src(kind, i, c):
        return total(kind, i) if kind < 2 else own(2, i, c)

    def z_dst(kind, n, c):
        return zslot[kind].at[n] if kind < 2 else zs2.at[n, c]

    def z_sems(kind, level, n, c):
        if kind < 2:
            return z_send.at[kind, level], z_recv.at[kind, n]
        return zb_send.at[level, c], zb_recv.at[n, c]

    def z_copy(kind, i, c, up):
        level = L[i]
        n = level if up else level + (LINE - level) * (1 - jnp.minimum(z - 1 - level, 1))
        s, r = z_sems(kind, level, n, c)
        return pltpu.make_async_remote_copy(
            src_ref=z_src(kind, i, c), dst_ref=z_dst(kind, n, c), send_sem=s, recv_sem=r,
            device_id=(half, f + QUAD if up else f - QUAD), device_id_type=MESH,
        )

    def z_take(kind, i, n, c):
        s, r = z_sems(kind, L[i], n, c)
        pltpu.make_async_remote_copy(
            src_ref=z_src(kind, i, c), dst_ref=z_dst(kind, n, c), send_sem=s, recv_sem=r,
            device_id=(1 - half, f), device_id_type=MESH,
        ).wait_recv()
        if kind < 2:
            for h in (0, 1):
                add_into(total(kind, i).at[h], z_dst(kind, n, c).at[h])
        else:
            add_into(own(2, i, c), z_dst(kind, n, c))

    def early(kind, i, c=None):
        @pl.when((L[i] > z) & (z == 0))
        def _():
            z_copy(kind, i, c, True).start()

        @pl.when((L[i] < z) & (z == LINE - 1))
        def _():
            z_copy(kind, i, c, False).start()

    def late(kind, i, c=None):
        @pl.when((L[i] > z) & (z > 0))
        def _():
            z_take(kind, i, L[i], c)
            z_copy(kind, i, c, True).start()

        @pl.when((L[i] < z) & (z < LINE - 1))
        def _():
            z_take(kind, i, L[i], c)
            z_copy(kind, i, c, False).start()

    def home(kind, c=None):
        @pl.when(z > 0)
        def _():
            z_take(kind, 0, z, c)

        @pl.when(z < LINE - 1)
        def _():
            z_take(kind, 0, LINE, c)

    def line_sent(kind, i, c=None):
        @pl.when(L[i] > z)
        def _():
            z_copy(kind, i, c, True).wait_send()

        @pl.when(L[i] < z)
        def _():
            z_copy(kind, i, c, False).wait_send()

    def quad_sent(kind, i):
        for axis in (0, 1):
            for what in (0, 1, 2):
                q_copy(kind, i, axis, what).wait_send()

    def early_b(i):
        for c in range(QUAD):
            early(2, i, c)

    def late_b(i):
        for c in range(QUAD):
            late(2, i, c)

    def produce(i):
        level = L[i]

        @pl.when(level < 2)
        def _():
            fetch_rows(i).wait()

        @pl.when(level >= 2)
        def _():
            for c in range(QUAD):
                here = span_mask((PAIRBINS, WIDE), 2 * (level - 2) + c // 2)
                rows = act[:, (c % 2) * WIDE : (c % 2 + 1) * WIDE].astype(F32)
                xt[0:PAIRBINS, c * WIDE : (c + 1) * WIDE] = jnp.where(here, rows, 0.0).astype(BF)

        for k in (3, 1, 2, 0):
            c = column_of(k)

            def store(dr, value):
                if dr < 2:
                    g1[i % 2, c, :, dr * STRIP : (dr + 1) * STRIP] = value.astype(BF)
                else:
                    g1[i % 2, c, :, 2 * STRIP : CUT] = value[:, 0:WIDE].astype(BF)
                    b_all[level * QUAD + c] = value[:, WIDE:].astype(BF)

            @pl.when(level < 2)
            def _():
                for dr in range(3):
                    store(dr, mm(xt[:, block(c, WIDE)], d3[pl.ds(32 * (2 - dr), ROWS), :], ((0,), (0,))))

            @pl.when(level >= 2)
            def _():
                for dr in range(3):
                    store(dr, mm(xt[0:PAIRBINS, block(c, WIDE)], ud[:, dr * STRIP : (dr + 1) * STRIP], ((0,), (0,))))

            if k == 3:
                q_copy(1, i, 0, 0).start()
                q_copy(1, i, 1, 0).start()
            elif k:
                q_copy(1, i, k - 1, 2).start()
        if i:
            rows_start(i - 1)

    def w_load(n):
        return pltpu.make_async_copy(w_hbm.at[n], wbuf.at[n % 2], w_sem.at[n % 2])

    def spans(b):
        start, _, room = SPANS[b]
        return [pl.ds(c * NB + start, room) for c in (0, 1)]

    def far_rows(n):
        return pltpu.make_async_remote_copy(
            src_ref=far_stage.at[0, pl.ds(n * NB, NB)], dst_ref=far_stage.at[1, pl.ds((1 - n) * NB, NB)],
            send_sem=act_send.at[n], recv_sem=act_recv.at[n], device_id=(1 - half, f), device_id_type=MESH,
        )

    def bin_gradients():
        w_load(8).start()
        for n in range(8):
            w_load(8 + n).wait()
            if n < 7:
                w_load(9 + n).start()
            b, h = n // 2, n % 2
            lhs = jnp.concatenate([ud[s, :] for s in spans(b)], axis=0)
            value = mm(lhs, wbuf[n % 2], ((1,), (1,)))
            room = SPANS[b][2]
            for c, s in enumerate(spans(b)):
                own_stage[0, pl.ds(h * PAIRBINS + c * NB + SPANS[b][0], room), :] = value[c * room : (c + 1) * room]
        w_load(0).start()
        away = pl.ds(pl.multiple_of((1 - half) * PAIRBINS, PAIRBINS), PAIRBINS)
        far_stage[0, 0:PAIRBINS, :] = own_stage[0, away, :].astype(BF)
        for n in (0, 1):
            far_rows(n).start()

    def branch_gradients():
        for n in (0, 1):
            far_rows(n).wait_recv()
        home_rows = pl.multiple_of(half * PAIRBINS, PAIRBINS)
        cols = pl.ds(pl.multiple_of(half * WIDE, WIDE), WIDE)
        dzw[...] = jnp.zeros((PAIRBINS, 4 * WIDE), BF)
        for b, (start, size, room) in enumerate(SPANS):
            gain = gain_ref[b : b + 1, cols].astype(F32)
            bias = bias_ref[b : b + 1, cols].astype(F32)
            both_c, both_d = [], []
            for c in (0, 1):
                rows = pl.ds(c * NB + start, room)
                centred = own_stage[1, rows, :]
                grad = own_stage[0, pl.ds(home_rows + c * NB + start, room), :] + far_stage[1, rows, :].astype(F32)
                normed = centred * gain + bias
                sigma = jax.nn.sigmoid(normed)
                both_c.append(centred)
                both_d.append(grad * (sigma * (1.0 + normed * (1.0 - sigma))))
            sum_b = sum(jnp.sum(d, axis=0, keepdims=True) for d in both_d)
            sum_g = sum(jnp.sum(d * e, axis=0, keepdims=True) for d, e in zip(both_d, both_c))
            small[0, 26 + b : 27 + b, :] = sum_g
            small[0, 30 + b : 31 + b, :] = sum_b
            for c in (0, 1):
                value = (gain * inv_ref[b : b + 1, :]) * (both_d[c] - (sum_b + both_c[c] * sum_g) / (2.0 * size))
                dzw[c * NB + start : c * NB + start + room, b * WIDE : (b + 1) * WIDE] = value.astype(BF)
        small[0, 34:40, :] = jnp.zeros((6, WIDE), F32)

    def pool_load(i):
        return pltpu.make_async_copy(
            pooled_hbm.at[:, pl.ds(pl.multiple_of(L[i] * 512, 512), 512)], pooled, pool_sem.at[0]
        )

    def produce_branch(i):
        pool_load(i).wait()
        g0[i % 2] = mm(pooled[...], dzw[...], ((0,), (0,))).astype(BF).reshape(QUAD, 128, 4 * WIDE)
        if i:
            pool_load(i - 1).start()

    def own_copy(n):
        return pltpu.make_async_copy(own_stage.at[n % 2], own_out.at[:, block(n, WIDE)], own_sem.at[n % 2])

    def far_copy(n):
        return pltpu.make_async_remote_copy(
            src_ref=far_stage.at[n % 2], dst_ref=far_out.at[:, block(n, WIDE)], send_sem=far_send.at[n % 2],
            recv_sem=far_recv.at[n], device_id=(1 - half, f), device_id_type=MESH,
        )

    def bg_load(n):
        return pltpu.make_async_copy(branch_hbm.at[pl.ds(n * 2, 2)], bgbuf.at[n % 2], bg_sem.at[n % 2])

    def jobs(first, last):
        def job(n, _):
            w_load(n).wait()
            bg_load(n).wait()

            @pl.when(n < 7)
            def _():
                w_load(n + 1).start()
                bg_load(n + 1).start()

            @pl.when(n >= 2)
            def _():
                own_copy(n - 2).wait()
                far_copy(n - 2).wait_send()

            bins = (mm(dzw[...], bgbuf[n % 2].reshape(WIDE, 4 * WIDE), ((1,), (1,))) / cnt[:, 0:1]).astype(BF)
            for canvas in (0, 1):
                value = mm(pt[canvas], bins[canvas * NB : (canvas + 1) * NB])
                for dr in range(3):
                    value = value + mm(
                        d3[pl.ds(32 * (2 - dr) + canvas * PIX, PIX), :], wbuf[n % 2, :, dr * STRIP : (dr + 1) * STRIP],
                        ((1,), (1,)),
                    )
                first_bins = lax.broadcasted_iota(jnp.int32, (PIX, LANES), 1) < IMG
                inside = jnp.sum(
                    jnp.where(first_bins, pt[canvas, :, 0:LANES].astype(F32), 0.0), axis=1, keepdims=True
                )
                value = value * inside
                if canvas == 0:
                    own_stage[n % 2] = value
                else:
                    far_stage[n % 2] = value.astype(BF)
            own_copy(n).start()
            far_copy(n).start()
            return 0

        lax.fori_loop(first, last, job, 0)

    def sum_copy(n):
        zz = z + 1 - 2 * (z % 2) if n == 2 else z + 2 - 4 * (z // 2)
        to = (z * QUAD + xq, z * QUAD + yq, zz * QUAD + q, zz * QUAD + q)[n]
        return pltpu.make_async_remote_copy(
            src_ref=small.at[n], dst_ref=small_in.at[n], send_sem=sum_send.at[n], recv_sem=sum_recv.at[n],
            device_id=(half, to), device_id_type=MESH,
        )

    def sum_take(n):
        sum_copy(n).wait_recv()
        small[n + 1] = small[n] + small_in[n]
        if n < 3:
            sum_copy(n + 1).start()

    pool_load(3).start()
    bg_load(0).start()
    produce(3)
    early_b(3)
    produce(2)
    early_b(2)
    bin_gradients()
    fold(1, 3)
    branch_gradients()
    sum_copy(0).start()
    produce_branch(3)
    raw(0, 3)
    produce_branch(2)
    gathered(1, 3)
    early(1, 3)
    late_b(3)
    for n in (0, 1):
        far_rows(n).wait_send()
    jobs(0, 2)
    sum_take(0)
    quad_sent(1, 3)
    fold(1, 2)
    produce(1)
    early_b(1)
    fold(0, 3)
    raw(0, 2)
    late(1, 3)
    late_b(2)
    gathered(0, 3)
    early(0, 3)
    jobs(2, 4)
    sum_take(1)
    gathered(1, 2)
    early(1, 2)
    quad_sent(1, 2)
    fold(1, 1)
    produce(0)
    quad_sent(0, 3)
    produce_branch(1)
    fold(0, 2)
    raw(0, 1)
    late(0, 3)
    late(1, 2)
    late_b(1)
    jobs(4, 6)
    sum_take(2)
    gathered(0, 2)
    early(0, 2)
    quad_sent(0, 2)
    produce_branch(0)
    raw(0, 0)
    gathered(1, 1)
    early(1, 1)
    fold(1, 0)
    fold(0, 1)
    jobs(6, 8)
    sum_take(3)
    for c in range(QUAD):
        home(2, c)
    raw(2, 0)
    gathered(0, 1)
    early(0, 1)
    late(0, 2)
    late(1, 1)
    late(0, 1)
    fold(0, 0)
    fold(2, 0)
    gathered(1, 0)
    gathered(0, 0)
    gathered(2, 0)
    home(1)
    home(0)

    ends = []

    def give(src, into, n):
        c = pltpu.make_async_remote_copy(
            src_ref=src, dst_ref=into(half), send_sem=end_send.at[n], recv_sem=end_recv.at[n],
            device_id=(1 - half, f), device_id_type=MESH,
        )
        c.start()
        k = pltpu.make_async_copy(src, into(half), end_local.at[n])
        k.start()
        back = pltpu.make_async_remote_copy(
            src_ref=src, dst_ref=into(1 - half), send_sem=end_send.at[n], recv_sem=end_recv.at[n],
            device_id=(1 - half, f), device_id_type=MESH,
        )
        ends.append((c, k, back))

    def columns(ref, t):
        return lambda h: ref.at[:, :, pl.ds(pl.multiple_of(t * MID + h * WIDE, WIDE), WIDE)]

    for t in range(TAPS):
        src = total(1, 0).at[:, :, pl.ds(t * WIDE, WIDE)] if t < 7 else total(2, 0).at[:, :, pl.ds((t - 7) * WIDE, WIDE)]
        give(src, columns(merge_out, t), t)
    for t in range(4):
        give(total(0, 0).at[:, :, pl.ds(t * WIDE, WIDE)], columns(branch_out, t), TAPS + t)
    give(small.at[4], lambda h: small_out.at[h], 13)

    for n in range(4):
        sum_copy(n).wait_send()
    for i in range(LINE):
        if i < 2:
            quad_sent(0, i)
            quad_sent(1, i)
        if i:
            line_sent(0, i)
            line_sent(1, i)
            for c in range(QUAD):
                line_sent(2, i, c)
    quad_sent(2, 0)
    for n in (6, 7):
        own_copy(n).wait()
        far_copy(n).wait_send()
    for n in range(8):
        far_copy(n).wait_recv()
    for c, k, back in ends:
        c.wait_send()
        k.wait()
        back.wait_recv()


def backward_call(x, d3, act, ud, w, branch, pooled, xhat, pt, cnt, small, inv, gains, biases):
    D = pltpu.SemaphoreType.DMA
    V = lambda *s: pltpu.VMEM(s, BF)
    W = lambda *s: pltpu.VMEM(s, F32)
    S = jax.ShapeDtypeStruct
    hbm = pl.BlockSpec(memory_space=pl.ANY)
    vmem = pl.BlockSpec(memory_space=pltpu.VMEM)
    outs = (
        S((2, 128, TAPS * MID), BF), S((2, 64, 4 * MID), BF), S((PIX, CIN), F32), S((PIX, CIN), BF), S((2, 40, WIDE), F32),
    )
    return pl.pallas_call(
        backward_kernel,
        out_shape=outs,
        in_specs=[hbm] * 11 + [vmem] * 3,
        out_specs=(hbm,) * len(outs),
        scratch_shapes=[
            V(ROWS, 1024), V(PAIRBINS, MID), V(ROWS + 64, STRIP), V(PAIRBINS, TAPS * WIDE), V(2, 4, 128, 1024),
            V(2, 4, 256, CUT), V(16, 256, 512), V(4, 3, 64, 1024), V(4, 3, 64, 1024), V(4, 3, 128, CUT), V(4, 3, 128, CUT),
            V(1, 3, 128, 512), V(1, 3, 128, 512), V(5, 2, 64, 1024), V(5, 2, 128, CUT), V(5, 4, 256, 512),
            V(2, 256, TAPS * WIDE), W(2, PIX, WIDE), V(2, PIX, WIDE), V(PAIRBINS, 512), V(PAIRBINS, 4 * WIDE),
            V(2, PIX, NB), W(PAIRBINS, LANES), V(2, 2, 128, 4 * WIDE), W(5, 40, WIDE), W(4, 40, WIDE),
            D((8,)), D((3, 4, 2, 3)), D((3, 4, 2, 3)), D((2, 4)), D((2, 5)), D((4, 4)), D((5, 4)), D((14,)), D((14,)),
            D((2,)), D((2,)), D((2,)), D((8,)), D((14,)), D((2,)), D((2,)), D((2,)), D((1,)), D((4,)), D((4,)),
        ],
        compiler_params=pltpu.CompilerParams(collective_id=1, has_side_effects=True, vmem_limit_bytes=63 * 1024 * 1024),
        name="backward",
    )(x, d3, act, ud, w, branch, pooled, xhat, pt, cnt, small, inv, gains, biases)


def paired(features, region_boxes, branch_w, merge_w, class_w, norm_gain, norm_bias, grad_logits):
    (
        merge_g, branch_g, masked, spread_grad, binned, active, pooled, centred, inverse, pool_t, counts,
        logit_own, logit_far, small,
    ) = forward_call(
        merge_w, branch_w, features.reshape(PIX, CIN), grad_logits[0], region_boxes[0], class_w, norm_gain, norm_bias,
    )
    logits = (logit_own + logit_far)[None]
    share_merge, share_branch, own_part, far_part, sums = backward_call(
        masked, spread_grad, active, binned, merge_g, branch_g, pooled, centred, pool_t, counts, small, inverse,
        norm_gain, norm_bias,
    )
    grad_features = (own_part + far_part.astype(F32))[None]
    sums = jnp.transpose(sums, (1, 0, 2)).reshape(40, MID)
    total_class = sums[:CLS].T
    total_gain = jnp.concatenate([sums[26:30], sums[24:25]], axis=0)
    total_bias = jnp.concatenate([sums[30:34], sums[25:26]], axis=0)
    return (
        logits,
        grad_features,
        share_branch.reshape(128, 4 * MID).astype(F32),
        share_merge.reshape(256, TAPS * MID).astype(F32),
        total_class,
        total_gain,
        total_bias,
    )


def solution(mesh):
    placed = (
        P(("bn", "fsdp"), None, None),
        P(("bn", "fsdp"), None, None),
        P("fsdp", None),
        P("fsdp", None),
        P(),
        P(),
        P(),
        P(("bn", "fsdp"), None, None),
    )
    run = paired if dict(mesh.shape) == {"bn": 2, "fsdp": LINE * QUAD} else body
    return jax.shard_map(
        run,
        mesh=mesh,
        in_specs=placed,
        out_specs=(
            P(("bn", "fsdp"), None, None),
            P(("bn", "fsdp"), None, None),
            P("fsdp", None),
            P("fsdp", None),
            P(),
            P(),
            P(),
        ),
        check_vma=False,
    )
```

```python
import jax
import jax.numpy as jnp

from jax import lax
from jax.experimental import pallas as pl
from jax.experimental.pallas import tpu as pltpu
from jax.sharding import PartitionSpec as P

CIN = 2048
MID = 512
CLS = 19
IMG = 4
SIDE_R = 32
SIDE_C = 32
PIX = 1024
TAPS = 9
EPSILON = 1e-05
BIN_COUNTS = (1, 2, 3, 6)
SIZES = tuple(IMG * bins * bins for bins in BIN_COUNTS)
STARTS = (0, 4, 20, 56)
BINS = 200


def region_maps(region_boxes, bins):
    canvases = region_boxes.shape[0]
    top = region_boxes[:, :, 0][:, :, None]
    left = region_boxes[:, :, 1][:, :, None]
    height = region_boxes[:, :, 2][:, :, None]
    width = region_boxes[:, :, 3][:, :, None]
    pixel = jnp.arange(PIX, dtype=jnp.int32)
    rel_row = (pixel // SIDE_C)[None, None, :] - top
    rel_col = (pixel % SIDE_C)[None, None, :] - left
    index = jnp.arange(bins, dtype=jnp.int32)[None, None, :, None]
    row_low = index * height[..., None] // bins
    row_high = ((index + 1) * height[..., None] + bins - 1) // bins
    col_low = index * width[..., None] // bins
    col_high = ((index + 1) * width[..., None] + bins - 1) // bins
    row_in = (rel_row[:, :, None, :] >= row_low) & (rel_row[:, :, None, :] < row_high)
    col_in = (rel_col[:, :, None, :] >= col_low) & (rel_col[:, :, None, :] < col_high)
    pool = (row_in[:, :, :, None, :] & col_in[:, :, None, :, :]).reshape(
        canvases, IMG * bins * bins, PIX
    )
    inside_row = (rel_row >= 0) & (rel_row < height)
    inside_col = (rel_col >= 0) & (rel_col < width)
    near_row = rel_row * bins // height
    near_col = rel_col * bins // width
    up_row = inside_row[:, :, None, :] & (near_row[:, :, None, :] == index)
    up_col = inside_col[:, :, None, :] & (near_col[:, :, None, :] == index)
    upmap = (up_row[:, :, :, None, :] & up_col[:, :, None, :, :]).reshape(
        canvases, IMG * bins * bins, PIX
    )
    inside = jnp.any(inside_row & inside_col, axis=1)
    return (pool, upmap, inside)


def silu_slope(value):
    sigma = jax.nn.sigmoid(value)
    return sigma * (1.0 + value * (1.0 - sigma))


def swap(value):
    return lax.ppermute(value, "bn", [(0, 1), (1, 0)])


def both(value):
    return jnp.concatenate([value, swap(value)], axis=0)


def dot(a, b, dims=((1,), (0,))):
    return lax.dot_general(a, b, (dims, ((), ())), preferred_element_type=jnp.float32)


def rolled(value, shift):
    rows = value.shape[0]
    if shift == 0:
        return value
    pad = jnp.zeros((abs(shift),) + value.shape[1:], value.dtype)
    if shift > 0:
        return jnp.concatenate([value[shift:], pad], axis=0)
    return jnp.concatenate([pad, value[: rows + shift]], axis=0)


def own_half(value, half, width):
    rows = value.shape[0]
    cut = value.reshape(rows, -1, 2, width)
    return lax.dynamic_index_in_dim(cut, half, axis=2, keepdims=False).reshape(rows, -1)


def gather_weights(branch_half, merge_half):
    return (
        lax.all_gather(branch_half, "fsdp", axis=0, tiled=True),
        lax.all_gather(merge_half, "fsdp", axis=0, tiled=True),
    )


def scatter_grads(grad_branch, grad_merge):
    return (
        lax.psum_scatter(grad_branch, "fsdp", scatter_dimension=0, tiled=True),
        lax.psum_scatter(grad_merge, "fsdp", scatter_dimension=0, tiled=True),
    )


def body(features, region_boxes, branch_w, merge_w, class_w, norm_gain, norm_bias, grad_logits):
    half = lax.axis_index("bn")
    wide = MID // 2
    branch_full, merge_full = gather_weights(
        own_half(branch_w, half, wide), own_half(merge_w, half, wide)
    )
    gains = lax.dynamic_slice_in_dim(norm_gain, half * wide, wide, 1).astype(jnp.float32)
    biases = lax.dynamic_slice_in_dim(norm_bias, half * wide, wide, 1).astype(jnp.float32)
    class_half = lax.dynamic_slice_in_dim(class_w, half * wide, wide, 0)
    feats = both(features)
    boxes = both(region_boxes)
    cotangent = both(grad_logits)
    pair = feats.shape[0]
    rows = pair * PIX
    pools = []
    upmaps = []
    inside = None
    for bins in BIN_COUNTS:
        pool, upmap, inside = region_maps(boxes, bins)
        pools.append(pool)
        upmaps.append(upmap)
    counts = jnp.concatenate(
        [jnp.sum(pool.astype(jnp.float32), axis=2) for pool in pools], axis=1
    )
    pools = jnp.concatenate(pools, axis=1).astype(jnp.bfloat16)
    upmaps = jnp.concatenate(upmaps, axis=1).astype(jnp.bfloat16)
    inside_float = inside.astype(jnp.float32)
    weight_in = inside_float.reshape(rows, 1)
    masked = (feats * inside.astype(jnp.bfloat16)[:, :, None]).reshape(rows, CIN)
    pooled_sum = jnp.einsum("cnp,cpd->cnd", pools, feats, preferred_element_type=jnp.float32)
    pooled = (pooled_sum / counts[:, :, None]).astype(jnp.bfloat16)

    spans = [slice(s, s + n) for s, n in zip(STARTS, SIZES)]
    outs = []
    stats = []
    for branch, span in enumerate(spans):
        entries = pair * SIZES[branch]
        value = jnp.einsum(
            "cnd,do->cno",
            pooled[:, span],
            branch_full[:, branch * wide : (branch + 1) * wide],
            preferred_element_type=jnp.float32,
        )
        mean = jnp.sum(value, axis=(0, 1)) / entries
        spread = jnp.sum(value * value, axis=(0, 1)) / entries - mean * mean
        inverse = lax.rsqrt(spread + EPSILON)
        centred = (value - mean) * inverse
        normed = centred * gains[branch] + biases[branch]
        outs.append(jax.nn.silu(normed).astype(jnp.bfloat16))
        stats.append((inverse, centred, normed, entries))
    active = jnp.concatenate(outs, axis=1)
    other = swap(active)
    active_full = jnp.where(
        half == 0,
        jnp.concatenate([active, other[::-1]], axis=2),
        jnp.concatenate([other[::-1], active], axis=2),
    )
    lifted = jnp.concatenate(
        [
            jnp.einsum(
                "cno,ok->cnk",
                active_full[:, span],
                merge_full[CIN + branch * MID : CIN + (branch + 1) * MID],
                preferred_element_type=jnp.float32,
            ).astype(jnp.bfloat16)
            for branch, span in enumerate(spans)
        ],
        axis=1,
    )
    spans_up = jnp.swapaxes(upmaps, 1, 2).reshape(rows, BINS)
    strip = 3 * wide
    column = jnp.zeros((rows, strip), jnp.float32)
    for dr in range(3):
        shift = (dr - 1) * SIDE_C
        cut = slice(dr * strip, (dr + 1) * strip)
        column = column + dot(rolled(masked, shift), merge_full[:CIN, cut])
        raised = rolled(spans_up, shift).reshape(pair, PIX, BINS)
        column = column + jnp.einsum(
            "cpn,cnk->cpk", raised, lifted[:, :, cut], preferred_element_type=jnp.float32
        ).reshape(rows, strip)
    convolved = (
        rolled(column[:, :wide], -1)
        + column[:, wide : 2 * wide]
        + rolled(column[:, 2 * wide :], 1)
    )
    pixel_count = jnp.sum(inside_float)
    mean_merged = jnp.sum(convolved * weight_in, axis=0) / pixel_count
    spread_merged = (
        jnp.sum(convolved * convolved * weight_in, axis=0) / pixel_count
        - mean_merged * mean_merged
    )
    inverse_merged = lax.rsqrt(spread_merged + EPSILON)
    centred_merged = (convolved - mean_merged) * inverse_merged
    normed_merged = centred_merged * gains[4] + biases[4]
    hidden = jax.nn.silu(normed_merged).astype(jnp.bfloat16)
    logits_part = (dot(hidden, class_half) * weight_in).reshape(pair, PIX, CLS)
    logits = logits_part[:1] + swap(logits_part[1:])

    masked_grad = (cotangent * inside.astype(jnp.bfloat16)[:, :, None]).reshape(rows, CLS)
    grad_class = dot(hidden, masked_grad, ((0,), (0,)))
    grad_hidden = dot(masked_grad, class_half, ((1,), (1,)))
    grad_normed = grad_hidden * silu_slope(normed_merged)
    gain_merged = jnp.sum(grad_normed * centred_merged * weight_in, axis=0)
    bias_merged = jnp.sum(grad_normed * weight_in, axis=0)
    grad_conv = (
        weight_in
        * gains[4]
        * inverse_merged
        * (grad_normed - (bias_merged + centred_merged * gain_merged) / pixel_count)
    ).astype(jnp.bfloat16)
    spread_grad = jnp.concatenate(
        [
            rolled(grad_conv, -((tap // 3 - 1) * SIDE_C + (tap % 3 - 1)))
            for tap in range(TAPS)
        ],
        axis=1,
    )
    binned = jnp.einsum(
        "cnp,cpk->cnk",
        upmaps,
        spread_grad.reshape(pair, PIX, TAPS * wide),
        preferred_element_type=jnp.float32,
    ).astype(jnp.bfloat16)
    merge_rows = [dot(masked, spread_grad, ((0,), (0,))).astype(jnp.bfloat16)]
    actives = []
    for branch, span in enumerate(spans):
        merge_rows.append(
            jnp.einsum(
                "cno,cnk->ok",
                active_full[:, span],
                binned[:, span],
                preferred_element_type=jnp.float32,
            ).astype(jnp.bfloat16)
        )
        actives.append(
            jnp.einsum(
                "cnk,ok->cno",
                binned[:, span],
                merge_full[CIN + branch * MID : CIN + (branch + 1) * MID],
                preferred_element_type=jnp.float32,
            )
        )
    grad_merge = jnp.concatenate(merge_rows, axis=0)
    grad_active = jnp.concatenate(actives, axis=1)
    mine = lax.dynamic_slice_in_dim(grad_active, half * wide, wide, 2)
    theirs = lax.dynamic_slice_in_dim(grad_active, (1 - half) * wide, wide, 2)
    grad_active = mine + swap(theirs.astype(jnp.bfloat16))[::-1].astype(jnp.float32)
    gain_rows = []
    bias_rows = []
    branch_columns = []
    pooled_grads = []
    for branch, span in enumerate(spans):
        inverse, centred, normed, entries = stats[branch]
        grad_branch_normed = grad_active[:, span] * silu_slope(normed)
        gain_row = jnp.sum(grad_branch_normed * centred, axis=(0, 1))
        bias_row = jnp.sum(grad_branch_normed, axis=(0, 1))
        gain_rows.append(gain_row)
        bias_rows.append(bias_row)
        grad_out = (
            gains[branch]
            * inverse
            * (grad_branch_normed - (bias_row + centred * gain_row) / entries)
        ).astype(jnp.bfloat16)
        branch_columns.append(
            jnp.einsum(
                "cnd,cno->do", pooled[:, span], grad_out, preferred_element_type=jnp.float32
            ).astype(jnp.bfloat16)
        )
        pooled_grads.append(
            jnp.einsum(
                "cno,do->cnd",
                grad_out,
                branch_full[:, branch * wide : (branch + 1) * wide],
                preferred_element_type=jnp.float32,
            )
        )
    grad_branch = jnp.concatenate(branch_columns, axis=1)
    grad_pooled = (jnp.concatenate(pooled_grads, axis=1) / counts[:, :, None]).astype(jnp.bfloat16)
    grad_masked = dot(spread_grad, merge_full[:CIN], ((1,), (1,))).reshape(pair, PIX, CIN)
    grad_masked = grad_masked + jnp.einsum(
        "cnp,cnd->cpd", pools, grad_pooled, preferred_element_type=jnp.float32
    )
    away = swap(grad_masked[1:].astype(jnp.bfloat16))
    grad_features = (grad_masked[:1] + away.astype(jnp.float32)) * inside_float[:1, :, None]

    share_branch, share_merge = scatter_grads(grad_branch, grad_merge)
    share_branch = whole_rows(share_branch, half, wide)
    share_merge = whole_rows(share_merge, half, wide)

    def placed(value, axis):
        shape = list(value.shape)
        shape[axis] = MID
        return lax.dynamic_update_slice_in_dim(
            jnp.zeros(shape, jnp.float32), value, half * wide, axis
        )

    total_class, total_gain, total_bias = lax.psum(
        (
            placed(grad_class, 0),
            placed(jnp.stack(gain_rows + [gain_merged]), 1),
            placed(jnp.stack(bias_rows + [bias_merged]), 1),
        ),
        ("bn", "fsdp"),
    )
    return (logits, grad_features, share_branch, share_merge, total_class, total_gain, total_bias)


def whole_rows(share, half, wide):
    rows = share.shape[0]
    other = swap(share)
    mine = share.reshape(rows, -1, 1, wide)
    other = other.reshape(rows, -1, 1, wide)
    joined = jnp.where(
        half == 0,
        jnp.concatenate([mine, other], axis=2),
        jnp.concatenate([other, mine], axis=2),
    )
    return joined.reshape(rows, -1).astype(jnp.float32)


MESH = pl.DeviceIdType.MESH
LINE, QUAD, WIDE = 4, 4, 256
QUART = 128
COLS = TAPS * QUART
CUT = 7 * QUART
KINDS = (0, 1, 2) if CUT < COLS else (0, 1)
BF = jnp.bfloat16
F32 = jnp.float32
CANV = 4
ROWS = CANV * PIX
SENT = PIX - SIDE_C
STRIP = 3 * QUART
TAIL = CUT - 2 * STRIP
NB = 256
BINS4 = CANV * NB
LANES = 128
SMALL = 32
SPANS = ((0, 4, 16), (16, 16, 16), (32, 36, 48), (80, 144, 176))


def place():
    half = lax.axis_index("bn")
    f = lax.axis_index("fsdp")
    q = f % QUAD
    return half, f, f // QUAD, q // 2, q % 2


def turn(z, step):
    if step == 0:
        return z
    if step == 1:
        return z + 1 - 2 * (z % 2)
    if step == 2:
        return 2 - z // 2
    return 3 - 3 * (z // 2)


def friends(half, f, x):
    beside = f + 1 - 2 * x
    return (1 - half, f), (half, beside), (1 - half, beside)


def greet(half, f, z, y, x, far=False):
    barrier = pltpu.get_barrier_semaphore()

    def signal(device):
        pl.semaphore_signal(barrier, inc=1, device_id=device, device_id_type=MESH)

    for device in friends(half, f, x) + ((half, f + 2 - 4 * y),):
        signal(device)

    @pl.when(z < LINE - 1)
    def _():
        signal((half, f + QUAD))

    @pl.when(z > 0)
    def _():
        signal((half, f - QUAD))

    if far:
        signal((half, f + 2 * QUAD - 4 * QUAD * (z // 2)))
    pl.semaphore_wait(barrier, 6 + int(far) - (z // (LINE - 1)) - ((LINE - 1 - z) // (LINE - 1)))


def span_mask(shape, branch):
    row = jnp.bitwise_and(lax.broadcasted_iota(jnp.int32, shape, 0), NB - 1)
    if isinstance(branch, int):
        start, _, room = SPANS[branch]
        return (row >= start) & (row < start + room)
    kind = (row >= 16).astype(jnp.int32) + (row >= 32).astype(jnp.int32) + (row >= 80).astype(jnp.int32)
    return kind == branch


def mm(a, b, dims=((1,), (0,))):
    return lax.dot_general(a, b, (dims, ((), ())), preferred_element_type=F32)


def block(n, size):
    return pl.ds(pl.multiple_of(n * size, size), size)


def forward_kernel(
    merge_ref, branch_ref, feats_ref, g_ref, box_ref, class_ref, gain_ref, bias_ref,
    merge_out, branch_out, x_out, d3_out, ud_out, act_out, pooled_out, xhat_out, inv_out, pt_out, count_out,
    logit_own, logit_far, small_out,
    branch_own, merge_own, x, acc, wfeat, wbuf, bfull, awb, pm, um, ut, pt, pooled, act, act_own, act_in, xhat, inv, cv, dy, d3,
    cnt, t2, g, stage, small,
    local_sem, z_send, z_recv, y_send, y_recv, x_send, x_recv, zb_send, zb_recv, table_send, table_recv, feat_send,
    feat_recv, act_send, act_recv, logit_send, logit_recv, w_sem, out_sem, raise_sem,
):
    half, f, z, y, xx = place()
    L = [turn(z, i) for i in range(LINE)]
    core, xdev, diag = friends(half, f, xx)
    ydev = (half, f + 2 - 4 * y)
    quarter = pl.multiple_of(half * WIDE + xx * QUART, QUART)
    other = pl.multiple_of(half * WIDE + (1 - xx) * QUART, QUART)

    def cut_copy(src, dst, j, t, n):
        start = pl.multiple_of(t * MID + (other if j else quarter), QUART)
        return pltpu.make_async_copy(src.at[:, pl.ds(start, QUART)], dst.at[j, :, pl.ds(t * QUART, QUART)], local_sem.at[n])

    own_copies = [cut_copy(branch_ref, branch_own, j, t, 4 * j + t) for j in (1, 0) for t in range(4)]
    own_copies += [cut_copy(merge_ref, merge_own, j, t, 8 + TAPS * j + t) for j in (1, 0) for t in range(TAPS)]
    for c in own_copies:
        c.start()
    own_loads = [
        pltpu.make_async_copy(g_ref, g.at[0], local_sem.at[26]),
        pltpu.make_async_copy(feats_ref, x.at[pl.ds(32, PIX)], local_sem.at[27]),
    ]
    for c in own_loads:
        c.start()

    def send(src, dst, s, r, dev):
        return pltpu.make_async_remote_copy(
            src_ref=src, dst_ref=dst, send_sem=s, recv_sem=r, device_id=dev, device_id_type=MESH
        )

    def tables(n):
        ref = (t2, g)[n]
        src = t2.at[0] if n == 0 else g_ref
        return [
            send(src, ref.at[j + 1], table_send.at[n, j], table_recv.at[n, j], dev) for j, dev in enumerate((core, xdev, diag))
        ]

    def base(c):
        return 32 + c * PIX + 32 * (c // 2)

    def feature_rows(c, n):
        return x.at[pl.ds(base(c), SENT), block(n, WIDE)]

    whole = send(feats_ref, x.at[pl.ds(32 + PIX, PIX)], feat_send.at[0, 0], feat_recv.at[0, 0], core)

    def first_level():
        return z * (1 - z // 2) + z // 2

    def part_of(n):
        return (n // QUAD) * (1 - 2 * first_level()) + first_level(), n % QUAD

    def channel(n):
        level, c = part_of(n)
        return level * QUAD + c

    def along(n):
        return send(
            feats_ref.at[pl.ds(0, SENT), block(channel(n), WIDE)], feature_rows(2, channel(n)), feat_send.at[1, n],
            feat_recv.at[1, n], xdev,
        )

    def onward(n):
        return send(
            feature_rows(2, channel(n)), feature_rows(3, channel(n)), feat_send.at[2, n], feat_recv.at[2, n], core
        )

    greet(half, f, z, y, xx)
    for c in own_copies:
        c.wait()
    keep = [
        pltpu.make_async_copy(branch_own.at[0], branch_out.at[f], local_sem.at[0]),
        pltpu.make_async_copy(merge_own.at[0], merge_out.at[f], local_sem.at[1]),
    ]

    def columns(kind):
        return pl.ds(0, CUT) if kind == 1 else pl.ds(CUT, COLS - CUT)

    def piece(kind, owner):
        return branch_out.at[owner] if kind == 0 else merge_out.at[owner, :, columns(kind)]

    def own_piece(kind, j):
        return branch_own.at[j] if kind == 0 else merge_own.at[j, :, columns(kind)]

    def column_of(k):
        return (xx + k % 2) % 2 + 2 * ((y + k // 2) % 2)

    def owner(i, k):
        return L[i] * QUAD + column_of(k)

    def passing(kind, i, k, s, r, dev):
        ref = piece(kind, owner(i, k))
        return send(own_piece(kind, 0) if i == 0 and k == 0 else ref, ref, s, r, dev)

    def beside(d):
        return (half, f + QUAD if d == 0 else f - QUAD)

    def x_copy(kind):
        return send(own_piece(kind, 1), piece(kind, f), x_send.at[kind], x_recv.at[kind], xdev)

    def x_arrive(kind):
        if kind not in KINDS:
            return
        ref = piece(kind, owner(0, 1))
        send(ref, ref, x_send.at[kind], x_recv.at[kind], xdev).wait_recv()

    def z_copy(kind, i, k, d):
        return passing(kind, i, k, z_send.at[kind, d, L[i], k], z_recv.at[kind, L[i], k], beside(d))

    def z_both(i, fn):
        @pl.when((L[i] <= z) & (z < LINE - 1))
        def _():
            fn(0)

        @pl.when((L[i] >= z) & (z > 0))
        def _():
            fn(1)

    def z_step(kind, i, ks):
        for k in ks:
            if i:
                z_copy(kind, i, k, 0).wait_recv()
            z_both(i, lambda d: z_copy(kind, i, k, d).start())
            if i and kind == 1:
                bring(1, i, k)

    def y_copy(kind, i, k):
        return passing(kind, i, k, y_send.at[kind, L[i], k], y_recv.at[kind, L[i], k], ydev)

    def spread(kind, i, ks):
        if kind not in KINDS:
            return
        for k in ks:
            y_copy(kind, i, k).start()

    def y_arrive(kind, i):
        if kind not in KINDS:
            return
        for k in (0, 1):
            ref = piece(kind, owner(i, k + 2))
            send(ref, ref, y_send.at[kind, L[i], k], y_recv.at[kind, L[i], k], ydev).wait_recv()
            if kind == 1:
                bring(1, i, k + 2)

    def near(kind, i, k):
        cols = columns(kind)
        return pltpu.make_async_copy(
            merge_out.at[owner(i, k), :, cols], wfeat.at[owner(i, k), :, cols], w_sem.at[kind - 1, i, k]
        )

    def bring(kind, i, k):
        if kind not in KINDS:
            return

        @pl.when(L[i] < 2)
        def _():
            near(kind, i, k).start()

    def zb_copy(i, k, d):
        return passing(2, i, k, zb_send.at[d, L[i], k], zb_recv.at[L[i], k], beside(d))

    def zb_step(i):
        if 2 not in KINDS:
            return
        for k in range(QUAD):
            if i:
                zb_copy(i, k, 0).wait_recv()
            z_both(i, lambda d: zb_copy(i, k, d).start())
            if i:
                bring(2, i, k)

    def bounds():
        shape = (8, NB)
        bin_ = lax.broadcasted_iota(jnp.int32, shape, 1)
        what = lax.broadcasted_iota(jnp.int32, shape, 0)
        by_row = what < 4
        ceil = jnp.bitwise_and(what, 3) > 0
        result = jnp.zeros(shape, jnp.int32)
        for (start, size, room), bins in zip(SPANS, BIN_COUNTS):
            at = bin_ - start
            image = lax.shift_right_logical(at * -(-65536 // (bins * bins)), 16)
            rest = at - image * (bins * bins)
            down = lax.shift_right_logical(rest * -(-65536 // bins), 16)
            index = jnp.where(by_row, down, rest - down * bins) + jnp.bitwise_and(what, 1)
            base = jnp.zeros(shape, jnp.int32)
            extent = jnp.zeros(shape, jnp.int32)
            for k in range(IMG):
                base = jnp.where(image == k, jnp.where(by_row, box_ref[k, 0], box_ref[k, 1]), base)
                extent = jnp.where(image == k, jnp.where(by_row, box_ref[k, 2], box_ref[k, 3]), extent)
            value = index * extent + jnp.where(ceil, bins - 1, 0)
            value = base + lax.shift_right_logical(value * -(-65536 // bins), 16)
            result = jnp.where((at >= 0) & (at < size), value, result)
        t2[0] = result

    def maps(c):
        def down(n, _):
            p = lax.broadcasted_iota(jnp.int32, (LANES, NB), 0) + n * LANES
            row, col = lax.shift_right_logical(p, 5), jnp.bitwise_and(p, 31)
            cell = lambda k: t2[c, k : k + 1, :]
            for k in (0, 2):
                hit = (row >= cell(k)) & (row < cell(k + 1)) & (col >= cell(k + 4)) & (col < cell(k + 5))
                value = jnp.where(hit, 1.0, 0.0)
                if k == 0:
                    pt[c, block(n, LANES), :] = value.astype(BF)
                    pm[c, :, block(n, LANES)] = value.T.astype(BF)
                else:
                    ut[c, pl.ds(pl.multiple_of(32 + n * LANES, 32), LANES), :] = value.astype(BF)
                    um[c, :, block(n, LANES)] = value.T.astype(BF)
            return 0

        lax.fori_loop(0, PIX // LANES, down, 0)
        ut[c, 0:32, :] = jnp.zeros((32, NB), BF)
        ut[c, 32 + PIX : 64 + PIX, :] = jnp.zeros((32, NB), BF)
        total = jnp.sum(pm[c].astype(F32), axis=1, keepdims=True)
        cnt[c * NB : (c + 1) * NB, :] = jnp.broadcast_to(jnp.maximum(total, 1.0), (NB, LANES))

    def inside(c, start, size):
        value = ut[c, pl.ds(start, size), 0:LANES].astype(F32)
        first = lax.broadcasted_iota(jnp.int32, (size, LANES), 1) < IMG
        return jnp.sum(jnp.where(first, value, 0.0), axis=1, keepdims=True)

    def mask_pool(c, cols):
        def mask(n, _):
            at = pl.ds(pl.multiple_of(base(c) + n * 64, 32), 64)
            w = inside(c, pl.multiple_of(32 + n * 64, 32), 64)
            x[at, cols] = (x[at, cols].astype(F32) * w).astype(BF)
            return 0

        lax.fori_loop(0, PIX // 64, mask, 0)
        total = mm(pm[c], x[pl.ds(base(c), PIX), cols])
        pooled[c * NB : (c + 1) * NB, cols] = (total / cnt[c * NB : (c + 1) * NB, 0:1]).astype(BF)

    def own_mask_pool(c):
        def part(n, _):
            mask_pool(c, block(n, 512))
            return 0

        lax.fori_loop(0, CIN // 512, part, 0)

    def feature_step(n):
        along(n).wait_recv()
        onward(n).start()
        if n < 6:
            along(n + 2).start()

    def feature_done(n):
        onward(n).wait()
        for c in (2, 3):
            mask_pool(c, block(channel(n), WIDE))

    def act_copies(pair):
        rows = pl.ds(pair * 2 * NB, 2 * NB)
        return [
            send(act_own.at[rows], act_in.at[j, rows], act_send.at[pair, j], act_recv.at[pair, j], dev)
            for j, dev in enumerate((core, xdev, diag))
        ]

    def branches(pair):
        if pair == 0:
            load = pltpu.make_async_copy(branch_out, bfull, local_sem.at[2])
            load.start()
            load.wait()
        rows = pl.ds(pair * 2 * NB, 2 * NB)
        for b, (_, size, _) in enumerate(SPANS):
            weight = bfull[:, :, b * QUART : (b + 1) * QUART].reshape(CIN, QUART)
            here = span_mask((2 * NB, QUART), b)
            value = jnp.where(here, mm(pooled[rows, :], weight), 0.0)
            entries = 2.0 * size
            mean = jnp.sum(value, axis=0, keepdims=True) / entries
            spread_ = jnp.sum(value * value, axis=0, keepdims=True) / entries - mean * mean
            inverse = lax.rsqrt(spread_ + EPSILON)
            centred = (value - mean) * inverse
            normed = centred * gain_ref[b : b + 1, pl.ds(quarter, QUART)].astype(F32) + bias_ref[
                b : b + 1, pl.ds(quarter, QUART)
            ].astype(F32)
            active = normed * jax.nn.sigmoid(normed)
            inv[pair * 4 + b : pair * 4 + b + 1, :] = inverse
            if b == 0:
                xhat[rows, :] = jnp.where(here, centred, 0.0)
                act_own[rows, :] = jnp.where(here, active, 0.0).astype(BF)
            else:
                xhat[rows, :] = jnp.where(here, centred, xhat[rows, :])
                act_own[rows, :] = jnp.where(here, active, act_own[rows, :].astype(F32)).astype(BF)
        for c in act_copies(pair):
            c.start()
        act[rows, pl.ds(quarter, QUART)] = act_own[rows, :]

    def act_arrive(sent_pair):
        copies = act_copies(sent_pair)
        for j in range(3):
            copies[j].wait_recv()
            cols = pl.multiple_of(
                ((1 - half) if j != 1 else half) * WIDE + ((1 - xx) if j else xx) * QUART, QUART
            )
            for c in (2 * sent_pair, 2 * sent_pair + 1):
                mine = c ^ (j + 1)
                act[mine * NB : (mine + 1) * NB, pl.ds(cols, QUART)] = act_in[j, c * NB : (c + 1) * NB, :]

    def contract(kind, owners, count, pair, wanted, pending):
        @pl.when(wanted)
        def _():
            def unit(m, _):
                n = m // 2
                o = owners(n)
                canvas = 2 * pair + m % 2
                if pending is not None:

                    @pl.when(m % 2 == 0)
                    def _():
                        near(kind, pending[0], pending[1] + n).wait()

                lanes = block(o, WIDE)
                rows = block(canvas, PIX)
                shifted = lambda dr: x[pl.ds(pl.multiple_of(canvas * PIX + 32 * (pair + dr), 32), PIX), lanes]
                if kind == 1:
                    two = mm(shifted(0), wfeat[o, :, 0:STRIP]) + mm(shifted(1), wfeat[o, :, STRIP : 2 * STRIP])
                    three = mm(shifted(2), wfeat[o, :, 2 * STRIP : CUT])
                    if TAIL == STRIP:
                        acc[rows, :] = acc[rows, :] + (two + three)
                    else:
                        acc[rows, :] = acc[rows, :] + two
                        acc[rows, 0:TAIL] = acc[rows, 0:TAIL] + three
                else:
                    acc[rows, TAIL:STRIP] = acc[rows, TAIL:STRIP] + mm(shifted(2), wfeat[o, :, CUT:])
                return 0

            lax.fori_loop(0, 2 * count, unit, 0)

    def features_of(kind, i, pair, first=0, count=4):
        if kind not in KINDS:
            return
        pending = None if pair else (i, first)
        contract(kind, lambda n: owner(i, first + n), count, pair, L[i] < 2, pending)

    def arrived(n):
        contract(1, lambda _: channel(n), 1, 1, z < 2, None)

    def raise_bins():
        load = lambda b: pltpu.make_async_copy(
            merge_out.at[pl.ds(8 + 2 * b, 2)], wbuf.at[pl.ds(2 * (b % 2), 2)], raise_sem.at[b % 2]
        )
        load(0).start()
        load(1).start()
        for b, (start, _, room) in enumerate(SPANS):
            load(b).wait()
            lhs = jnp.concatenate([act[c * NB + start : c * NB + start + room, :] for c in range(CANV)], axis=0)
            value = mm(lhs, wbuf[2 * (b % 2) : 2 * (b % 2) + 2].reshape(MID, COLS)).astype(BF)
            for c in range(CANV):
                awb[c * NB + start : c * NB + start + room, :] = value[c * room : (c + 1) * room]
            if b < 2:
                load(b + 2).start()
        for c in range(CANV):
            awb[c * NB + 224 : (c + 1) * NB, :] = jnp.zeros((NB - 224, COLS), BF)

    def clear():
        x[0:32, :] = jnp.zeros((32, CIN), BF)
        for start in (base(2) - 32, base(2) + SENT, base(3) + SENT, base(3) + PIX):
            x[start : start + 32, :] = jnp.zeros((32, CIN), BF)

        def clear_acc(n, _):
            acc[block(n, LANES), :] = jnp.zeros((LANES, STRIP), F32)
            return 0

        lax.fori_loop(0, ROWS // LANES, clear_acc, 0)

    for kind in KINDS:
        x_copy(kind).start()
    z_step(0, 0, (0,))
    spread(0, 0, (0,))
    spread(2, 0, (0,))
    for c in keep:
        c.start()
    whole.start()
    bounds()
    for n in (0, 1):
        for c in tables(n):
            c.start()
    x_arrive(0)
    z_step(0, 0, (1,))
    spread(0, 0, (1,))
    z_step(0, 1, (0, 1))
    spread(0, 1, (0, 1))
    z_step(1, 0, (0,))
    maps(0)
    z_step(0, 2, (0, 1))
    spread(0, 2, (0, 1))
    z_step(0, 3, (0, 1))
    spread(0, 3, (0, 1))
    spread(1, 0, (0,))
    x_arrive(1)
    z_step(1, 0, (1,))
    spread(1, 0, (1,))
    x_arrive(2)
    spread(2, 0, (1,))
    along(0).start()
    along(1).start()
    for c in own_loads:
        c.wait()
    own_mask_pool(0)
    for n in (0, 1):
        for c in tables(n):
            c.wait_recv()
    maps(1)
    z_step(1, 1, (0,))
    spread(1, 1, (0,))
    feature_step(0)
    whole.wait_recv()
    own_mask_pool(1)
    z_step(1, 1, (1,))
    spread(1, 1, (1,))
    y_arrive(2, 0)
    zb_step(0)
    feature_step(1)
    clear()
    x_save = [
        pltpu.make_async_copy(x.at[pl.ds(base(2 * p), 2 * PIX)], x_out.at[pl.ds(p * 2 * PIX, 2 * PIX)], out_sem.at[p])
        for p in (0, 1)
    ]
    x_save[0].start()
    for c in keep:
        c.wait()
    for k in (0, 1):
        bring(1, 0, k)
    for k in range(QUAD):
        bring(2, 0, k)
    z_step(1, 2, (0,))
    spread(1, 2, (0,))
    for i in range(LINE):
        y_arrive(0, i)
    branches(0)
    feature_step(2)
    z_step(1, 2, (1,))
    spread(1, 2, (1,))
    y_arrive(1, 0)
    features_of(1, 0, 0)
    feature_step(3)
    maps(2)
    z_step(1, 3, (0,))
    spread(1, 3, (0,))
    maps(3)
    feature_done(0)
    feature_done(1)
    y_arrive(1, 1)
    feature_step(4)
    feature_done(2)
    feature_done(3)
    z_step(1, 3, (1,))
    spread(1, 3, (1,))
    features_of(1, 0, 1)
    features_of(1, 3, 0, 0, 2)
    features_of(1, 1, 0)
    feature_step(5)
    feature_done(4)
    arrived(4)
    zb_step(1)
    features_of(2, 0, 0)
    y_arrive(1, 2)
    features_of(1, 2, 0)
    feature_step(6)
    features_of(1, 2, 1)
    features_of(2, 0, 1)
    feature_done(5)
    arrived(5)
    zb_step(2)
    features_of(2, 2, 0)
    feature_done(6)
    arrived(6)
    features_of(2, 2, 1)
    feature_step(7)
    features_of(2, 1, 0)
    feature_done(7)
    branches(1)
    x_save[1].start()
    act_arrive(0)
    arrived(7)
    features_of(1, 3, 1, 0, 2)
    features_of(2, 1, 1)
    zb_step(3)
    features_of(2, 3, 0)
    features_of(2, 3, 1)
    act_arrive(1)

    @pl.when(z >= 2)
    def _():
        raise_bins()

    y_arrive(1, 3)
    features_of(1, 3, 0, 2, 2)
    features_of(1, 3, 1, 2, 2)

    @pl.when(z < 2)
    def _():
        raise_bins()

    none = lambda: jnp.zeros((1, QUART), F32)
    gain = gain_ref[4:5, pl.ds(quarter, QUART)].astype(F32)
    bias = bias_ref[4:5, pl.ds(quarter, QUART)].astype(F32)
    weight = class_ref[:, pl.ds(quarter, QUART)]
    sums = []
    sum_c = jnp.zeros((CLS, QUART), F32)
    for pair in (0, 1):
        s1, s2, n2 = none(), none(), jnp.zeros((1, 1), F32)
        for c in (2 * pair, 2 * pair + 1):
            rows = pl.ds(c * PIX, PIX)
            for dr in range(3):
                acc[rows, :] = acc[rows, :] + mm(
                    ut[c, 32 * dr : 32 * dr + PIX, :], awb[c * NB : (c + 1) * NB, dr * STRIP : (dr + 1) * STRIP]
                )
            value = (
                pltpu.roll(acc[rows, 0:QUART], 1, 0)
                + acc[rows, QUART : 2 * QUART]
                + pltpu.roll(acc[rows, 2 * QUART : STRIP], PIX - 1, 0)
            )
            cv[rows, :] = value
            w = inside(c, 32, PIX)
            kept = value * w
            s1 = s1 + jnp.sum(kept, axis=0, keepdims=True)
            s2 = s2 + jnp.sum(kept * value, axis=0, keepdims=True)
            n2 = n2 + jnp.sum(w, axis=0, keepdims=True)
        mean = s1 / n2
        inverse = lax.rsqrt(s2 / n2 - mean * mean + EPSILON)

        def slopes(n, carry):
            sum_b, sum_g, total = carry
            c = 2 * pair + n // 4
            at = pl.ds(pl.multiple_of(c * PIX + (n % 4) * 256, 256), 256)
            w = inside(c, pl.multiple_of(32 + (n % 4) * 256, 32), 256)
            centred = (cv[at, :] - mean) * inverse
            normed = centred * gain + bias
            sigma = jax.nn.sigmoid(normed)
            hidden = (normed * sigma * w).astype(BF)
            pixels = block(n % 4, 256)
            stage[c, :, pixels] = mm(weight, hidden, ((1,), (1,)))
            grad = g[c, :, pixels]
            total = total + mm(grad, hidden)
            slope = mm(grad, weight, ((0,), (0,))) * (w * (sigma * (1.0 + normed * (1.0 - sigma))))
            dy[at, :] = slope
            cv[at, :] = centred
            return (
                sum_b + jnp.sum(slope, axis=0, keepdims=True),
                sum_g + jnp.sum(slope * centred, axis=0, keepdims=True),
                total,
            )

        sum_b, sum_g, sum_c = lax.fori_loop(0, 8, slopes, (none(), none(), sum_c))
        sums.append((sum_b, sum_g, inverse, n2))
    logit_sends = [
        send(
            stage.at[j + 1], logit_far.at[j], logit_send.at[j], logit_recv.at[j], dev
        )
        for j, dev in enumerate((core, xdev, diag))
    ]
    for c in logit_sends:
        c.start()
    logit_keep = pltpu.make_async_copy(stage.at[0], logit_own, out_sem.at[2])
    logit_keep.start()
    small[...] = jnp.zeros((SMALL, WIDE), F32)
    here = pl.ds(pl.multiple_of(xx * QUART, QUART), QUART)
    small[0:CLS, here] = sum_c
    small[24:25, here] = sums[0][1] + sums[1][1]
    small[25:26, here] = sums[0][0] + sums[1][0]
    d3[0:32, :] = jnp.zeros((32, STRIP), BF)
    d3[32 + ROWS : 64 + ROWS, :] = jnp.zeros((32, STRIP), BF)
    for c in range(CANV):
        sum_b, sum_g, inverse, n2 = sums[c // 2]
        rows = pl.ds(c * PIX, PIX)
        value = (inside(c, 32, PIX) * (gain * inverse)) * (dy[rows, :] - (sum_b + cv[rows, :] * sum_g) / n2)
        to = pl.ds(32 + c * PIX, PIX)
        d3[to, 0:QUART] = pltpu.roll(value, PIX - 1, 0).astype(BF)
        d3[to, QUART : 2 * QUART] = value.astype(BF)
        d3[to, 2 * QUART : STRIP] = pltpu.roll(value, 1, 0).astype(BF)
    d3_save = pltpu.make_async_copy(d3, d3_out, out_sem.at[3])
    d3_save.start()
    for c in range(CANV):
        for dr in range(3):
            awb[c * NB : (c + 1) * NB, dr * STRIP : (dr + 1) * STRIP] = mm(
                um[c], d3[pl.ds(32 * (2 - dr) + c * PIX, PIX), :]
            ).astype(BF)
    saves = [
        pltpu.make_async_copy(a, b, out_sem.at[4 + n])
        for n, (a, b) in enumerate(
            (
                (awb, ud_out), (act, act_out), (pooled, pooled_out), (xhat, xhat_out), (inv, inv_out), (pt, pt_out),
                (cnt, count_out), (small, small_out),
            )
        )
    ]
    for c in saves:
        c.start()

    for i in range(LINE):
        for k in (0, 1):
            for kind in (0, 1):
                z_both(i, lambda d: z_copy(kind, i, k, d).wait_send())
                y_copy(kind, i, k).wait_send()
            if i == 0 and 2 in KINDS:
                y_copy(2, i, k).wait_send()
        for k in range(QUAD if 2 in KINDS else 0):
            z_both(i, lambda d: zb_copy(i, k, d).wait_send())
    for kind in KINDS:
        x_copy(kind).wait_send()
    for n in (0, 1):
        for c in tables(n):
            c.wait_send()
    whole.wait_send()
    for n in range(8):
        along(n).wait_send()
    for pair in (0, 1):
        for c in act_copies(pair):
            c.wait_send()
    for c in logit_sends:
        c.wait_send()
        c.wait_recv()
    logit_keep.wait()
    d3_save.wait()
    for c in x_save + saves:
        c.wait()


def forward_call(merge_w, branch_w, feats, g, boxes, class_w, gains, biases):
    D = pltpu.SemaphoreType.DMA
    V = lambda *s: pltpu.VMEM(s, BF)
    W = lambda *s: pltpu.VMEM(s, F32)
    I = lambda *s: pltpu.VMEM(s, jnp.int32)
    S = jax.ShapeDtypeStruct
    hbm = pl.BlockSpec(memory_space=pl.ANY)
    vmem = pl.BlockSpec(memory_space=pltpu.VMEM)
    outs = (
        S((16, 256, COLS), BF), S((16, 128, 4 * QUART), BF), S((ROWS, CIN), BF), S((ROWS + 64, STRIP), BF),
        S((BINS4, COLS), BF), S((BINS4, MID), BF), S((BINS4, CIN), BF), S((BINS4, QUART), F32), S((8, QUART), F32),
        S((CANV, PIX, NB), BF), S((BINS4, LANES), F32), S((CLS, PIX), F32), S((3, CLS, PIX), F32),
        S((SMALL, WIDE), F32),
    )
    return pl.pallas_call(
        forward_kernel,
        out_shape=outs,
        in_specs=[hbm] * 4 + [pl.BlockSpec(memory_space=pltpu.SMEM)] + [vmem] * 3,
        out_specs=(hbm,) * len(outs),
        scratch_shapes=[
            V(2, 128, 4 * QUART), V(2, 256, COLS), V(ROWS + 96, CIN), W(ROWS, STRIP), V(8, 256, COLS), V(QUAD, 256, COLS),
            V(16, 128, 4 * QUART), V(BINS4, COLS), V(CANV, NB, PIX), V(CANV, NB, PIX),
            V(CANV, PIX + 64, NB), V(CANV, PIX, NB), V(BINS4, CIN), V(BINS4, MID), V(BINS4, QUART), V(3, BINS4, QUART),
            W(BINS4, QUART), W(8, QUART), W(ROWS, QUART), W(ROWS, QUART), V(ROWS + 64, STRIP),
            W(BINS4, LANES), I(CANV, 8, NB), V(CANV, CLS, PIX), W(CANV, CLS, PIX), W(SMALL, WIDE),
            D((28,)), D((2, 2, 4, 2)), D((2, 4, 2)), D((3, 4, 2)), D((3, 4, 2)), D((3,)), D((3,)), D((2, 4, 4)), D((4, 4)),
            D((2, 3)), D((2, 3)), D((3, 8)), D((3, 8)), D((2, 3)), D((2, 3)), D((3,)), D((3,)), D((2, 4, 4)), D((12,)), D((2,)),
        ],
        compiler_params=pltpu.CompilerParams(collective_id=0, has_side_effects=True, vmem_limit_bytes=63 * 1024 * 1024),
        name="forward",
    )(merge_w, branch_w, feats, g, boxes, class_w, gains, biases)


def backward_kernel(
    x_hbm, d3_hbm, act_hbm, ud_hbm, w_hbm, branch_hbm, pooled_hbm, xhat_hbm, pt_hbm, cnt_hbm, small_hbm, inv_ref, gain_ref, bias_ref,
    merge_out, branch_out, feat_out, own_out, far_out, xfar_out, small_out,
    xt, act, d3, ud, g0, g1, g2, ys0, ys1, ys2, zs0, zs1, zs2, xs0, xs1, xs2, wbuf, own_stage, near_stage, mid_stage,
    far_sum, far_stage, mid, dact, dact_send, dact_in, pooled, dzw, xhat, pt, cnt, bgbuf, fin0, fin1, small, small_in,
    local_sem, x_sem, y_send, y_recv, z_send, z_recv, zb_send, zb_recv, end_send, end_recv, end_local, w_sem, own_sem,
    near_send, near_recv, mid_send, mid_recv, far_send, far_recv, act_send, act_recv, bg_sem, pool_sem, sum_send, sum_recv,
    last_send, last_recv, fin_sem,
):
    half, f, z, y, xx = place()
    L = [turn(z, i) for i in range(LINE)]
    core, xdev, diag = friends(half, f, xx)
    ydev = (half, f + 2 - 4 * y)
    quarter = pl.multiple_of(half * WIDE + xx * QUART, QUART)
    here = pl.ds(pl.multiple_of(xx * QUART, QUART), QUART)
    loads = [
        pltpu.make_async_copy(a, b, local_sem.at[n])
        for n, (a, b) in enumerate(
            (
                (d3_hbm, d3), (ud_hbm, ud), (act_hbm, act), (pt_hbm, pt), (cnt_hbm, cnt), (xhat_hbm, xhat),
                (small_hbm, small.at[0, pl.ds(0, SMALL)]),
            )
        )
    ]
    for c in loads:
        c.start()

    def send(src, dst, s, r, dev):
        return pltpu.make_async_remote_copy(
            src_ref=src, dst_ref=dst, send_sem=s, recv_sem=r, device_id=dev, device_id_type=MESH
        )

    def column_of(k):
        return (xx + k % 2) % 2 + 2 * ((y + k // 2) % 2)

    def owner(i, k):
        return L[i] * QUAD + column_of(k)

    ORDER = (2, 3, 0, 1)

    def x_load(i, j):
        return pltpu.make_async_copy(x_hbm.at[:, block(owner(i, ORDER[j]), WIDE)], xt.at[j % 2], x_sem.at[j % 2])

    def rows_start(i):
        @pl.when(L[i] < 2)
        def _():
            for j in (0, 1):
                x_load(i, j).start()

    rows_start(3)
    grads, yslot, zslot, xslot = (g0, g1, g2), (ys0, ys1, ys2), (zs0, zs1, zs2), (xs0, xs1, xs2)

    def add_into(dst, other):
        def rows16(n, _):
            at = block(n, 16)
            dst[at, :] = (dst[at, :].astype(F32) + other[at, :].astype(F32)).astype(BF)
            return 0

        lax.fori_loop(0, dst.shape[0] // 16, rows16, 0)

    def y_copy(kind, i, s):
        n = L[i] if kind < 2 else 0
        return send(
            grads[kind].at[owner(i, 2 + s)], yslot[kind].at[n, s], y_send.at[kind, L[i], s], y_recv.at[kind, L[i], s], ydev
        )

    def fold(kind, i):
        for s in (0, 1):
            y_copy(kind, i, s).wait_recv()
            add_into(grads[kind].at[owner(i, s)], yslot[kind].at[L[i] if kind < 2 else 0, s])

    def z_src(kind, i, c):
        if kind < 2:
            return grads[kind].at[pl.ds(L[i] * QUAD + 2 * y, 2)]
        return g2.at[L[i] * QUAD + c]

    def z_dst(kind, n, c):
        return zslot[kind].at[n] if kind < 2 else zs2.at[n, c]

    def z_sems(kind, level, n, c):
        if kind < 2:
            return z_send.at[kind, level], z_recv.at[kind, n]
        return zb_send.at[level, c], zb_recv.at[n, c]

    def z_copy(kind, i, c, up):
        level = L[i]
        n = level if up else level + (LINE - level) * (1 - jnp.minimum(z - 1 - level, 1))
        s, r = z_sems(kind, level, n, c)
        return send(z_src(kind, i, c), z_dst(kind, n, c), s, r, (half, f + QUAD if up else f - QUAD))

    def z_take(kind, i, n, c):
        s, r = z_sems(kind, L[i], n, c)
        send(z_src(kind, i, c), z_dst(kind, n, c), s, r, core).wait_recv()
        if kind < 2:
            for s in (0, 1):
                add_into(z_src(kind, i, c).at[s], z_dst(kind, n, c).at[s])
        else:
            add_into(z_src(kind, i, c), z_dst(kind, n, c))

    def early(kind, i, c=None):
        @pl.when((L[i] > z) & (z == 0))
        def _():
            z_copy(kind, i, c, True).start()

        @pl.when((L[i] < z) & (z == LINE - 1))
        def _():
            z_copy(kind, i, c, False).start()

    def late(kind, i, c=None):
        @pl.when((L[i] > z) & (z > 0))
        def _():
            z_take(kind, i, L[i], c)
            z_copy(kind, i, c, True).start()

        @pl.when((L[i] < z) & (z < LINE - 1))
        def _():
            z_take(kind, i, L[i], c)
            z_copy(kind, i, c, False).start()

    def home(kind, c=None):
        @pl.when(z > 0)
        def _():
            z_take(kind, 0, z, c)

        @pl.when(z < LINE - 1)
        def _():
            z_take(kind, 0, LINE, c)

    def line_sent(kind, i, c=None):
        @pl.when(L[i] > z)
        def _():
            z_copy(kind, i, c, True).wait_send()

        @pl.when(L[i] < z)
        def _():
            z_copy(kind, i, c, False).wait_send()

    def early_b(i):
        for c in range(QUAD):
            early(2, i, c)

    def late_b(i):
        for c in range(QUAD):
            late(2, i, c)

    def produce(i):
        for j, k in enumerate(ORDER):

            def store(dr, value):
                if dr < 2:
                    g1[owner(i, k), :, dr * STRIP : (dr + 1) * STRIP] = value.astype(BF)
                else:
                    g1[owner(i, k), :, 2 * STRIP : CUT] = value[:, 0:QUART].astype(BF)
                    g2[owner(i, k)] = value[:, QUART:].astype(BF)

            @pl.when(L[i] < 2)
            def _():
                x_load(i, j).wait()
                for dr in range(3):
                    store(dr, mm(xt[j % 2], d3[pl.ds(32 * (2 - dr), ROWS), :], ((0,), (0,))))
                if j < 2:
                    x_load(i, j + 2).start()

            @pl.when(L[i] >= 2)
            def _():
                c = column_of(k)
                mine = span_mask((BINS4, WIDE), 2 * (L[i] - 2) + c // 2)
                lhs = jnp.where(mine, act[:, block(c % 2, WIDE)].astype(F32), 0.0).astype(BF)
                for dr in range(3):
                    store(dr, mm(lhs, ud[:, dr * STRIP : (dr + 1) * STRIP], ((0,), (0,))))

            if k >= 2:
                y_copy(1, i, k - 2).start()
        if i:
            rows_start(i - 1)

    def w_load(n):
        return pltpu.make_async_copy(w_hbm.at[n], wbuf.at[n % 2], w_sem.at[n % 2])

    def spans(b, canvases):
        start, _, room = SPANS[b]
        return [pl.ds(c * NB + start, room) for c in canvases]

    def dact_copies():
        return [send(dact_send.at[j], dact_in.at[j], act_send.at[j], act_recv.at[j], dev) for j, dev in enumerate((core, xdev, diag))]

    def bin_gradients():
        for n in range(8):
            w_load(8 + n).wait()
            if n < 7:
                w_load(9 + n).start()
            b, h = n // 2, n % 2
            room = SPANS[b][2]
            lhs = jnp.concatenate([ud[s, :] for s in spans(b, range(CANV))], axis=0)
            value = mm(lhs, wbuf[n % 2], ((1,), (1,)))
            for c, s in enumerate(spans(b, range(CANV))):
                for xq in (0, 1):
                    dact[h, xq, s, :] = value[c * room : (c + 1) * room, xq * QUART : (xq + 1) * QUART]
        w_load(0).start()
        for j, (h, xq) in enumerate(((1 - half, xx), (half, 1 - xx), (1 - half, 1 - xx))):
            dact_send[j] = dact[h, xq].astype(BF)
        for c in dact_copies():
            c.start()

    def branch_gradients():
        for c in dact_copies():
            c.wait_recv()
        dzw[...] = jnp.zeros((BINS4, MID), BF)
        for b, (start, size, room) in enumerate(SPANS):
            gain = gain_ref[b : b + 1, pl.ds(quarter, QUART)].astype(F32)
            bias = bias_ref[b : b + 1, pl.ds(quarter, QUART)].astype(F32)
            all_g, all_b = jnp.zeros((1, QUART), F32), jnp.zeros((1, QUART), F32)
            for pair in (0, 1):
                both_c, both_d = [], []
                for c in (2 * pair, 2 * pair + 1):
                    centred = xhat[c * NB + start : c * NB + start + room, :]
                    grad = dact[half, xx, c * NB + start : c * NB + start + room, :]
                    for j in range(3):
                        theirs = (c ^ (j + 1)) * NB + start
                        grad = grad + dact_in[j, theirs : theirs + room, :].astype(F32)
                    normed = centred * gain + bias
                    sigma = jax.nn.sigmoid(normed)
                    both_c.append(centred)
                    both_d.append(grad * (sigma * (1.0 + normed * (1.0 - sigma))))
                sum_b = sum(jnp.sum(d, axis=0, keepdims=True) for d in both_d)
                sum_g = sum(jnp.sum(d * e, axis=0, keepdims=True) for d, e in zip(both_d, both_c))
                all_b, all_g = all_b + sum_b, all_g + sum_g
                for n in (0, 1):
                    value = (gain * inv_ref[pair * 4 + b : pair * 4 + b + 1, :]) * (
                        both_d[n] - (sum_b + both_c[n] * sum_g) / (2.0 * size)
                    )
                    at = (2 * pair + n) * NB + start
                    dzw[at : at + room, b * QUART : (b + 1) * QUART] = value.astype(BF)
            small[0, 26 + b : 27 + b, here] = all_g
            small[0, 30 + b : 31 + b, here] = all_b

    def pool_load(i):
        return pltpu.make_async_copy(pooled_hbm.at[:, block(L[i], 512)], pooled, pool_sem.at[0])

    def produce_branch(i):
        pool_load(i).wait()
        g0[pl.ds(L[i] * QUAD, QUAD)] = mm(pooled[...], dzw[...], ((0,), (0,))).astype(BF).reshape(QUAD, 128, MID)
        for s in (0, 1):
            y_copy(0, i, s).start()
        if i:
            pool_load(i - 1).start()

    def cols(n):
        return block(n, WIDE)

    def own_copy(n):
        return pltpu.make_async_copy(own_stage.at[n % 2], own_out.at[:, cols(n)], own_sem.at[n % 2])

    def near_copy(n):
        return send(near_stage.at[n % 2], far_out.at[pl.ds(0, SENT), cols(n)], near_send.at[n % 2], near_recv.at[n], core)

    def mid_copy(n):
        return send(mid_stage.at[n % 2], mid.at[n], mid_send.at[n % 2], mid_recv.at[n], core)

    def far_copy(n):
        return send(far_stage.at[n % 2], xfar_out.at[pl.ds(0, SENT), cols(n)], far_send.at[n % 2], far_recv.at[n], xdev)

    def bg_load(n):
        return pltpu.make_async_copy(branch_hbm.at[pl.ds(n * 2, 2)], bgbuf.at[n % 2], bg_sem.at[n % 2])

    def relay(n):
        mid_copy(n).wait_recv()

        @pl.when(n >= 2)
        def _():
            far_copy(n - 2).wait_send()

        def rows32(r, _):
            at = block(r, 32)
            far_stage[n % 2, at, :] = (far_sum[n % 2, at, :] + mid[n, at, :].astype(F32)).astype(BF)
            return 0

        lax.fori_loop(0, SENT // 32, rows32, 0)
        far_copy(n).start()

    def jobs(first, last):
        def job(n, _):
            w_load(n).wait()
            bg_load(n).wait()

            @pl.when(n < 7)
            def _():
                w_load(n + 1).start()
                bg_load(n + 1).start()

            @pl.when(n >= 2)
            def _():
                own_copy(n - 2).wait()
                near_copy(n - 2).wait_send()
                mid_copy(n - 2).wait_send()

            bins = (mm(dzw[...], bgbuf[n % 2].reshape(WIDE, MID), ((1,), (1,))) / cnt[:, 0:1]).astype(BF)
            for canvas in (3, 2, 1, 0):
                value = mm(pt[canvas], bins[canvas * NB : (canvas + 1) * NB])
                for dr in range(3):
                    value = value + mm(
                        d3[pl.ds(32 * (2 - dr) + canvas * PIX, PIX), :], wbuf[n % 2, :, dr * STRIP : (dr + 1) * STRIP],
                        ((1,), (1,)),
                    )
                first_bins = lax.broadcasted_iota(jnp.int32, (PIX, LANES), 1) < IMG
                inside = jnp.sum(
                    jnp.where(first_bins, pt[canvas, :, 0:LANES].astype(F32), 0.0), axis=1, keepdims=True
                )
                value = value * inside
                if canvas == 3:
                    mid_stage[n % 2] = value[0:SENT].astype(BF)
                    mid_copy(n).start()
                elif canvas == 2:
                    far_sum[n % 2] = value[0:SENT]
                elif canvas == 1:
                    near_stage[n % 2] = value[0:SENT].astype(BF)
                    near_copy(n).start()
                else:
                    own_stage[n % 2] = value
                    own_copy(n).start()

            @pl.when(n >= 1)
            def _():
                relay(n - 1)

            return 0

        lax.fori_loop(first, last, job, 0)

    def sums():
        for n in (6, 7):
            own_copy(n).wait()
            near_copy(n).wait_send()
            mid_copy(n).wait_send()
            far_copy(n).wait_send()
        take = lambda n: [
            pltpu.make_async_copy(own_out.at[:, cols(n)], own_stage.at[n % 2], fin_sem.at[0, n % 2]),
            pltpu.make_async_copy(far_out.at[pl.ds(0, SENT), cols(n)], near_stage.at[n % 2], fin_sem.at[1, n % 2]),
            pltpu.make_async_copy(xfar_out.at[pl.ds(0, SENT), cols(n)], mid_stage.at[n % 2], fin_sem.at[2, n % 2]),
        ]

        def give_(n):
            return pltpu.make_async_copy(fin_sum.at[n % 2], feat_out.at[:, cols(n)], fin_sem.at[3, n % 2])

        fin_sum = xt.at[:, pl.ds(0, PIX)]

        def arrive(n):
            near_copy(n).wait_recv()
            far_copy(n).wait_recv()
            for c in take(n):
                c.start()

        arrive(0)

        def step(n, _):
            @pl.when(n < 7)
            def _():
                arrive(n + 1)

            for c in take(n):
                c.wait()

            @pl.when(n >= 2)
            def _():
                give_(n - 2).wait()

            total = own_stage[n % 2, 0:SENT, :] + near_stage[n % 2].astype(F32) + mid_stage[n % 2].astype(F32)
            xt[n % 2, 0:SENT, :] = total.astype(BF)
            xt[n % 2, SENT:PIX, :] = jnp.zeros((PIX - SENT, WIDE), BF)
            give_(n).start()
            return 0

        lax.fori_loop(0, 8, step, 0)
        for n in (6, 7):
            give_(n).wait()

    def sum_copy(n):
        zz = z + 1 - 2 * (z % 2) if n == 2 else z + 2 - 4 * (z // 2)
        to = (f + 1 - 2 * xx, f + 2 - 4 * y, f + (zz - z) * QUAD, f + (zz - z) * QUAD)[n]
        return send(small.at[n], small_in.at[n], sum_send.at[n], sum_recv.at[n], (half, to))

    def sum_take(n):
        sum_copy(n).wait_recv()
        small[n + 1] = small[n] + small_in[n]
        if n < 3:
            sum_copy(n + 1).start()

    pool_load(3).start()
    w_load(8).start()
    bg_load(0).start()
    greet(half, f, z, y, xx, True)
    for c in loads:
        c.wait()
    small[0, 32:40, :] = jnp.zeros((8, WIDE), F32)
    bin_gradients()
    produce(3)
    early_b(3)
    branch_gradients()
    sum_copy(0).start()
    jobs(0, 2)
    produce_branch(3)
    produce(2)
    early_b(2)
    fold(1, 3)
    early(1, 3)
    jobs(2, 3)
    fold(0, 3)
    early(0, 3)
    late_b(3)
    produce_branch(2)
    sum_take(0)
    jobs(3, 4)
    fold(1, 2)
    early(1, 2)
    late(1, 3)
    produce(1)
    early_b(1)
    late_b(2)
    produce_branch(1)
    fold(0, 2)
    early(0, 2)
    late(0, 3)
    jobs(4, 6)
    sum_take(1)
    late(1, 2)
    produce(0)
    produce_branch(0)
    fold(1, 1)
    early(1, 1)
    fold(0, 1)
    early(0, 1)
    late_b(1)
    late(0, 2)
    jobs(6, 8)
    relay(7)
    sum_take(2)
    for c in range(QUAD):
        home(2, c)
    for s in (0, 1):
        y_copy(2, 0, s).start()
    late(1, 1)
    late(0, 1)
    fold(1, 0)
    fold(0, 0)
    fold(2, 0)
    sum_take(3)

    def last(kind):
        return send(grads[kind].at[f + 1 - 2 * xx], xslot[kind], last_send.at[kind], last_recv.at[kind], xdev)

    last(2).start()
    home(0)
    last(0).start()
    home(1)
    last(1).start()
    sums()
    ends = []

    def give(src, into, n):
        c = send(src, into(half), end_send.at[n], end_recv.at[n], core)
        c.start()
        k = pltpu.make_async_copy(src, into(half), end_local.at[n])
        k.start()
        ends.append((c, k, send(src, into(1 - half), end_send.at[n], end_recv.at[n], core)))

    def columns(ref, t):
        return lambda h: ref.at[:, pl.ds(pl.multiple_of(t * MID + h * WIDE, WIDE), WIDE)]

    there = pl.ds(pl.multiple_of((1 - xx) * QUART, QUART), QUART)
    last(2).wait_recv()
    last(0).wait_recv()
    for t in range(4):
        at = slice(t * QUART, (t + 1) * QUART)
        fin0[t, :, here] = g0[f, :, at]
        fin0[t, :, there] = xs0[:, at]
        give(fin0.at[t], columns(branch_out, t), TAPS + t)
    for t in (7, 8):
        at = slice((t - 7) * QUART, (t - 6) * QUART)
        fin1[t, :, here] = g2[f, :, at]
        fin1[t, :, there] = xs2[:, at]
        give(fin1.at[t], columns(merge_out, t), t)
    give(small.at[4], lambda h: small_out.at[h], 13)
    last(1).wait_recv()
    for t in range(7):
        at = slice(t * QUART, (t + 1) * QUART)
        fin1[t, :, here] = g1[f, :, at]
        fin1[t, :, there] = xs1[:, at]
        give(fin1.at[t], columns(merge_out, t), t)

    for n in range(4):
        sum_copy(n).wait_send()
    for c in dact_copies():
        c.wait_send()
    for i in range(LINE):
        for s in (0, 1):
            y_copy(0, i, s).wait_send()
            y_copy(1, i, s).wait_send()
            if i == 0:
                y_copy(2, i, s).wait_send()
        if i:
            line_sent(0, i)
            line_sent(1, i)
            for c in range(QUAD):
                line_sent(2, i, c)
    for kind in (0, 1, 2):
        last(kind).wait_send()
    for c, k, back in ends:
        c.wait_send()
        k.wait()
        back.wait_recv()


def backward_call(x, d3, act, ud, w, branch, pooled, xhat, pt, cnt, small, inv, gains, biases):
    D = pltpu.SemaphoreType.DMA
    V = lambda *s: pltpu.VMEM(s, BF)
    W = lambda *s: pltpu.VMEM(s, F32)
    S = jax.ShapeDtypeStruct
    hbm = pl.BlockSpec(memory_space=pl.ANY)
    vmem = pl.BlockSpec(memory_space=pltpu.VMEM)
    outs = (
        S((256, TAPS * MID), BF), S((128, 4 * MID), BF), S((PIX, CIN), BF), S((PIX, CIN), F32), S((PIX, CIN), BF),
        S((PIX, CIN), BF), S((2, 40, WIDE), F32),
    )
    return pl.pallas_call(
        backward_kernel,
        out_shape=outs,
        in_specs=[hbm] * 11 + [vmem] * 3,
        out_specs=(hbm,) * len(outs),
        scratch_shapes=[
            V(2, ROWS, WIDE), V(BINS4, MID), V(ROWS + 64, STRIP), V(BINS4, COLS), V(16, 128, MID), V(16, 256, CUT),
            V(16, 256, WIDE), V(4, 2, 128, MID), V(4, 2, 256, CUT), V(1, 2, 256, WIDE), V(5, 2, 128, MID),
            V(5, 2, 256, CUT), V(5, 4, 256, WIDE), V(128, MID), V(256, CUT), V(256, WIDE), V(2, 256, COLS),
            W(2, PIX, WIDE), V(2, SENT, WIDE), V(2, SENT, WIDE), W(2, SENT, WIDE), V(2, SENT, WIDE), V(8, SENT, WIDE),
            W(2, 2, BINS4, QUART), V(3, BINS4, QUART), V(3, BINS4, QUART), V(BINS4, 512), V(BINS4, MID), W(BINS4, QUART),
            V(CANV, PIX, NB), W(BINS4, LANES), V(2, 2, 128, MID), V(4, 128, WIDE),
            V(TAPS, 256, WIDE), W(5, 40, WIDE), W(4, 40, WIDE),
            D((7,)), D((2,)), D((3, 4, 2)), D((3, 4, 2)), D((2, 4)), D((2, 5)), D((4, 4)), D((5, 4)), D((14,)), D((14,)),
            D((14,)), D((2,)), D((2,)), D((2,)), D((8,)), D((2,)), D((8,)), D((2,)), D((8,)), D((3,)), D((3,)), D((2,)),
            D((1,)), D((4,)), D((4,)), D((3,)), D((3,)), D((4, 2)),
        ],
        compiler_params=pltpu.CompilerParams(collective_id=1, has_side_effects=True, vmem_limit_bytes=63 * 1024 * 1024),
        name="backward",
    )(x, d3, act, ud, w, branch, pooled, xhat, pt, cnt, small, inv, gains, biases)


def paired(features, region_boxes, branch_w, merge_w, class_w, norm_gain, norm_bias, grad_logits):
    (
        merge_g, branch_g, masked, spread_grad, binned, active, pooled, centred, inverse, bounds, counts,
        logit_own, logit_far, small,
    ) = forward_call(
        merge_w, branch_w, features.reshape(PIX, CIN), grad_logits[0].T, region_boxes[0], class_w.T, norm_gain, norm_bias,
    )
    logits = (logit_own + (logit_far[0] + (logit_far[1] + logit_far[2]))).T[None]
    share_merge, share_branch, grad_features, _, _, _, sums = backward_call(
        masked, spread_grad, active, binned, merge_g, branch_g, pooled, centred, bounds, counts, small, inverse,
        norm_gain, norm_bias,
    )
    sums = jnp.transpose(sums, (1, 0, 2)).reshape(40, MID)
    return (
        logits,
        grad_features.astype(F32)[None],
        share_branch.astype(F32),
        share_merge.astype(F32),
        sums[:CLS].T,
        jnp.concatenate([sums[26:30], sums[24:25]], axis=0),
        jnp.concatenate([sums[30:34], sums[25:26]], axis=0),
    )


def solution(mesh):
    placed = (
        P(("bn", "fsdp"), None, None),
        P(("bn", "fsdp"), None, None),
        P("fsdp", None),
        P("fsdp", None),
        P(),
        P(),
        P(),
        P(("bn", "fsdp"), None, None),
    )
    run = paired if dict(mesh.shape) == {"bn": 2, "fsdp": LINE * QUAD} else body
    return jax.shard_map(
        run,
        mesh=mesh,
        in_specs=placed,
        out_specs=(
            P(("bn", "fsdp"), None, None),
            P(("bn", "fsdp"), None, None),
            P("fsdp", None),
            P("fsdp", None),
            P(),
            P(),
            P(),
        ),
        check_vma=False,
    )
```

```python
import jax
import jax.numpy as jnp

from jax import lax
from jax.experimental import pallas as pl
from jax.experimental.pallas import tpu as pltpu
from jax.sharding import PartitionSpec as P

CIN = 2048
MID = 512
CLS = 19
IMG = 4
SIDE_R = 32
SIDE_C = 32
PIX = 1024
TAPS = 9
EPSILON = 1e-05
BIN_COUNTS = (1, 2, 3, 6)
SIZES = tuple(IMG * bins * bins for bins in BIN_COUNTS)
STARTS = (0, 4, 20, 56)
BINS = 200


def region_maps(region_boxes, bins):
    canvases = region_boxes.shape[0]
    top = region_boxes[:, :, 0][:, :, None]
    left = region_boxes[:, :, 1][:, :, None]
    height = region_boxes[:, :, 2][:, :, None]
    width = region_boxes[:, :, 3][:, :, None]
    pixel = jnp.arange(PIX, dtype=jnp.int32)
    rel_row = (pixel // SIDE_C)[None, None, :] - top
    rel_col = (pixel % SIDE_C)[None, None, :] - left
    index = jnp.arange(bins, dtype=jnp.int32)[None, None, :, None]
    row_low = index * height[..., None] // bins
    row_high = ((index + 1) * height[..., None] + bins - 1) // bins
    col_low = index * width[..., None] // bins
    col_high = ((index + 1) * width[..., None] + bins - 1) // bins
    row_in = (rel_row[:, :, None, :] >= row_low) & (rel_row[:, :, None, :] < row_high)
    col_in = (rel_col[:, :, None, :] >= col_low) & (rel_col[:, :, None, :] < col_high)
    pool = (row_in[:, :, :, None, :] & col_in[:, :, None, :, :]).reshape(
        canvases, IMG * bins * bins, PIX
    )
    inside_row = (rel_row >= 0) & (rel_row < height)
    inside_col = (rel_col >= 0) & (rel_col < width)
    near_row = rel_row * bins // height
    near_col = rel_col * bins // width
    up_row = inside_row[:, :, None, :] & (near_row[:, :, None, :] == index)
    up_col = inside_col[:, :, None, :] & (near_col[:, :, None, :] == index)
    upmap = (up_row[:, :, :, None, :] & up_col[:, :, None, :, :]).reshape(
        canvases, IMG * bins * bins, PIX
    )
    inside = jnp.any(inside_row & inside_col, axis=1)
    return (pool, upmap, inside)


def silu_slope(value):
    sigma = jax.nn.sigmoid(value)
    return sigma * (1.0 + value * (1.0 - sigma))


def swap(value):
    return lax.ppermute(value, "bn", [(0, 1), (1, 0)])


def both(value):
    return jnp.concatenate([value, swap(value)], axis=0)


def dot(a, b, dims=((1,), (0,))):
    return lax.dot_general(a, b, (dims, ((), ())), preferred_element_type=jnp.float32)


def rolled(value, shift):
    rows = value.shape[0]
    if shift == 0:
        return value
    pad = jnp.zeros((abs(shift),) + value.shape[1:], value.dtype)
    if shift > 0:
        return jnp.concatenate([value[shift:], pad], axis=0)
    return jnp.concatenate([pad, value[: rows + shift]], axis=0)


def own_half(value, half, width):
    rows = value.shape[0]
    cut = value.reshape(rows, -1, 2, width)
    return lax.dynamic_index_in_dim(cut, half, axis=2, keepdims=False).reshape(rows, -1)


def gather_weights(branch_half, merge_half):
    return (
        lax.all_gather(branch_half, "fsdp", axis=0, tiled=True),
        lax.all_gather(merge_half, "fsdp", axis=0, tiled=True),
    )


def scatter_grads(grad_branch, grad_merge):
    return (
        lax.psum_scatter(grad_branch, "fsdp", scatter_dimension=0, tiled=True),
        lax.psum_scatter(grad_merge, "fsdp", scatter_dimension=0, tiled=True),
    )


def body(features, region_boxes, branch_w, merge_w, class_w, norm_gain, norm_bias, grad_logits):
    half = lax.axis_index("bn")
    wide = MID // 2
    branch_full, merge_full = gather_weights(
        own_half(branch_w, half, wide), own_half(merge_w, half, wide)
    )
    gains = lax.dynamic_slice_in_dim(norm_gain, half * wide, wide, 1).astype(jnp.float32)
    biases = lax.dynamic_slice_in_dim(norm_bias, half * wide, wide, 1).astype(jnp.float32)
    class_half = lax.dynamic_slice_in_dim(class_w, half * wide, wide, 0)
    feats = both(features)
    boxes = both(region_boxes)
    cotangent = both(grad_logits)
    pair = feats.shape[0]
    rows = pair * PIX
    pools = []
    upmaps = []
    inside = None
    for bins in BIN_COUNTS:
        pool, upmap, inside = region_maps(boxes, bins)
        pools.append(pool)
        upmaps.append(upmap)
    counts = jnp.concatenate(
        [jnp.sum(pool.astype(jnp.float32), axis=2) for pool in pools], axis=1
    )
    pools = jnp.concatenate(pools, axis=1).astype(jnp.bfloat16)
    upmaps = jnp.concatenate(upmaps, axis=1).astype(jnp.bfloat16)
    inside_float = inside.astype(jnp.float32)
    weight_in = inside_float.reshape(rows, 1)
    masked = (feats * inside.astype(jnp.bfloat16)[:, :, None]).reshape(rows, CIN)
    pooled_sum = jnp.einsum("cnp,cpd->cnd", pools, feats, preferred_element_type=jnp.float32)
    pooled = (pooled_sum / counts[:, :, None]).astype(jnp.bfloat16)

    spans = [slice(s, s + n) for s, n in zip(STARTS, SIZES)]
    outs = []
    stats = []
    for branch, span in enumerate(spans):
        entries = pair * SIZES[branch]
        value = jnp.einsum(
            "cnd,do->cno",
            pooled[:, span],
            branch_full[:, branch * wide : (branch + 1) * wide],
            preferred_element_type=jnp.float32,
        )
        mean = jnp.sum(value, axis=(0, 1)) / entries
        spread = jnp.sum(value * value, axis=(0, 1)) / entries - mean * mean
        inverse = lax.rsqrt(spread + EPSILON)
        centred = (value - mean) * inverse
        normed = centred * gains[branch] + biases[branch]
        outs.append(jax.nn.silu(normed).astype(jnp.bfloat16))
        stats.append((inverse, centred, normed, entries))
    active = jnp.concatenate(outs, axis=1)
    other = swap(active)
    active_full = jnp.where(
        half == 0,
        jnp.concatenate([active, other[::-1]], axis=2),
        jnp.concatenate([other[::-1], active], axis=2),
    )
    lifted = jnp.concatenate(
        [
            jnp.einsum(
                "cno,ok->cnk",
                active_full[:, span],
                merge_full[CIN + branch * MID : CIN + (branch + 1) * MID],
                preferred_element_type=jnp.float32,
            ).astype(jnp.bfloat16)
            for branch, span in enumerate(spans)
        ],
        axis=1,
    )
    spans_up = jnp.swapaxes(upmaps, 1, 2).reshape(rows, BINS)
    strip = 3 * wide
    column = jnp.zeros((rows, strip), jnp.float32)
    for dr in range(3):
        shift = (dr - 1) * SIDE_C
        cut = slice(dr * strip, (dr + 1) * strip)
        column = column + dot(rolled(masked, shift), merge_full[:CIN, cut])
        raised = rolled(spans_up, shift).reshape(pair, PIX, BINS)
        column = column + jnp.einsum(
            "cpn,cnk->cpk", raised, lifted[:, :, cut], preferred_element_type=jnp.float32
        ).reshape(rows, strip)
    convolved = (
        rolled(column[:, :wide], -1)
        + column[:, wide : 2 * wide]
        + rolled(column[:, 2 * wide :], 1)
    )
    pixel_count = jnp.sum(inside_float)
    mean_merged = jnp.sum(convolved * weight_in, axis=0) / pixel_count
    spread_merged = (
        jnp.sum(convolved * convolved * weight_in, axis=0) / pixel_count
        - mean_merged * mean_merged
    )
    inverse_merged = lax.rsqrt(spread_merged + EPSILON)
    centred_merged = (convolved - mean_merged) * inverse_merged
    normed_merged = centred_merged * gains[4] + biases[4]
    hidden = jax.nn.silu(normed_merged).astype(jnp.bfloat16)
    logits_part = (dot(hidden, class_half) * weight_in).reshape(pair, PIX, CLS)
    logits = logits_part[:1] + swap(logits_part[1:])

    masked_grad = (cotangent * inside.astype(jnp.bfloat16)[:, :, None]).reshape(rows, CLS)
    grad_class = dot(hidden, masked_grad, ((0,), (0,)))
    grad_hidden = dot(masked_grad, class_half, ((1,), (1,)))
    grad_normed = grad_hidden * silu_slope(normed_merged)
    gain_merged = jnp.sum(grad_normed * centred_merged * weight_in, axis=0)
    bias_merged = jnp.sum(grad_normed * weight_in, axis=0)
    grad_conv = (
        weight_in
        * gains[4]
        * inverse_merged
        * (grad_normed - (bias_merged + centred_merged * gain_merged) / pixel_count)
    ).astype(jnp.bfloat16)
    spread_grad = jnp.concatenate(
        [
            rolled(grad_conv, -((tap // 3 - 1) * SIDE_C + (tap % 3 - 1)))
            for tap in range(TAPS)
        ],
        axis=1,
    )
    binned = jnp.einsum(
        "cnp,cpk->cnk",
        upmaps,
        spread_grad.reshape(pair, PIX, TAPS * wide),
        preferred_element_type=jnp.float32,
    ).astype(jnp.bfloat16)
    merge_rows = [dot(masked, spread_grad, ((0,), (0,))).astype(jnp.bfloat16)]
    actives = []
    for branch, span in enumerate(spans):
        merge_rows.append(
            jnp.einsum(
                "cno,cnk->ok",
                active_full[:, span],
                binned[:, span],
                preferred_element_type=jnp.float32,
            ).astype(jnp.bfloat16)
        )
        actives.append(
            jnp.einsum(
                "cnk,ok->cno",
                binned[:, span],
                merge_full[CIN + branch * MID : CIN + (branch + 1) * MID],
                preferred_element_type=jnp.float32,
            )
        )
    grad_merge = jnp.concatenate(merge_rows, axis=0)
    grad_active = jnp.concatenate(actives, axis=1)
    mine = lax.dynamic_slice_in_dim(grad_active, half * wide, wide, 2)
    theirs = lax.dynamic_slice_in_dim(grad_active, (1 - half) * wide, wide, 2)
    grad_active = mine + swap(theirs.astype(jnp.bfloat16))[::-1].astype(jnp.float32)
    gain_rows = []
    bias_rows = []
    branch_columns = []
    pooled_grads = []
    for branch, span in enumerate(spans):
        inverse, centred, normed, entries = stats[branch]
        grad_branch_normed = grad_active[:, span] * silu_slope(normed)
        gain_row = jnp.sum(grad_branch_normed * centred, axis=(0, 1))
        bias_row = jnp.sum(grad_branch_normed, axis=(0, 1))
        gain_rows.append(gain_row)
        bias_rows.append(bias_row)
        grad_out = (
            gains[branch]
            * inverse
            * (grad_branch_normed - (bias_row + centred * gain_row) / entries)
        ).astype(jnp.bfloat16)
        branch_columns.append(
            jnp.einsum(
                "cnd,cno->do", pooled[:, span], grad_out, preferred_element_type=jnp.float32
            ).astype(jnp.bfloat16)
        )
        pooled_grads.append(
            jnp.einsum(
                "cno,do->cnd",
                grad_out,
                branch_full[:, branch * wide : (branch + 1) * wide],
                preferred_element_type=jnp.float32,
            )
        )
    grad_branch = jnp.concatenate(branch_columns, axis=1)
    grad_pooled = (jnp.concatenate(pooled_grads, axis=1) / counts[:, :, None]).astype(jnp.bfloat16)
    grad_masked = dot(spread_grad, merge_full[:CIN], ((1,), (1,))).reshape(pair, PIX, CIN)
    grad_masked = grad_masked + jnp.einsum(
        "cnp,cnd->cpd", pools, grad_pooled, preferred_element_type=jnp.float32
    )
    away = swap(grad_masked[1:].astype(jnp.bfloat16))
    grad_features = (grad_masked[:1] + away.astype(jnp.float32)) * inside_float[:1, :, None]

    share_branch, share_merge = scatter_grads(grad_branch, grad_merge)
    share_branch = whole_rows(share_branch, half, wide)
    share_merge = whole_rows(share_merge, half, wide)

    def placed(value, axis):
        shape = list(value.shape)
        shape[axis] = MID
        return lax.dynamic_update_slice_in_dim(
            jnp.zeros(shape, jnp.float32), value, half * wide, axis
        )

    total_class, total_gain, total_bias = lax.psum(
        (
            placed(grad_class, 0),
            placed(jnp.stack(gain_rows + [gain_merged]), 1),
            placed(jnp.stack(bias_rows + [bias_merged]), 1),
        ),
        ("bn", "fsdp"),
    )
    return (logits, grad_features, share_branch, share_merge, total_class, total_gain, total_bias)


def whole_rows(share, half, wide):
    rows = share.shape[0]
    other = swap(share)
    mine = share.reshape(rows, -1, 1, wide)
    other = other.reshape(rows, -1, 1, wide)
    joined = jnp.where(
        half == 0,
        jnp.concatenate([mine, other], axis=2),
        jnp.concatenate([other, mine], axis=2),
    )
    return joined.reshape(rows, -1).astype(jnp.float32)


MESH = pl.DeviceIdType.MESH
LINE, QUAD, WIDE = 4, 4, 256
CUT = 7 * WIDE
BF = jnp.bfloat16
F32 = jnp.float32
ROWS = 2048
STRIP = 3 * WIDE
NB = 256
PAIRBINS = 2 * NB
LANES = 128
SMALL = 32
SPANS = ((0, 4, 16), (16, 16, 16), (32, 36, 48), (80, 144, 176))


def place():
    half = lax.axis_index("bn")
    f = lax.axis_index("fsdp")
    return half, f, f // QUAD, f % QUAD


def turn(z, step):
    if step == 0:
        return z
    if step == 1:
        return z + 1 - 2 * (z % 2)
    if step == 2:
        return 2 - z // 2
    return 3 - 3 * (z // 2)


def greet(half, f, z, q, far=False):
    barrier = pltpu.get_barrier_semaphore()
    xq, yq = q + 1 - 2 * (q % 2), q + 2 - 4 * (q // 2)

    def signal(device):
        pl.semaphore_signal(barrier, inc=1, device_id=device, device_id_type=MESH)

    for device in ((half, z * QUAD + xq), (half, z * QUAD + yq), (1 - half, f)):
        signal(device)

    @pl.when(z < LINE - 1)
    def _():
        signal((half, f + QUAD))

    @pl.when(z > 0)
    def _():
        signal((half, f - QUAD))

    if far:
        signal((half, f + 2 * QUAD - 4 * QUAD * (z // 2)))
    pl.semaphore_wait(barrier, 5 + int(far) - (z // (LINE - 1)) - ((LINE - 1 - z) // (LINE - 1)))


def span_mask(shape, branch):
    row = lax.broadcasted_iota(jnp.int32, shape, 0)
    row = jnp.where(row >= NB, row - NB, row)
    if isinstance(branch, int):
        start, _, room = SPANS[branch]
        return (row >= start) & (row < start + room)
    kind = (row >= 16).astype(jnp.int32) + (row >= 32).astype(jnp.int32) + (row >= 80).astype(jnp.int32)
    return kind == branch


def mm(a, b, dims=((1,), (0,))):
    return lax.dot_general(a, b, (dims, ((), ())), preferred_element_type=F32)


def block(n, size):
    return pl.ds(pl.multiple_of(n * size, size), size)


def forward_kernel(
    merge_ref, branch_ref, feats_ref, g_ref, box_ref, class_ref, gain_ref, bias_ref,
    merge_out, branch_out, x_out, d3_out, ud_out, act_out, pooled_out, xhat_out, inv_out, pt_out, count_out,
    logit_own, logit_far, small_out,
    branch_own, merge_own, x, acc, wbuf, bfull, aw, awb, pm, um, ut, pt, pooled, act, act_own, xhat, inv, cv, dy, d3, ud,
    w_in, cnt, t1, t2, g, stage, small,
    local_sem, z_send, z_recv, q_send, q_recv, zb_send, zb_recv, core_send, core_recv, w_sem, out_sem,
):
    half, f, z, q = place()
    xq, yq, dq = q + 1 - 2 * (q % 2), q + 2 - 4 * (q // 2), 3 - q
    L = [turn(z, i) for i in range(LINE)]

    def cut_copy(src, dst, t, n):
        return pltpu.make_async_copy(
            src.at[:, pl.ds(pl.multiple_of(t * MID + half * WIDE, WIDE), WIDE)],
            dst.at[:, pl.ds(t * WIDE, WIDE)],
            local_sem.at[n],
        )

    own_copies = [cut_copy(branch_ref, branch_own, t, t) for t in range(4)] + [
        cut_copy(merge_ref, merge_own, t, 4 + t) for t in range(TAPS)
    ]
    for c in own_copies:
        c.start()
    core = (1 - half, f)
    own_loads = [
        pltpu.make_async_copy(g_ref, g.at[0], local_sem.at[15]),
        pltpu.make_async_copy(feats_ref, x.at[pl.ds(32, PIX)], local_sem.at[16]),
    ]
    for c in own_loads:
        c.start()

    def to_core(src, dst, n):
        return pltpu.make_async_remote_copy(
            src_ref=src, dst_ref=dst, send_sem=core_send.at[n], recv_sem=core_recv.at[n], device_id=core, device_id_type=MESH
        )

    crossing = [
        to_core(t1.at[0], t1.at[1], 0),
        to_core(t2.at[0], t2.at[1], 1),
        to_core(g_ref, g.at[1], 2),
        to_core(feats_ref, x.at[pl.ds(32 + PIX, PIX)], 3),
    ]
    greet(half, f, z, q)
    for c in own_copies:
        c.wait()
    keep = [
        pltpu.make_async_copy(branch_own, branch_out.at[f], local_sem.at[0]),
        pltpu.make_async_copy(merge_own, merge_out.at[f], local_sem.at[1]),
    ]

    def columns(kind):
        return pl.ds(0, CUT) if kind == 1 else pl.ds(CUT, 2 * WIDE)

    def piece(kind, owner, part=None):
        rows = 128 if kind == 0 else 256
        at = slice(None) if part is None else pl.ds(part * (rows // 2), rows // 2)
        return branch_out.at[owner, at] if kind == 0 else merge_out.at[owner, at, columns(kind)]

    def own_piece(kind):
        return branch_own if kind == 0 else merge_own.at[:, columns(kind)]

    def remote(ref, s, r, dev, src=None):
        return pltpu.make_async_remote_copy(
            src_ref=ref if src is None else src, dst_ref=ref, send_sem=s, recv_sem=r, device_id=dev, device_id_type=MESH
        )

    def beside(d):
        return (half, f + QUAD if d == 0 else f - QUAD)

    def z_copy(kind, i, d):
        src = own_piece(kind) if i == 0 else None
        return remote(piece(kind, L[i] * QUAD + q), z_send.at[kind, d, L[i]], z_recv.at[kind, L[i]], beside(d), src)

    def zb_copy(i, c, d):
        return remote(piece(2, L[i] * QUAD + c), zb_send.at[d, L[i], c], zb_recv.at[L[i], c], beside(d))

    def z_both(i, fn):
        @pl.when((L[i] <= z) & (z < LINE - 1))
        def _():
            fn(0)

        @pl.when((L[i] >= z) & (z > 0))
        def _():
            fn(1)

    def q_copy(kind, i, axis, what):
        dev = (half, z * QUAD + (xq if axis == 0 else yq))
        if what == 0:
            ref = piece(kind, L[i] * QUAD + q)
        else:
            ref = piece(kind, L[i] * QUAD + (yq if axis == 0 else xq), 1 - axis)
        src = own_piece(kind) if i == 0 and what == 0 else None
        return remote(ref, q_send.at[kind, L[i], axis, what], q_recv.at[kind, L[i], axis, what], dev, src)

    def q_arrive(kind, i, axis, what):
        owner = L[i] * QUAD + ((xq if axis == 0 else yq) if what == 0 else dq)
        ref = piece(kind, owner, None if what == 0 else 1 - axis)
        remote(ref, q_send.at[kind, L[i], axis, what], q_recv.at[kind, L[i], axis, what], core).wait_recv()

    def spread(kind, i):
        for axis in (0, 1):
            q_copy(kind, i, axis, 0).start()

    def pass_on(kind, i):
        for axis in (0, 1):
            q_arrive(kind, i, axis, 0)
            q_copy(kind, i, 1 - axis, 1).start()

    def corner(kind, i):
        for axis in (0, 1):
            q_arrive(kind, i, axis, 1)

    def z_step(kind, i):
        if i:
            remote(piece(kind, L[i] * QUAD + q), z_send.at[kind, 0, L[i]], z_recv.at[kind, L[i]], core).wait_recv()
        z_both(i, lambda d: z_copy(kind, i, d).start())

    def zb_step(i):
        for c in range(QUAD):
            if i:
                remote(piece(2, L[i] * QUAD + c), zb_send.at[0, L[i], c], zb_recv.at[L[i], c], core).wait_recv()
            z_both(i, lambda d: zb_copy(i, c, d).start())

    def bounds():
        for ref, axis in ((t1, 0), (t2, 1)):
            shape = (NB, 8) if axis == 0 else (8, NB)
            bin_ = lax.broadcasted_iota(jnp.int32, shape, axis)
            what = lax.broadcasted_iota(jnp.int32, shape, 1 - axis)
            by_row = what < 4
            ceil = jnp.bitwise_and(what, 3) > 0
            result = jnp.zeros(shape, jnp.int32)
            for (start, size, room), bins in zip(SPANS, BIN_COUNTS):
                at = bin_ - start
                image = lax.shift_right_logical(at * -(-65536 // (bins * bins)), 16)
                rest = at - image * (bins * bins)
                down = lax.shift_right_logical(rest * -(-65536 // bins), 16)
                index = jnp.where(by_row, down, rest - down * bins) + jnp.bitwise_and(what, 1)
                base = jnp.zeros(shape, jnp.int32)
                extent = jnp.zeros(shape, jnp.int32)
                for k in range(IMG):
                    base = jnp.where(image == k, jnp.where(by_row, box_ref[k, 0], box_ref[k, 1]), base)
                    extent = jnp.where(image == k, jnp.where(by_row, box_ref[k, 2], box_ref[k, 3]), extent)
                value = index * extent + jnp.where(ceil, bins - 1, 0)
                value = base + lax.shift_right_logical(value * -(-65536 // bins), 16)
                result = jnp.where((at >= 0) & (at < size), value, result)
            ref[0] = result

    def maps(c):
        def across(n, _):
            at = block(n, 32)
            p = lax.broadcasted_iota(jnp.int32, (32, PIX), 1)
            row, col = lax.shift_right_logical(p, 5), jnp.bitwise_and(p, 31)
            t = t1[c, at, :]
            cell = lambda k: t[:, k : k + 1]
            for ref, k in ((pm, 0), (um, 2)):
                hit = (row >= cell(k)) & (row < cell(k + 1)) & (col >= cell(k + 4)) & (col < cell(k + 5))
                value = jnp.where(hit, 1.0, 0.0)
                ref[c, at, :] = value.astype(BF)
                if k == 0:
                    total = jnp.maximum(jnp.sum(value, axis=1, keepdims=True), 1.0)
                    cnt[pl.ds(pl.multiple_of(c * NB + n * 32, 32), 32), :] = jnp.broadcast_to(total, (32, LANES))
            return 0

        lax.fori_loop(0, NB // 32, across, 0)

        def down(n, _):
            p = lax.broadcasted_iota(jnp.int32, (LANES, NB), 0) + n * LANES
            row, col = lax.shift_right_logical(p, 5), jnp.bitwise_and(p, 31)
            cell = lambda k: t2[c, k : k + 1, :]
            for k in (0, 2):
                hit = (row >= cell(k)) & (row < cell(k + 1)) & (col >= cell(k + 4)) & (col < cell(k + 5))
                value = jnp.where(hit, 1.0, 0.0)
                if k == 0:
                    pt[c, block(n, LANES), :] = value.astype(BF)
                else:
                    ut[c, pl.ds(pl.multiple_of(32 + n * LANES, 32), LANES), :] = value.astype(BF)
                    first = lax.broadcasted_iota(jnp.int32, (LANES, NB), 1) < IMG
                    inside = jnp.sum(jnp.where(first, value, 0.0), axis=1, keepdims=True)
                    w_in[pl.ds(pl.multiple_of(c * PIX + n * LANES, LANES), LANES), :] = inside
            return 0

        lax.fori_loop(0, PIX // LANES, down, 0)
        ut[c, 0:32, :] = jnp.zeros((32, NB), BF)
        ut[c, 32 + PIX : 64 + PIX, :] = jnp.zeros((32, NB), BF)

    def mask_pool(c):
        def mask(n, _):
            at = pl.ds(pl.multiple_of(32 + c * PIX + n * 64, 32), 64)
            w = w_in[pl.ds(pl.multiple_of(c * PIX + n * 64, 64), 64), :]
            x[at, :] = (x[at, :].astype(F32) * w).astype(BF)
            return 0

        lax.fori_loop(0, PIX // 64, mask, 0)

        def pool(n, _):
            cols = block(n, 512)
            total = mm(pm[c], x[pl.ds(32 + c * PIX, PIX), cols])
            pooled[pl.ds(c * NB, NB), cols] = (total / cnt[pl.ds(c * NB, NB), 0:1]).astype(BF)
            return 0

        lax.fori_loop(0, CIN // 512, pool, 0)

    def branches():
        load = pltpu.make_async_copy(branch_out, bfull, local_sem.at[2])
        load.start()
        load.wait()
        for b, (_, size, _) in enumerate(SPANS):
            weight = bfull[:, :, b * WIDE : (b + 1) * WIDE].reshape(CIN, WIDE)
            here = span_mask((PAIRBINS, WIDE), b)
            value = jnp.where(here, mm(pooled[...], weight), 0.0)
            entries = 2.0 * size
            mean = jnp.sum(value, axis=0, keepdims=True) / entries
            spread_ = jnp.sum(value * value, axis=0, keepdims=True) / entries - mean * mean
            inverse = lax.rsqrt(spread_ + EPSILON)
            centred = (value - mean) * inverse
            gain = gain_ref[b : b + 1, pl.ds(pl.multiple_of(half * WIDE, WIDE), WIDE)].astype(F32)
            bias = bias_ref[b : b + 1, pl.ds(pl.multiple_of(half * WIDE, WIDE), WIDE)].astype(F32)
            normed = centred * gain + bias
            active = normed * jax.nn.sigmoid(normed)
            inv[b : b + 1, :] = inverse
            if b == 0:
                xhat[...] = jnp.where(here, centred, 0.0)
                act_own[...] = jnp.where(here, active, 0.0).astype(BF)
            else:
                xhat[...] = jnp.where(here, centred, xhat[...])
                act_own[...] = jnp.where(here, active, act_own[...].astype(F32)).astype(BF)
        inv[4:8, :] = jnp.zeros((4, WIDE), F32)
        cols = pl.ds(pl.multiple_of(half * WIDE, WIDE), WIDE)
        sends = [
            to_core(act_own.at[pl.ds(c * NB, NB)], act.at[pl.ds((1 - c) * NB, NB), cols], 4 + c) for c in (0, 1)
        ]
        for s in sends:
            s.start()
        act[:, cols] = act_own[...]
        return sends

    def act_arrive():
        cols = pl.ds(pl.multiple_of((1 - half) * WIDE, WIDE), WIDE)
        for c in (0, 1):
            to_core(act_own.at[pl.ds(c * NB, NB)], act.at[pl.ds((1 - c) * NB, NB), cols], 4 + c).wait_recv()

    def w_load(kind, i, k, c):
        cols = columns(kind)
        return pltpu.make_async_copy(merge_out.at[L[i] * QUAD + c, :, cols], wbuf.at[k, :, cols], w_sem.at[k])

    def column_of(k):
        return (q % 2 + k % 2) % 2 + 2 * ((q // 2 + k // 2) % 2)

    def contract(kind, i, ks):
        for k in ks:
            w_load(kind, i, k, column_of(k)).start()

        def feature(k, _):
            c = column_of(k)
            w_load(kind, i, k, c).wait()
            lanes = block(L[i] * QUAD + c, WIDE)
            for canvas in (0, 1):
                r = canvas * PIX
                rows = pl.ds(r, PIX)
                if kind == 1:
                    acc[rows, :] = acc[rows, :] + (
                        mm(x[pl.ds(r, PIX), lanes], wbuf[k, :, 0:STRIP])
                        + mm(x[pl.ds(r + 32, PIX), lanes], wbuf[k, :, STRIP : 2 * STRIP])
                    )
                    acc[rows, 0:WIDE] = acc[rows, 0:WIDE] + mm(x[pl.ds(r + 64, PIX), lanes], wbuf[k, :, 2 * STRIP : CUT])
                else:
                    acc[rows, WIDE:STRIP] = acc[rows, WIDE:STRIP] + mm(x[pl.ds(r + 64, PIX), lanes], wbuf[k, :, CUT:])
            return 0

        def raised(k, _):
            c = column_of(k)
            w_load(kind, i, k, c).wait()
            here = span_mask((PAIRBINS, WIDE), 2 * (L[i] - 2) + c // 2)
            lhs = jnp.where(here, act[:, block(c % 2, WIDE)].astype(F32), 0.0).astype(BF)

            def strip(n, _):
                cols = block(n, WIDE)
                aw[:, cols] = aw[:, cols] + mm(lhs, wbuf[k, :, cols])
                return 0

            if kind == 1:
                lax.fori_loop(0, 7, strip, 0)
            else:
                lax.fori_loop(7, TAPS, strip, 0)
            return 0

        @pl.when(L[i] < 2)
        def _():
            lax.fori_loop(ks[0], ks[-1] + 1, feature, 0)

        @pl.when(L[i] >= 2)
        def _():
            lax.fori_loop(ks[0], ks[-1] + 1, raised, 0)

    def clear():
        x[0:32, :] = jnp.zeros((32, CIN), BF)
        x[32 + ROWS : 64 + ROWS, :] = jnp.zeros((32, CIN), BF)

        def clear_acc(n, _):
            acc[block(n, LANES), :] = jnp.zeros((LANES, STRIP), F32)
            return 0

        lax.fori_loop(0, ROWS // LANES, clear_acc, 0)

        def clear_aw(n, _):
            aw[block(n, 32), :] = jnp.zeros((32, TAPS * WIDE), F32)
            return 0

        lax.fori_loop(0, PAIRBINS // 32, clear_aw, 0)

    z_step(0, 0)
    spread(0, 0)
    spread(2, 0)
    bounds()
    for c in crossing:
        c.start()
    for c in keep:
        c.start()
    z_step(0, 1)
    spread(0, 1)
    maps(0)
    z_step(0, 2)
    spread(0, 2)
    z_step(0, 3)
    spread(0, 3)
    z_step(1, 0)
    spread(1, 0)
    for c in own_loads:
        c.wait()
    mask_pool(0)
    pass_on(0, 0)
    pass_on(2, 0)
    pass_on(0, 1)
    for c in crossing:
        c.wait_recv()
    maps(1)
    pass_on(0, 2)
    pass_on(0, 3)
    mask_pool(1)
    x_save = pltpu.make_async_copy(x.at[pl.ds(32, ROWS)], x_out, out_sem.at[0])
    x_save.start()
    z_step(1, 1)
    spread(1, 1)
    corner(2, 0)
    for c in keep:
        c.wait()
    zb_step(0)
    clear()
    pass_on(1, 0)
    z_step(1, 2)
    spread(1, 2)
    for i in range(LINE):
        corner(0, i)
    act_sends = branches()
    pass_on(1, 1)
    act_arrive()
    contract(1, 0, (0, 1, 2))
    z_step(1, 3)
    spread(1, 3)
    corner(1, 0)
    contract(1, 0, (3,))
    contract(1, 1, (0, 1, 2))
    zb_step(1)
    pass_on(1, 2)
    contract(2, 0, (0, 1, 2, 3))
    contract(1, 2, (0, 1, 2))
    corner(1, 1)
    contract(1, 1, (3,))
    contract(2, 1, (0, 1, 2, 3))
    zb_step(2)
    pass_on(1, 3)
    contract(2, 2, (0, 1, 2, 3))
    contract(1, 3, (0, 1, 2))
    corner(1, 2)
    contract(1, 2, (3,))
    zb_step(3)
    contract(2, 3, (0, 1, 2, 3))
    corner(1, 3)
    contract(1, 3, (3,))

    def lower(n, _):
        at = block(n, 32)
        awb[at, :] = aw[at, :].astype(BF)
        return 0

    lax.fori_loop(0, PAIRBINS // 32, lower, 0)
    ones = lambda: jnp.zeros((1, WIDE), F32)
    s1, s2, n2 = ones(), ones(), jnp.zeros((1, 1), F32)
    for c in (0, 1):
        rows = pl.ds(c * PIX, PIX)
        for dr in range(3):
            acc[rows, :] = acc[rows, :] + mm(
                ut[c, 32 * dr : 32 * dr + PIX, :], awb[c * NB : (c + 1) * NB, dr * STRIP : (dr + 1) * STRIP]
            )
        value = (
            pltpu.roll(acc[rows, 0:WIDE], 1, 0)
            + acc[rows, WIDE : 2 * WIDE]
            + pltpu.roll(acc[rows, 2 * WIDE : STRIP], PIX - 1, 0)
        )
        cv[rows, :] = value
        w = w_in[rows, :]
        kept = value * w
        s1 = s1 + jnp.sum(kept, axis=0, keepdims=True)
        s2 = s2 + jnp.sum(kept * value, axis=0, keepdims=True)
        n2 = n2 + jnp.sum(w, axis=0, keepdims=True)
    mean = s1 / n2
    inverse = lax.rsqrt(s2 / n2 - mean * mean + EPSILON)
    cols = pl.ds(pl.multiple_of(half * WIDE, WIDE), WIDE)
    gain = gain_ref[4:5, cols].astype(F32)
    bias = bias_ref[4:5, cols].astype(F32)
    weight = class_ref[:, cols]

    def slopes(n, carry):
        sum_b, sum_g, sum_c = carry
        at = block(n, 256)
        w = w_in[at, :]
        centred = (cv[at, :] - mean) * inverse
        normed = centred * gain + bias
        sigma = jax.nn.sigmoid(normed)
        hidden = (normed * sigma * w).astype(BF)
        pixels = block(n % 4, 256)
        stage[n // 4, :, pixels] = mm(weight, hidden, ((1,), (1,)))
        grad = g[n // 4, :, pixels]
        sum_c = sum_c + mm(grad, hidden)
        slope = mm(grad, weight, ((0,), (0,))) * (w * (sigma * (1.0 + normed * (1.0 - sigma))))
        dy[at, :] = slope
        cv[at, :] = centred
        return (
            sum_b + jnp.sum(slope, axis=0, keepdims=True),
            sum_g + jnp.sum(slope * centred, axis=0, keepdims=True),
            sum_c,
        )

    sum_b, sum_g, sum_c = lax.fori_loop(0, ROWS // 256, slopes, (ones(), ones(), jnp.zeros((CLS, WIDE), F32)))
    logit_sends = [
        pltpu.make_async_copy(stage.at[0], logit_own, out_sem.at[1]),
        to_core(stage.at[1], logit_far, 6),
    ]
    for c in logit_sends:
        c.start()
    small[0:CLS, :] = sum_c
    small[CLS:24, :] = jnp.zeros((24 - CLS, WIDE), F32)
    small[24:25, :] = sum_g
    small[25:26, :] = sum_b
    small[26:SMALL, :] = jnp.zeros((SMALL - 26, WIDE), F32)
    d3[0:32, :] = jnp.zeros((32, STRIP), BF)
    d3[32 + ROWS : 64 + ROWS, :] = jnp.zeros((32, STRIP), BF)
    for c in (0, 1):
        rows = pl.ds(c * PIX, PIX)
        value = (w_in[rows, :] * (gain * inverse)) * (dy[rows, :] - (sum_b + cv[rows, :] * sum_g) / n2)
        to = pl.ds(32 + c * PIX, PIX)
        d3[to, 0:WIDE] = pltpu.roll(value, PIX - 1, 0).astype(BF)
        d3[to, WIDE : 2 * WIDE] = value.astype(BF)
        d3[to, 2 * WIDE : STRIP] = pltpu.roll(value, 1, 0).astype(BF)
    for c in (0, 1):
        for dr in range(3):
            ud[c * NB : (c + 1) * NB, dr * STRIP : (dr + 1) * STRIP] = mm(
                um[c], d3[pl.ds(32 * (2 - dr) + c * PIX, PIX), :]
            ).astype(BF)
    saves = [
        pltpu.make_async_copy(a, b, out_sem.at[2 + n])
        for n, (a, b) in enumerate(
            (
                (d3, d3_out), (ud, ud_out), (act, act_out), (pooled, pooled_out), (xhat, xhat_out),
                (inv, inv_out), (pt, pt_out), (cnt, count_out), (small, small_out),
            )
        )
    ]
    for c in saves:
        c.start()

    for i in range(LINE):
        for kind in (0, 1):
            z_both(i, lambda d: z_copy(kind, i, d).wait_send())
        for c in range(QUAD):
            z_both(i, lambda d: zb_copy(i, c, d).wait_send())
        for kind in (0, 1) + ((2,) if i == 0 else ()):
            for axis in (0, 1):
                for what in (0, 1):
                    q_copy(kind, i, axis, what).wait_send()
    for c in crossing:
        c.wait_send()
    for c in act_sends:
        c.wait_send()
    logit_sends[0].wait()
    logit_sends[1].wait()
    x_save.wait()
    for c in saves:
        c.wait()


def forward_call(merge_w, branch_w, feats, g, boxes, class_w, gains, biases):
    D = pltpu.SemaphoreType.DMA
    V = lambda *s: pltpu.VMEM(s, BF)
    W = lambda *s: pltpu.VMEM(s, F32)
    S = jax.ShapeDtypeStruct
    hbm = pl.BlockSpec(memory_space=pl.ANY)
    vmem = pl.BlockSpec(memory_space=pltpu.VMEM)
    outs = (
        S((16, 256, TAPS * WIDE), BF), S((16, 128, 4 * WIDE), BF), S((ROWS, CIN), BF), S((ROWS + 64, STRIP), BF),
        S((PAIRBINS, TAPS * WIDE), BF), S((PAIRBINS, MID), BF), S((PAIRBINS, CIN), BF), S((PAIRBINS, WIDE), F32),
        S((8, WIDE), F32), S((2, PIX, NB), BF), S((PAIRBINS, LANES), F32), S((CLS, PIX), F32), S((CLS, PIX), F32),
        S((SMALL, WIDE), F32),
    )
    return pl.pallas_call(
        forward_kernel,
        out_shape=outs,
        in_specs=[hbm] * 4 + [pl.BlockSpec(memory_space=pltpu.SMEM)] + [vmem] * 3,
        out_specs=(hbm,) * len(outs),
        scratch_shapes=[
            V(128, 4 * WIDE), V(256, TAPS * WIDE), V(ROWS + 64, CIN), W(ROWS, STRIP), V(QUAD, 256, TAPS * WIDE),
            V(16, 128, 4 * WIDE), W(PAIRBINS, TAPS * WIDE), V(PAIRBINS, TAPS * WIDE), V(2, NB, PIX), V(2, NB, PIX),
            V(2, PIX + 64, NB), V(2, PIX, NB), V(PAIRBINS, CIN), V(PAIRBINS, MID), V(PAIRBINS, WIDE),
            W(PAIRBINS, WIDE), W(8, WIDE), W(ROWS, WIDE), W(ROWS, WIDE), V(ROWS + 64, STRIP), V(PAIRBINS, TAPS * WIDE),
            W(ROWS, 1), W(PAIRBINS, LANES), pltpu.VMEM((2, NB, 8), jnp.int32), pltpu.VMEM((2, 8, NB), jnp.int32),
            V(2, CLS, PIX), W(2, CLS, PIX), W(SMALL, WIDE),
            D((17,)), D((2, 2, 4)), D((2, 4)), D((3, 4, 2, 2)), D((3, 4, 2, 2)), D((2, 4, 4)), D((4, 4)),
            D((7,)), D((7,)), D((4,)), D((11,)),
        ],
        compiler_params=pltpu.CompilerParams(collective_id=0, has_side_effects=True, vmem_limit_bytes=63 * 1024 * 1024),
        name="forward",
    )(merge_w, branch_w, feats, g, boxes, class_w, gains, biases)


def backward_kernel(
    x_hbm, d3_hbm, act_hbm, ud_hbm, w_hbm, branch_hbm, pooled_hbm, xhat_hbm, pt_hbm, cnt_hbm, small_hbm, inv_ref, gain_ref, bias_ref,
    merge_out, branch_out, own_out, far_out, small_out,
    xt, act, d3, ud, g0, g1, b_all, fx0, fy0, fx1, fy1, fx2, fy2, zs0, zs1, zs2, wbuf, own_stage, far_stage,
    pooled, dzw, pt, cnt, bgbuf, small, small_in,
    local_sem, q_send, q_recv, z_send, z_recv, zb_send, zb_recv, end_send, end_recv, w_sem, own_sem, far_send, far_recv, end_local,
    act_send, act_recv, bg_sem, pool_sem, sum_send, sum_recv,
):
    half, f, z, q = place()
    xq, yq, dq = q + 1 - 2 * (q % 2), q + 2 - 4 * (q // 2), 3 - q
    L = [turn(z, i) for i in range(LINE)]
    xhat = own_stage.at[1, pl.ds(0, PAIRBINS)]
    loads = [
        pltpu.make_async_copy(a, b, local_sem.at[n])
        for n, (a, b) in enumerate(
            (
                (d3_hbm, d3), (ud_hbm, ud), (act_hbm, act), (pt_hbm, pt), (cnt_hbm, cnt), (xhat_hbm, xhat),
                (small_hbm, small.at[0, pl.ds(0, SMALL)]),
            )
        )
    ]
    for c in loads:
        c.start()

    def fetch_rows(i):
        return pltpu.make_async_copy(
            x_hbm.at[:, pl.ds(pl.multiple_of(L[i] * 1024, 1024), 1024)], xt, local_sem.at[7]
        )

    def rows_start(i):
        @pl.when(L[i] < 2)
        def _():
            fetch_rows(i).start()

    rows_start(3)
    greet(half, f, z, q, True)
    for c in loads:
        c.wait()
    from_x, from_y, zslot = (fx0, fx1, fx2), (fy0, fy1, fy2), (zs0, zs1, zs2)
    HALF = (64, 128, 128)

    def column_of(k):
        return (q % 2 + k % 2) % 2 + 2 * ((q // 2 + k // 2) % 2)

    def own(kind, i, c):
        if kind == 0:
            return g0.at[i % 2, c]
        return g1.at[i % 2, c] if kind == 1 else b_all.at[L[i] * QUAD + c]

    def part(ref, kind, h):
        return ref.at[pl.ds(h * HALF[kind], HALF[kind])]

    def slot(kind, i, axis, what):
        ref = (from_x, from_y)[axis][kind]
        return ref.at[L[i], what] if kind < 2 else ref.at[0, what]

    def q_copy(kind, i, axis, what):
        to = xq if axis == 0 else yq
        if what == 0:
            src = part(own(kind, i, dq), kind, 1 - axis)
        elif what == 1:
            src = part(own(kind, i, to), kind, axis)
        else:
            src = part(own(kind, i, to), kind, 1 - axis)
        return pltpu.make_async_remote_copy(
            src_ref=src, dst_ref=slot(kind, i, axis, what), send_sem=q_send.at[kind, L[i], axis, what],
            recv_sem=q_recv.at[kind, L[i], axis, what], device_id=(half, z * QUAD + to), device_id_type=MESH,
        )

    def add_into(dst, *others):
        def rows16(n, _):
            at = block(n, 16)
            total = dst[at, :].astype(F32)
            for o in others:
                total = total + o[at, :].astype(F32)
            dst[at, :] = total.astype(BF)
            return 0

        lax.fori_loop(0, dst.shape[0] // 16, rows16, 0)

    def raw(kind, i):
        for what in (0, 2):
            for axis in (0, 1):
                q_copy(kind, i, axis, what).start()

    def fold(kind, i):
        for axis in (1, 0):
            q_copy(kind, i, axis, 0).wait_recv()
            to = xq if axis == 1 else yq
            add_into(part(own(kind, i, to), kind, 1 - axis), slot(kind, i, axis, 0))
            q_copy(kind, i, 1 - axis, 1).start()

    def gathered(kind, i):
        for axis in (0, 1):
            for what in (1, 2):
                q_copy(kind, i, axis, what).wait_recv()
        mine = own(kind, i, q)
        add_into(slot(kind, i, 0, 1), part(mine, kind, 0), slot(kind, i, 1, 2))
        add_into(slot(kind, i, 0, 2), part(mine, kind, 1), slot(kind, i, 1, 1))

    def total(kind, i):
        return from_x[kind].at[L[i] if kind < 2 else 0, pl.ds(1, 2)]

    def z_src(kind, i, c):
        return total(kind, i) if kind < 2 else own(2, i, c)

    def z_dst(kind, n, c):
        return zslot[kind].at[n] if kind < 2 else zs2.at[n, c]

    def z_sems(kind, level, n, c):
        if kind < 2:
            return z_send.at[kind, level], z_recv.at[kind, n]
        return zb_send.at[level, c], zb_recv.at[n, c]

    def z_copy(kind, i, c, up):
        level = L[i]
        n = level if up else level + (LINE - level) * (1 - jnp.minimum(z - 1 - level, 1))
        s, r = z_sems(kind, level, n, c)
        return pltpu.make_async_remote_copy(
            src_ref=z_src(kind, i, c), dst_ref=z_dst(kind, n, c), send_sem=s, recv_sem=r,
            device_id=(half, f + QUAD if up else f - QUAD), device_id_type=MESH,
        )

    def z_take(kind, i, n, c):
        s, r = z_sems(kind, L[i], n, c)
        pltpu.make_async_remote_copy(
            src_ref=z_src(kind, i, c), dst_ref=z_dst(kind, n, c), send_sem=s, recv_sem=r,
            device_id=(1 - half, f), device_id_type=MESH,
        ).wait_recv()
        if kind < 2:
            for h in (0, 1):
                add_into(total(kind, i).at[h], z_dst(kind, n, c).at[h])
        else:
            add_into(own(2, i, c), z_dst(kind, n, c))

    def early(kind, i, c=None):
        @pl.when((L[i] > z) & (z == 0))
        def _():
            z_copy(kind, i, c, True).start()

        @pl.when((L[i] < z) & (z == LINE - 1))
        def _():
            z_copy(kind, i, c, False).start()

    def late(kind, i, c=None):
        @pl.when((L[i] > z) & (z > 0))
        def _():
            z_take(kind, i, L[i], c)
            z_copy(kind, i, c, True).start()

        @pl.when((L[i] < z) & (z < LINE - 1))
        def _():
            z_take(kind, i, L[i], c)
            z_copy(kind, i, c, False).start()

    def home(kind, c=None):
        @pl.when(z > 0)
        def _():
            z_take(kind, 0, z, c)

        @pl.when(z < LINE - 1)
        def _():
            z_take(kind, 0, LINE, c)

    def line_sent(kind, i, c=None):
        @pl.when(L[i] > z)
        def _():
            z_copy(kind, i, c, True).wait_send()

        @pl.when(L[i] < z)
        def _():
            z_copy(kind, i, c, False).wait_send()

    def quad_sent(kind, i):
        for axis in (0, 1):
            for what in (0, 1, 2):
                q_copy(kind, i, axis, what).wait_send()

    def early_b(i):
        for c in range(QUAD):
            early(2, i, c)

    def late_b(i):
        for c in range(QUAD):
            late(2, i, c)

    def produce(i):
        level = L[i]

        @pl.when(level < 2)
        def _():
            fetch_rows(i).wait()

        @pl.when(level >= 2)
        def _():
            for c in range(QUAD):
                here = span_mask((PAIRBINS, WIDE), 2 * (level - 2) + c // 2)
                rows = act[:, (c % 2) * WIDE : (c % 2 + 1) * WIDE].astype(F32)
                xt[0:PAIRBINS, c * WIDE : (c + 1) * WIDE] = jnp.where(here, rows, 0.0).astype(BF)

        for k in (3, 1, 2, 0):
            c = column_of(k)

            def store(dr, value):
                if dr < 2:
                    g1[i % 2, c, :, dr * STRIP : (dr + 1) * STRIP] = value.astype(BF)
                else:
                    g1[i % 2, c, :, 2 * STRIP : CUT] = value[:, 0:WIDE].astype(BF)
                    b_all[level * QUAD + c] = value[:, WIDE:].astype(BF)

            @pl.when(level < 2)
            def _():
                for dr in range(3):
                    store(dr, mm(xt[:, block(c, WIDE)], d3[pl.ds(32 * (2 - dr), ROWS), :], ((0,), (0,))))

            @pl.when(level >= 2)
            def _():
                for dr in range(3):
                    store(dr, mm(xt[0:PAIRBINS, block(c, WIDE)], ud[:, dr * STRIP : (dr + 1) * STRIP], ((0,), (0,))))

            if k == 3:
                q_copy(1, i, 0, 0).start()
                q_copy(1, i, 1, 0).start()
            elif k:
                q_copy(1, i, k - 1, 2).start()
        if i:
            rows_start(i - 1)

    def w_load(n):
        return pltpu.make_async_copy(w_hbm.at[n], wbuf.at[n % 2], w_sem.at[n % 2])

    def spans(b):
        start, _, room = SPANS[b]
        return [pl.ds(c * NB + start, room) for c in (0, 1)]

    def far_rows(n):
        return pltpu.make_async_remote_copy(
            src_ref=far_stage.at[0, pl.ds(n * NB, NB)], dst_ref=far_stage.at[1, pl.ds((1 - n) * NB, NB)],
            send_sem=act_send.at[n], recv_sem=act_recv.at[n], device_id=(1 - half, f), device_id_type=MESH,
        )

    def bin_gradients():
        w_load(8).start()
        for n in range(8):
            w_load(8 + n).wait()
            if n < 7:
                w_load(9 + n).start()
            b, h = n // 2, n % 2
            lhs = jnp.concatenate([ud[s, :] for s in spans(b)], axis=0)
            value = mm(lhs, wbuf[n % 2], ((1,), (1,)))
            room = SPANS[b][2]
            for c, s in enumerate(spans(b)):
                own_stage[0, pl.ds(h * PAIRBINS + c * NB + SPANS[b][0], room), :] = value[c * room : (c + 1) * room]
        w_load(0).start()
        away = pl.ds(pl.multiple_of((1 - half) * PAIRBINS, PAIRBINS), PAIRBINS)
        far_stage[0, 0:PAIRBINS, :] = own_stage[0, away, :].astype(BF)
        for n in (0, 1):
            far_rows(n).start()

    def branch_gradients():
        for n in (0, 1):
            far_rows(n).wait_recv()
        home_rows = pl.multiple_of(half * PAIRBINS, PAIRBINS)
        cols = pl.ds(pl.multiple_of(half * WIDE, WIDE), WIDE)
        dzw[...] = jnp.zeros((PAIRBINS, 4 * WIDE), BF)
        for b, (start, size, room) in enumerate(SPANS):
            gain = gain_ref[b : b + 1, cols].astype(F32)
            bias = bias_ref[b : b + 1, cols].astype(F32)
            both_c, both_d = [], []
            for c in (0, 1):
                rows = pl.ds(c * NB + start, room)
                centred = own_stage[1, rows, :]
                grad = own_stage[0, pl.ds(home_rows + c * NB + start, room), :] + far_stage[1, rows, :].astype(F32)
                normed = centred * gain + bias
                sigma = jax.nn.sigmoid(normed)
                both_c.append(centred)
                both_d.append(grad * (sigma * (1.0 + normed * (1.0 - sigma))))
            sum_b = sum(jnp.sum(d, axis=0, keepdims=True) for d in both_d)
            sum_g = sum(jnp.sum(d * e, axis=0, keepdims=True) for d, e in zip(both_d, both_c))
            small[0, 26 + b : 27 + b, :] = sum_g
            small[0, 30 + b : 31 + b, :] = sum_b
            for c in (0, 1):
                value = (gain * inv_ref[b : b + 1, :]) * (both_d[c] - (sum_b + both_c[c] * sum_g) / (2.0 * size))
                dzw[c * NB + start : c * NB + start + room, b * WIDE : (b + 1) * WIDE] = value.astype(BF)
        small[0, 34:40, :] = jnp.zeros((6, WIDE), F32)

    def pool_load(i):
        return pltpu.make_async_copy(
            pooled_hbm.at[:, pl.ds(pl.multiple_of(L[i] * 512, 512), 512)], pooled, pool_sem.at[0]
        )

    def produce_branch(i):
        pool_load(i).wait()
        g0[i % 2] = mm(pooled[...], dzw[...], ((0,), (0,))).astype(BF).reshape(QUAD, 128, 4 * WIDE)
        if i:
            pool_load(i - 1).start()

    def own_copy(n):
        return pltpu.make_async_copy(own_stage.at[n % 2], own_out.at[:, block(n, WIDE)], own_sem.at[n % 2])

    def far_copy(n):
        return pltpu.make_async_remote_copy(
            src_ref=far_stage.at[n % 2], dst_ref=far_out.at[:, block(n, WIDE)], send_sem=far_send.at[n % 2],
            recv_sem=far_recv.at[n], device_id=(1 - half, f), device_id_type=MESH,
        )

    def bg_load(n):
        return pltpu.make_async_copy(branch_hbm.at[pl.ds(n * 2, 2)], bgbuf.at[n % 2], bg_sem.at[n % 2])

    def jobs(first, last):
        def job(n, _):
            w_load(n).wait()
            bg_load(n).wait()

            @pl.when(n < 7)
            def _():
                w_load(n + 1).start()
                bg_load(n + 1).start()

            @pl.when(n >= 2)
            def _():
                own_copy(n - 2).wait()
                far_copy(n - 2).wait_send()

            bins = (mm(dzw[...], bgbuf[n % 2].reshape(WIDE, 4 * WIDE), ((1,), (1,))) / cnt[:, 0:1]).astype(BF)
            for canvas in (0, 1):
                value = mm(pt[canvas], bins[canvas * NB : (canvas + 1) * NB])
                for dr in range(3):
                    value = value + mm(
                        d3[pl.ds(32 * (2 - dr) + canvas * PIX, PIX), :], wbuf[n % 2, :, dr * STRIP : (dr + 1) * STRIP],
                        ((1,), (1,)),
                    )
                first_bins = lax.broadcasted_iota(jnp.int32, (PIX, LANES), 1) < IMG
                inside = jnp.sum(
                    jnp.where(first_bins, pt[canvas, :, 0:LANES].astype(F32), 0.0), axis=1, keepdims=True
                )
                value = value * inside
                if canvas == 0:
                    own_stage[n % 2] = value
                else:
                    far_stage[n % 2] = value.astype(BF)
            own_copy(n).start()
            far_copy(n).start()
            return 0

        lax.fori_loop(first, last, job, 0)

    def sum_copy(n):
        zz = z + 1 - 2 * (z % 2) if n == 2 else z + 2 - 4 * (z // 2)
        to = (z * QUAD + xq, z * QUAD + yq, zz * QUAD + q, zz * QUAD + q)[n]
        return pltpu.make_async_remote_copy(
            src_ref=small.at[n], dst_ref=small_in.at[n], send_sem=sum_send.at[n], recv_sem=sum_recv.at[n],
            device_id=(half, to), device_id_type=MESH,
        )

    def sum_take(n):
        sum_copy(n).wait_recv()
        small[n + 1] = small[n] + small_in[n]
        if n < 3:
            sum_copy(n + 1).start()

    pool_load(3).start()
    bg_load(0).start()
    produce(3)
    early_b(3)
    produce(2)
    early_b(2)
    bin_gradients()
    fold(1, 3)
    branch_gradients()
    sum_copy(0).start()
    produce_branch(3)
    raw(0, 3)
    produce_branch(2)
    gathered(1, 3)
    early(1, 3)
    late_b(3)
    for n in (0, 1):
        far_rows(n).wait_send()
    jobs(0, 2)
    sum_take(0)
    quad_sent(1, 3)
    fold(1, 2)
    produce(1)
    early_b(1)
    fold(0, 3)
    raw(0, 2)
    late(1, 3)
    late_b(2)
    gathered(0, 3)
    early(0, 3)
    jobs(2, 4)
    sum_take(1)
    gathered(1, 2)
    early(1, 2)
    quad_sent(1, 2)
    fold(1, 1)
    produce(0)
    quad_sent(0, 3)
    produce_branch(1)
    fold(0, 2)
    raw(0, 1)
    late(0, 3)
    late(1, 2)
    late_b(1)
    jobs(4, 6)
    sum_take(2)
    gathered(0, 2)
    early(0, 2)
    quad_sent(0, 2)
    produce_branch(0)
    raw(0, 0)
    gathered(1, 1)
    early(1, 1)
    fold(1, 0)
    fold(0, 1)
    jobs(6, 8)
    sum_take(3)
    for c in range(QUAD):
        home(2, c)
    raw(2, 0)
    gathered(0, 1)
    early(0, 1)
    late(0, 2)
    late(1, 1)
    late(0, 1)
    fold(0, 0)
    fold(2, 0)
    gathered(1, 0)
    gathered(0, 0)
    gathered(2, 0)
    home(1)
    home(0)

    ends = []

    def give(src, into, n):
        c = pltpu.make_async_remote_copy(
            src_ref=src, dst_ref=into(half), send_sem=end_send.at[n], recv_sem=end_recv.at[n],
            device_id=(1 - half, f), device_id_type=MESH,
        )
        c.start()
        k = pltpu.make_async_copy(src, into(half), end_local.at[n])
        k.start()
        back = pltpu.make_async_remote_copy(
            src_ref=src, dst_ref=into(1 - half), send_sem=end_send.at[n], recv_sem=end_recv.at[n],
            device_id=(1 - half, f), device_id_type=MESH,
        )
        ends.append((c, k, back))

    def columns(ref, t):
        return lambda h: ref.at[:, :, pl.ds(pl.multiple_of(t * MID + h * WIDE, WIDE), WIDE)]

    for t in range(TAPS):
        src = total(1, 0).at[:, :, pl.ds(t * WIDE, WIDE)] if t < 7 else total(2, 0).at[:, :, pl.ds((t - 7) * WIDE, WIDE)]
        give(src, columns(merge_out, t), t)
    for t in range(4):
        give(total(0, 0).at[:, :, pl.ds(t * WIDE, WIDE)], columns(branch_out, t), TAPS + t)
    give(small.at[4], lambda h: small_out.at[h], 13)

    for n in range(4):
        sum_copy(n).wait_send()
    for i in range(LINE):
        if i < 2:
            quad_sent(0, i)
            quad_sent(1, i)
        if i:
            line_sent(0, i)
            line_sent(1, i)
            for c in range(QUAD):
                line_sent(2, i, c)
    quad_sent(2, 0)
    for n in (6, 7):
        own_copy(n).wait()
        far_copy(n).wait_send()
    for n in range(8):
        far_copy(n).wait_recv()
    for c, k, back in ends:
        c.wait_send()
        k.wait()
        back.wait_recv()


def backward_call(x, d3, act, ud, w, branch, pooled, xhat, pt, cnt, small, inv, gains, biases):
    D = pltpu.SemaphoreType.DMA
    V = lambda *s: pltpu.VMEM(s, BF)
    W = lambda *s: pltpu.VMEM(s, F32)
    S = jax.ShapeDtypeStruct
    hbm = pl.BlockSpec(memory_space=pl.ANY)
    vmem = pl.BlockSpec(memory_space=pltpu.VMEM)
    outs = (
        S((2, 128, TAPS * MID), BF), S((2, 64, 4 * MID), BF), S((PIX, CIN), F32), S((PIX, CIN), BF), S((2, 40, WIDE), F32),
    )
    return pl.pallas_call(
        backward_kernel,
        out_shape=outs,
        in_specs=[hbm] * 11 + [vmem] * 3,
        out_specs=(hbm,) * len(outs),
        scratch_shapes=[
            V(ROWS, 1024), V(PAIRBINS, MID), V(ROWS + 64, STRIP), V(PAIRBINS, TAPS * WIDE), V(2, 4, 128, 1024),
            V(2, 4, 256, CUT), V(16, 256, 512), V(4, 3, 64, 1024), V(4, 3, 64, 1024), V(4, 3, 128, CUT), V(4, 3, 128, CUT),
            V(1, 3, 128, 512), V(1, 3, 128, 512), V(5, 2, 64, 1024), V(5, 2, 128, CUT), V(5, 4, 256, 512),
            V(2, 256, TAPS * WIDE), W(2, PIX, WIDE), V(2, PIX, WIDE), V(PAIRBINS, 512), V(PAIRBINS, 4 * WIDE),
            V(2, PIX, NB), W(PAIRBINS, LANES), V(2, 2, 128, 4 * WIDE), W(5, 40, WIDE), W(4, 40, WIDE),
            D((8,)), D((3, 4, 2, 3)), D((3, 4, 2, 3)), D((2, 4)), D((2, 5)), D((4, 4)), D((5, 4)), D((14,)), D((14,)),
            D((2,)), D((2,)), D((2,)), D((8,)), D((14,)), D((2,)), D((2,)), D((2,)), D((1,)), D((4,)), D((4,)),
        ],
        compiler_params=pltpu.CompilerParams(collective_id=1, has_side_effects=True, vmem_limit_bytes=63 * 1024 * 1024),
        name="backward",
    )(x, d3, act, ud, w, branch, pooled, xhat, pt, cnt, small, inv, gains, biases)


def paired(features, region_boxes, branch_w, merge_w, class_w, norm_gain, norm_bias, grad_logits):
    (
        merge_g, branch_g, masked, spread_grad, binned, active, pooled, centred, inverse, pool_t, counts,
        logit_own, logit_far, small,
    ) = forward_call(
        merge_w, branch_w, features.reshape(PIX, CIN), grad_logits[0].T, region_boxes[0], class_w.T, norm_gain, norm_bias,
    )
    logits = (logit_own + logit_far).T[None]
    share_merge, share_branch, own_part, far_part, sums = backward_call(
        masked, spread_grad, active, binned, merge_g, branch_g, pooled, centred, pool_t, counts, small, inverse,
        norm_gain, norm_bias,
    )
    grad_features = (own_part + far_part.astype(F32))[None]
    sums = jnp.transpose(sums, (1, 0, 2)).reshape(40, MID)
    total_class = sums[:CLS].T
    total_gain = jnp.concatenate([sums[26:30], sums[24:25]], axis=0)
    total_bias = jnp.concatenate([sums[30:34], sums[25:26]], axis=0)
    return (
        logits,
        grad_features,
        share_branch.reshape(128, 4 * MID).astype(F32),
        share_merge.reshape(256, TAPS * MID).astype(F32),
        total_class,
        total_gain,
        total_bias,
    )


def solution(mesh):
    placed = (
        P(("bn", "fsdp"), None, None),
        P(("bn", "fsdp"), None, None),
        P("fsdp", None),
        P("fsdp", None),
        P(),
        P(),
        P(),
        P(("bn", "fsdp"), None, None),
    )
    run = paired if dict(mesh.shape) == {"bn": 2, "fsdp": LINE * QUAD} else body
    return jax.shard_map(
        run,
        mesh=mesh,
        in_specs=placed,
        out_specs=(
            P(("bn", "fsdp"), None, None),
            P(("bn", "fsdp"), None, None),
            P("fsdp", None),
            P("fsdp", None),
            P(),
            P(),
            P(),
        ),
        check_vma=False,
    )
```
